32 devices in a mesh: grp: 2 (over y), az: 4 (over z), el: 2 (over x), fq: 2 (over core).
Axes of the slice: x: 2, y: 2, z: 4, core: 2. Of those that a mesh axis runs over, the one named last changes fastest.
Arguments:
- polar: bfloat16 [2, 64, 1024, 768], P(None, ('grp', 'el'), 'az', 'fq'), parts along dimension 1, may hold values from -6 to 6
- band_offset: int32 [1024, 768], P('az', 'fq'), may hold values from -8 to 5, as said below
- tap_count: int32 [1024, 768], P('az', 'fq'), may hold values from 4 to 8
- tap_weight: bfloat16 [8, 1024, 768], P(None, 'az', 'fq'), may hold values from -2.390625 to 2.390625
Outputs:
- image_out: bfloat16 [2, 64, 768, 1024], P(None, ('grp', 'el'), ('az', 'fq')), parts along dimension 1
The draws below stay inside these ranges and needn't reach their ends.
There are 2 independent parts, one for each index of `grp`. The reference program is written for one: setup_inputs(seed, part) draws one part's arguments, and reference() takes and returns one part's arrays. A program takes and returns all parts, laid end to end along the dimension named above; an argument that names none is the same for every part. Nothing has to cross between parts.
Inputs may be any that keep to these rules, and one draw needn't show every extreme that they name: band_offset[j, f] lies between -8 and 9 - tap_count[j, f], so a band reads azimuths j - 8 to j + 8; both ends are reached.
All inputs are finite; a program needn't handle non-finite values.
Results may differ from the reference program's by a relative error of at most 0.0074.
Values may be sent and summed in bfloat16 or wider, within the bound.
No kernel may reach another device: no remote copies, remote signals or barrier semaphores. Data moves between devices by JAX's collectives and lax.ppermute only.
A program may use at most 128 MiB of HBM per device.

```python
import math
import jax
import jax.numpy as jnp
from jax import lax

F = 768
A = 1024
E = 32
HW = 8
KT = 8


def band_pair(key):
    base_key = jax.random.fold_in(key, 4711)
    sub_keys = jax.random.split(base_key, 3)
    tap_draw = jax.random.randint(sub_keys[0], (A * F,), KT // 2, KT + 1, dtype=jnp.int32)
    raw_draw = jax.random.randint(sub_keys[1], (A * F,), 0, 1 << 20, dtype=jnp.int32)
    spread = 2 * HW + 2 - tap_draw
    offsets = raw_draw % spread - HW
    chosen = jax.random.randint(sub_keys[2], (3,), 0, A * F, dtype=jnp.int32)
    tap_draw = tap_draw.at[chosen[0]].set(KT)
    offsets = offsets.at[chosen[0]].set(-HW)
    offsets = offsets.at[chosen[1]].set(-HW)
    tap_draw = tap_draw.at[chosen[2]].set(KT // 2)
    offsets = offsets.at[chosen[2]].set(HW + 1 - KT // 2)
    return (offsets.reshape(A, F), tap_draw.reshape(A, F))


def draw_band_offset(key, part):
    return band_pair(key)[0]


def draw_tap_count(key, part):
    return band_pair(key)[1]


def block_scale(stream_key, shape, cuts, low, top_value):
    def one(position, shards_of):
        steps = jax.random.uniform(jax.random.fold_in(jax.random.fold_in(stream_key, 6), position), (shards_of,), jnp.float32, low / len(cuts), top_value / len(cuts))
        return jnp.repeat(jnp.exp(steps), shape[position] // shards_of).reshape((-1,) + (1,) * (len(shape) - position - 1))

    level = one(*cuts[0])
    for cut in cuts[1:]:
        level = level * one(*cut)
    return level


def normal_values(stream_key, dims, scale, bound, cuts=(), kind=jnp.bfloat16):
    array = jax.random.normal(stream_key, dims, jnp.float32) * scale
    if len(cuts) > 0:
        array = block_scale(stream_key, dims, cuts, -0.22, 0.18) * array
    return jnp.clip(array, min=-bound, max=bound).astype(kind)


def setup_inputs(seed: int = 0, part: int = 0) -> dict:
    streams_of = jax.random.split(jax.random.key(seed), 5)
    own_keys = jax.random.split(jax.random.fold_in(streams_of[4], part), 5)
    polar = normal_values(own_keys[0], (2, E, A, F), 1.0, 6.0, ((1, 2), (2, 4), (3, 2)))
    band_offset = draw_band_offset(jax.random.fold_in(streams_of[4], 71), part)
    tap_count = draw_tap_count(jax.random.fold_in(streams_of[4], 71), part)
    tap_weight = normal_values(streams_of[3], (KT, A, F), 0.4, 2.390625, ((1, 4), (2, 2)))
    return {"polar": polar, "band_offset": band_offset, "tap_count": tap_count, "tap_weight": tap_weight}


def table_pair(row_ids, col_ids, length):
    product = row_ids[:, None] * col_ids[None, :] % length
    angle = product.astype(jnp.float32) * (2.0 * math.pi / length)
    return (jnp.cos(angle).astype(jnp.bfloat16), jnp.sin(angle).astype(jnp.bfloat16))

def complex_dot(real_in, imag_in, cos_tab, sin_tab):
    real_wide = real_in.astype(jnp.float32)
    imag_wide = imag_in.astype(jnp.float32)
    cos_wide = cos_tab.astype(jnp.float32)
    sin_wide = sin_tab.astype(jnp.float32)
    high = lax.Precision.HIGHEST
    real_out = jnp.dot(real_wide, cos_wide, precision=high) - jnp.dot(imag_wide, sin_wide, precision=high)
    imag_out = jnp.dot(real_wide, sin_wide, precision=high) + jnp.dot(imag_wide, cos_wide, precision=high)
    return (real_out, imag_out)

def reference(polar, band_offset, tap_count, tap_weight):
    freq_ids = jnp.arange(F, dtype=jnp.int32)
    azim_ids = jnp.arange(A, dtype=jnp.int32)
    elev_ids = jnp.arange(E, dtype=jnp.int32)
    cos_f, sin_f = table_pair(freq_ids, freq_ids, F)
    cos_a, sin_a = table_pair(azim_ids, azim_ids, A)
    cos_e, sin_e = table_pair(elev_ids, elev_ids, E)
    weights = tap_weight.astype(jnp.float32)
    column_ids = azim_ids[:, None]

    def one_cut(cut_slab):
        padded = jnp.pad(cut_slab.astype(jnp.float32), ((0, 0), (HW, HW), (0, 0)))
        accumulated = jnp.zeros((2, A, F), jnp.float32)
        for tap_index in range(KT):
            source_index = jnp.minimum(column_ids + HW + band_offset + tap_index, A + 2 * HW - 1).astype(jnp.int32)
            gathered = jnp.take_along_axis(padded, jnp.broadcast_to(source_index[None], (2, A, F)), axis=1)
            accumulated = accumulated + jnp.where((tap_index < tap_count)[None], weights[tap_index][None] * gathered, 0.0)
        interpolated = accumulated.astype(jnp.bfloat16)
        range_real, range_imag = complex_dot(interpolated[0], interpolated[1], cos_f, sin_f)
        ranged = (jnp.stack([range_real, range_imag]) * (1.0 / math.sqrt(F))).astype(jnp.bfloat16)
        transposed = jnp.swapaxes(ranged, 1, 2)
        cross_real, cross_imag = complex_dot(transposed[0], transposed[1], cos_a, sin_a)
        return (jnp.stack([cross_real, cross_imag]) * (1.0 / math.sqrt(A))).astype(jnp.bfloat16)
    crossed = lax.map(one_cut, jnp.moveaxis(polar, 1, 0))
    flattened = crossed.astype(jnp.float32).reshape(E, 2, F * A)
    cos_wide = cos_e.astype(jnp.float32)
    sin_wide = sin_e.astype(jnp.float32)
    high = lax.Precision.HIGHEST
    height_real = jnp.einsum('eh,ex->hx', cos_wide, flattened[:, 0], precision=high) - jnp.einsum('eh,ex->hx', sin_wide, flattened[:, 1], precision=high)
    height_imag = jnp.einsum('eh,ex->hx', sin_wide, flattened[:, 0], precision=high) + jnp.einsum('eh,ex->hx', cos_wide, flattened[:, 1], precision=high)
    image_out = (jnp.stack([height_real, height_imag]) * (1.0 / math.sqrt(E))).astype(jnp.bfloat16)
    return image_out.reshape(2, E, F, A)
```

```python
import math

import jax
import jax.numpy as jnp
import ml_dtypes
import numpy as np
from jax import lax
from jax.experimental import pallas as pl
from jax.experimental.pallas import tpu as pltpu
from jax.sharding import PartitionSpec as P

F = 768
A = 1024
E = 32
HW = 8
KT = 8

LANES = 128
ROWS = 16


def with_halo(cells, sides, width):
    for axis, dim in sides:
        count = lax.axis_size(axis)
        ends = count - 1
        head = lax.slice_in_dim(cells, 0, width, axis=dim)
        tail = lax.slice_in_dim(cells, cells.shape[dim] - width, cells.shape[dim], axis=dim)
        cells = jnp.concatenate(
            [
                lax.ppermute(tail, axis, [(i, (i + 1) % count) for i in range(ends)]),
                cells,
                lax.ppermute(head, axis, [((i + 1) % count, i) for i in range(ends)]),
            ],
            axis=dim,
        )
    return cells


def table_pair(row_ids, col_ids, length):
    product = row_ids[:, None] * col_ids[None, :] % length
    angle = product.astype(jnp.float32) * (2.0 * math.pi / length)
    return (jnp.cos(angle).astype(jnp.bfloat16), jnp.sin(angle).astype(jnp.bfloat16))


def general_path(polar, band_offset, tap_count, tap_weight):
    shape_all = polar.shape
    col_count = shape_all[2]
    freq_count = shape_all[3]
    az_count = lax.axis_size("az")
    fq_count = lax.axis_size("fq")
    el_count = lax.axis_size("el")
    padded = with_halo(polar, (("az", 2),), HW)
    window = col_count + 2 * HW
    column = jnp.arange(col_count, dtype=jnp.int32)[:, None]
    position = jnp.arange(window, dtype=jnp.int32)[None, :, None]
    band_matrix = jnp.zeros((col_count, window, freq_count), jnp.bfloat16)
    for tap_index in range(KT):
        reach = column + HW + band_offset + tap_index
        matches = (position == reach[:, None, :]) & (tap_index < tap_count)[:, None, :]
        band_matrix = jnp.where(matches, tap_weight[tap_index][:, None, :], band_matrix)
    interpolated = jnp.einsum(
        "jaf,ceaf->cejf", band_matrix, padded, preferred_element_type=jnp.float32
    ).astype(jnp.bfloat16)
    fq_index = lax.axis_index("fq")
    bin_count = F // (fq_count * az_count)
    az_block = jnp.arange(az_count, dtype=jnp.int32)[:, None]
    bin_local = jnp.arange(bin_count, dtype=jnp.int32)[None, :]
    range_bins = ((az_block * fq_count + fq_index) * bin_count + bin_local).reshape(-1)
    cos_f, sin_f = table_pair(jnp.arange(F, dtype=jnp.int32), range_bins, F)
    shard_piece = lax.all_gather(interpolated, "fq", axis=3, tiled=True)
    cos_rows = cos_f
    sin_rows = sin_f
    real_part = jnp.einsum(
        "ejf,fk->ekj", shard_piece[0], cos_rows, preferred_element_type=jnp.float32
    ) - jnp.einsum("ejf,fk->ekj", shard_piece[1], sin_rows, preferred_element_type=jnp.float32)
    imag_part = jnp.einsum(
        "ejf,fk->ekj", shard_piece[0], sin_rows, preferred_element_type=jnp.float32
    ) + jnp.einsum("ejf,fk->ekj", shard_piece[1], cos_rows, preferred_element_type=jnp.float32)
    summed = jnp.stack([real_part, imag_part])
    ranged = (summed * (1.0 / math.sqrt(F))).astype(jnp.bfloat16)
    azim_ids = jnp.arange(A, dtype=jnp.int32)
    cos_a, sin_a = table_pair(azim_ids, azim_ids, A)
    block_data = lax.all_to_all(ranged, "az", split_axis=2, concat_axis=3, tiled=True)
    real_part = jnp.einsum(
        "ekj,jm->ekm", block_data[0], cos_a, preferred_element_type=jnp.float32
    ) - jnp.einsum("ekj,jm->ekm", block_data[1], sin_a, preferred_element_type=jnp.float32)
    imag_part = jnp.einsum(
        "ekj,jm->ekm", block_data[0], sin_a, preferred_element_type=jnp.float32
    ) + jnp.einsum("ekj,jm->ekm", block_data[1], cos_a, preferred_element_type=jnp.float32)
    crossed = (jnp.stack([real_part, imag_part]) * (1.0 / math.sqrt(A))).astype(jnp.bfloat16)
    elev_ids = jnp.arange(E, dtype=jnp.int32)
    el_index = lax.axis_index("el")
    height_count = E // el_count
    height_rows = el_index * height_count + jnp.arange(height_count, dtype=jnp.int32)
    cos_e, sin_e = table_pair(elev_ids, height_rows, E)
    shard_piece = lax.all_gather(crossed, "el", axis=1, tiled=True)
    cos_rows = cos_e
    sin_rows = sin_e
    real_part = jnp.einsum(
        "eh,ekm->hkm", cos_rows, shard_piece[0], preferred_element_type=jnp.float32
    ) - jnp.einsum("eh,ekm->hkm", sin_rows, shard_piece[1], preferred_element_type=jnp.float32)
    imag_part = jnp.einsum(
        "eh,ekm->hkm", sin_rows, shard_piece[0], preferred_element_type=jnp.float32
    ) + jnp.einsum("eh,ekm->hkm", cos_rows, shard_piece[1], preferred_element_type=jnp.float32)
    totals = jnp.stack([real_part, imag_part])
    image_out = (totals * (1.0 / math.sqrt(E))).astype(jnp.bfloat16)
    return image_out


CUTS = (2, 4, 4, 6)
SPLIT = 32
VMEM = 56 * 1024 * 1024


def host_table(row_ids, col_ids, length):
    product = (row_ids[:, None] * col_ids[None, :]) % length
    angle = product.astype(np.float32) * np.float32(2.0 * math.pi / length)
    return (np.cos(angle).astype(ml_dtypes.bfloat16), np.sin(angle).astype(ml_dtypes.bfloat16))


def params():
    return pltpu.CompilerParams(vmem_limit_bytes=VMEM)


def cost(flops, nbytes):
    return pl.CostEstimate(flops=int(flops), bytes_accessed=int(nbytes), transcendentals=0)


def band_kernel(offset_ref, count_ref, weight_ref, out_ref):
    rows, freqs = offset_ref.shape

    def tile(index, carry):
        row = pl.ds(pl.multiple_of(index * ROWS, ROWS), ROWS)
        for start in range(0, freqs, LANES):
            lane = pl.ds(start, LANES)
            base = offset_ref[row, lane] + HW
            count = count_ref[row, lane]
            zero = jnp.zeros((ROWS, LANES), jnp.float32)
            slots = [
                jnp.where(count > tap, weight_ref[tap, row, lane].astype(jnp.float32), zero)
                for tap in range(KT)
            ]
            step = 1
            while step < 2 * HW:
                chosen = (base & step) != 0
                size = min(len(slots) + step, 2 * HW + 1)
                slots = [
                    jnp.where(
                        chosen,
                        slots[d - step] if 0 <= d - step < len(slots) else zero,
                        slots[d] if d < len(slots) else zero,
                    )
                    for d in range(size)
                ]
                step *= 2
            for d in range(2 * HW + 1):
                value = slots[d] if d < len(slots) else zero
                out_ref[d, row, lane] = value.astype(jnp.bfloat16)
        return carry

    lax.fori_loop(0, rows // ROWS, tile, 0)


def expand_bands(band_offset, tap_count, tap_weight):
    cols, freqs = band_offset.shape
    step = cols // 4
    return pl.pallas_call(
        band_kernel,
        grid=(4,),
        in_specs=[
            pl.BlockSpec((step, freqs), lambda i: (i, 0)),
            pl.BlockSpec((step, freqs), lambda i: (i, 0)),
            pl.BlockSpec((KT, step, freqs), lambda i: (0, i, 0)),
        ],
        out_specs=pl.BlockSpec((2 * HW + 1, step, freqs), lambda i: (0, i, 0)),
        out_shape=jax.ShapeDtypeStruct((2 * HW + 1, cols, freqs), jnp.bfloat16),
        compiler_params=params(),
        cost_estimate=cost(100 * cols * freqs, 58 * cols * freqs),
        name="expand_bands",
    )(band_offset, tap_count, tap_weight)


def interp_kernel(polar_ref, halo_ref, band_ref, out_ref, pad_ref):
    _, cuts, cols, freqs = polar_ref.shape
    for part in range(2):
        for cut in range(cuts):
            plane = part * cuts + cut
            for f in range(freqs // LANES):
                lane = pl.ds(f * LANES, LANES)
                halo = halo_ref[part, cut, :, lane].astype(jnp.float32)
                pad_ref[plane, f, pl.ds(0, HW), :] = halo[:HW]
                pad_ref[plane, f, pl.ds(HW, cols), :] = polar_ref[part, cut, :, lane].astype(jnp.float32)
                pad_ref[plane, f, pl.ds(HW + cols, HW), :] = halo[HW:]

    def tile(index, carry):
        row = pl.multiple_of(index * ROWS, ROWS)
        for f in range(freqs // LANES):
            lane = pl.ds(f * LANES, LANES)
            bands = [
                band_ref[d, pl.ds(row, ROWS), lane].astype(jnp.float32) for d in range(2 * HW + 1)
            ]
            for part in range(2):
                for cut in range(cuts):
                    plane = part * cuts + cut
                    total = bands[0] * pad_ref[plane, f, pl.ds(row, ROWS), :]
                    for d in range(1, 2 * HW + 1):
                        total = total + bands[d] * pad_ref[plane, f, pl.ds(row + d, ROWS), :]
                    out_ref[part, cut, pl.ds(row, ROWS), lane] = total.astype(jnp.bfloat16)
        return carry

    lax.fori_loop(0, cols // ROWS, tile, 0)


def interpolate(polar, halo, bands, first, count):
    _, _, cols, freqs = polar.shape
    group = 2
    skip = first // group
    return pl.pallas_call(
        interp_kernel,
        grid=(count // group,),
        in_specs=[
            pl.BlockSpec((2, group, cols, freqs), lambda i: (0, skip + i, 0, 0)),
            pl.BlockSpec((2, group, 2 * HW, freqs), lambda i: (0, skip + i, 0, 0)),
            pl.BlockSpec((2 * HW + 1, cols, freqs), lambda i: (0, 0, 0)),
        ],
        out_specs=pl.BlockSpec((2, group, cols, freqs), lambda i: (0, i, 0, 0)),
        out_shape=jax.ShapeDtypeStruct((2, count, cols, freqs), jnp.bfloat16),
        scratch_shapes=[
            pltpu.VMEM((2 * group, freqs // LANES, cols + 2 * HW, LANES), jnp.float32)
        ],
        compiler_params=params(),
        cost_estimate=cost(2 * count * cols * freqs * 34, 8 * count * cols * freqs),
        name="interpolate",
    )(polar, halo, bands)


def range_kernel(ids_ref, own_ref, other_ref, table_ref, *refs):
    first_ref, rest, product = refs[0], refs[1:-1], refs[-1]
    blocks, rows2, _ = product.shape[1:]
    bins = rows2 // 2
    split = first_ref.shape[3]
    table = table_ref[0].reshape(blocks * rows2, table_ref.shape[3])
    for part in range(2):
        values = jnp.concatenate([own_ref[part, 0], other_ref[part, 0]], axis=1)
        product[part] = lax.dot_general(
            table, values, (((1,), (1,)), ((), ())), preferred_element_type=jnp.float32
        ).reshape(product.shape[1:])
    az = ids_ref[0]
    scale = 1.0 / math.sqrt(F)
    for s in range(blocks):
        block = az ^ s
        real = (product[0, block, :bins] - product[1, block, bins:]) * scale
        imag = (product[0, block, bins:] + product[1, block, :bins]) * scale
        for part, value in ((0, real), (1, imag)):
            value = value.astype(jnp.bfloat16)
            first_ref[part, 0, s] = value[:split]
            rest[s][part, 0] = value[split:]


def range_transform(ids, own, other, table, split):
    _, count, cols, freqs = own.shape
    _, blocks, rows2, full = table.shape
    bins = rows2 // 2
    rest = bins - split
    return pl.pallas_call(
        range_kernel,
        grid_spec=pltpu.PrefetchScalarGridSpec(
            num_scalar_prefetch=1,
            grid=(count,),
            in_specs=[
                pl.BlockSpec((2, 1, cols, freqs), lambda i, ids: (0, i, 0, 0)),
                pl.BlockSpec((2, 1, cols, freqs), lambda i, ids: (0, i, 0, 0)),
                pl.BlockSpec((1, blocks, rows2, full), lambda i, ids: (ids[1], 0, 0, 0)),
            ],
            out_specs=[pl.BlockSpec((2, 1, blocks, split, cols), lambda i, ids: (0, i, 0, 0, 0))]
            + [pl.BlockSpec((2, 1, rest, cols), lambda i, ids: (0, i, 0, 0))] * blocks,
            scratch_shapes=[pltpu.VMEM((2, blocks, rows2, cols), jnp.float32)],
        ),
        out_shape=[jax.ShapeDtypeStruct((2, count, blocks, split, cols), jnp.bfloat16)]
        + [jax.ShapeDtypeStruct((2, count, rest, cols), jnp.bfloat16)] * blocks,
        compiler_params=params(),
        cost_estimate=cost(4 * count * cols * full * blocks * rows2, 12 * count * cols * freqs),
        name="range_transform",
    )(ids, own, other, table)


def spin(value, real, imag):
    return (value[0] * real - value[1] * imag, value[0] * imag + value[1] * real)


def add(a, b):
    return (a[0] + b[0], a[1] + b[1])


def sub(a, b):
    return (a[0] - b[0], a[1] - b[1])


def turned(value, num, den):
    num %= den
    if num == 0:
        return value
    if 4 * num == den:
        return (-value[1], value[0])
    if 2 * num == den:
        return (-value[0], -value[1])
    angle = 2.0 * math.pi * num / den
    if 8 * num == den:
        root = math.sqrt(0.5)
        return ((value[0] - value[1]) * root, (value[0] + value[1]) * root)
    if 8 * num == 3 * den:
        root = math.sqrt(0.5)
        return ((value[0] + value[1]) * -root, (value[0] - value[1]) * root)
    return spin(value, math.cos(angle), math.sin(angle))


def fourier(points):
    n = len(points)
    if n == 1:
        return points
    even, odd = fourier(points[0::2]), fourier(points[1::2])
    odd = [turned(v, g, n) for g, v in enumerate(odd)]
    return [add(a, b) for a, b in zip(even, odd)] + [sub(a, b) for a, b in zip(even, odd)]


def half_fourier(points, sign):
    n = len(points)
    even, odd = fourier(points[0::2]), fourier(points[1::2])
    out = []
    for g in range(n // 2):
        angle = 2.0 * math.pi * g / n
        if g == 0:
            turn = (odd[g][0] * sign, odd[g][1] * sign)
        else:
            turn = spin(odd[g], sign * math.cos(angle), sign * math.sin(angle))
        out.append(add(even[g], turn))
    return out


def heights(own, other, sign):
    n = len(own)
    even = half_fourier([add(a, b) for a, b in zip(own, other)], sign)
    odd = []
    for e, (a, b) in enumerate(zip(own, other)):
        angle = math.pi * e / n
        odd.append(spin(sub(a, b), sign * math.cos(angle), sign * math.sin(angle)))
    odd = half_fourier(odd, sign)
    return [v for pair in zip(even, odd) for v in pair]


def height_kernel(ids_ref, *refs, chunks, outs, scale, aliased):
    ins = refs[: 2 * chunks]
    out_refs = refs[2 * chunks + aliased : 2 * chunks + aliased + outs]
    sign = (1 - 2 * ids_ref[2]).astype(jnp.float32)
    lanes = ins[0].shape[-1]

    def tile(index, carry):
        lane = pl.ds(pl.multiple_of(index * LANES, LANES), LANES)

        def cuts_of(group):
            found = []
            for ref in group:
                for e in range(ref.shape[1]):
                    pad = (0,) * (len(ref.shape) - 4)
                    found.append(
                        tuple(
                            ref[(part, e) + pad + (slice(None), lane)].astype(jnp.float32)
                            for part in range(2)
                        )
                    )
            return found

        result = heights(cuts_of(ins[:chunks]), cuts_of(ins[chunks:]), sign)
        h = 0
        for ref in out_refs:
            for row in range(ref.shape[1]):
                for part in range(2):
                    value = result[h][part]
                    if scale is not None:
                        value = value * scale
                    ref[part, row, :, lane] = value.astype(jnp.bfloat16)
                h += 1
        return carry

    lax.fori_loop(0, lanes // LANES, tile, 0)


def first_heights(ids, own, other, s, parts):
    chunks = len(own)
    _, _, _, split, cols = own[0].shape
    total = sum(v.shape[1] for v in own)
    spec = [
        pl.BlockSpec((2, v.shape[1], 1, ROWS, cols), lambda i, ids: (0, 0, s, i, 0)) for v in own
    ]
    return pl.pallas_call(
        lambda *refs: height_kernel(*refs, chunks=chunks, outs=len(parts), scale=None, aliased=0),
        grid_spec=pltpu.PrefetchScalarGridSpec(
            num_scalar_prefetch=1,
            grid=(split // ROWS,),
            in_specs=spec + spec,
            out_specs=[
                pl.BlockSpec((2, h, ROWS, cols), lambda i, ids: (0, 0, i, 0)) for h in parts
            ],
        ),
        out_shape=[jax.ShapeDtypeStruct((2, h, split, cols), jnp.bfloat16) for h in parts],
        compiler_params=params(),
        cost_estimate=cost(split * cols * 700, 12 * total * split * cols),
        name="first_heights",
    )(ids, *own, *other)


def last_heights(ids, own, other, image, shape, skip, rows, offset):
    chunks = len(own)
    full = own[0].shape[3]
    width = min(full, 512)
    total = sum(v.shape[1] for v in own)
    spec = [
        pl.BlockSpec((2, v.shape[1], ROWS, width), lambda i, j, ids: (0, 0, offset // ROWS + i, j))
        for v in own
    ]
    extra = [] if image is None else [image]
    first = skip // ROWS
    return pl.pallas_call(
        lambda *refs: height_kernel(
            *refs, chunks=chunks, outs=1, scale=1.0 / math.sqrt(2 * total), aliased=len(extra)
        ),
        grid_spec=pltpu.PrefetchScalarGridSpec(
            num_scalar_prefetch=1,
            grid=(rows // ROWS, full // width),
            in_specs=spec + spec + [pl.BlockSpec(memory_space=pl.ANY)] * len(extra),
            out_specs=pl.BlockSpec((2, total, ROWS, width), lambda i, j, ids: (0, 0, first + i, j)),
        ),
        out_shape=jax.ShapeDtypeStruct(shape, jnp.bfloat16),
        input_output_aliases={1 + 2 * chunks: 0} if extra else {},
        compiler_params=params(),
        cost_estimate=cost(rows * full * 700, 12 * total * rows * full),
        name="last_heights",
    )(ids, *own, *other, *extra)


def cross_kernel(ids_ref, *refs, blocks, scale, aliased):
    ins = refs[:blocks]
    cos_ref, sin_ref = refs[blocks : blocks + 2]
    out_ref, rows_ref = refs[blocks + 2 + aliased :]
    _, cuts, bins, cols = ins[0].shape
    rows = cuts * bins

    @pl.when(pl.program_id(0) == 0)
    def _():
        for s, ref in enumerate(ins):
            start = pl.multiple_of((ids_ref[0] ^ s) * cols, cols)
            rows_ref[:, pl.ds(start, cols)] = ref[...].reshape(2 * rows, cols)

    values = rows_ref[...]
    with_cos = jnp.dot(values, cos_ref[...], preferred_element_type=jnp.float32)
    with_sin = jnp.dot(values, sin_ref[...], preferred_element_type=jnp.float32)
    real = (with_cos[:rows] - with_sin[rows:]) * scale
    imag = (with_sin[:rows] + with_cos[rows:]) * scale
    out_ref[0] = real.astype(jnp.bfloat16).reshape(out_ref.shape[1:])
    out_ref[1] = imag.astype(jnp.bfloat16).reshape(out_ref.shape[1:])


def cross_transform(ids, ins, tables, scale, image=None, shape=None, place=0):
    blocks = len(ins)
    _, cuts, bins, cols = ins[0].shape
    full = tables[0].shape[1]
    width = min(full, 256)
    extra = [] if image is None else [image]
    if shape is None:
        shape = (2, cuts, bins, full)
    return pl.pallas_call(
        lambda *refs: cross_kernel(*refs, blocks=blocks, scale=scale, aliased=len(extra)),
        grid_spec=pltpu.PrefetchScalarGridSpec(
            num_scalar_prefetch=1,
            grid=(full // width,),
            in_specs=[pl.BlockSpec((2, cuts, bins, cols), lambda i, ids: (0, 0, 0, 0))] * blocks
            + [pl.BlockSpec((full, width), lambda i, ids: (0, i))] * 2
            + [pl.BlockSpec(memory_space=pl.ANY)] * len(extra),
            out_specs=pl.BlockSpec((2, cuts, bins, width), lambda i, ids: (0, place, 0, i)),
            scratch_shapes=[pltpu.VMEM((2 * cuts * bins, full), jnp.bfloat16)],
        ),
        out_shape=jax.ShapeDtypeStruct(shape, jnp.bfloat16),
        input_output_aliases={1 + blocks + 2: 0} if extra else {},
        compiler_params=params(),
        cost_estimate=cost(8 * cuts * bins * full * full, 8 * cuts * bins * full + 4 * full * full),
        name="cross_transform",
    )(ids, *ins, *tables, *extra)


def exchange(value, axis, s):
    return lax.ppermute(value, axis, [(i, i ^ s) for i in range(lax.axis_size(axis))])


def halo_rows(polar):
    count = lax.axis_size("az")
    cols = polar.shape[2]
    ends = count - 1
    head = lax.slice_in_dim(polar, 0, HW, axis=2)
    tail = lax.slice_in_dim(polar, cols - HW, cols, axis=2)
    return jnp.concatenate(
        [
            lax.ppermute(tail, "az", [(i, i + 1) for i in range(ends)]),
            lax.ppermute(head, "az", [(i + 1, i) for i in range(ends)]),
        ],
        axis=2,
    )


def planned_path(polar, band_offset, tap_count, tap_weight):
    _, cuts, cols, freqs = polar.shape
    az_count = lax.axis_size("az")
    fq_count = lax.axis_size("fq")
    bins = F // (az_count * fq_count)
    split = SPLIT
    ids = jnp.stack([lax.axis_index("az"), lax.axis_index("fq"), lax.axis_index("el")])
    tables = []
    for core in range(fq_count):
        order = np.concatenate([np.arange(freqs) + freqs * (core ^ s) for s in range(fq_count)])
        blocks = []
        for az in range(az_count):
            ks = (az * fq_count + core) * bins + np.arange(bins)
            blocks.append(np.concatenate(host_table(ks, order, F)))
        tables.append(np.stack(blocks))
    range_table = jnp.asarray(np.stack(tables))
    cross_tables = [jnp.asarray(t) for t in host_table(np.arange(A), np.arange(A), A)]

    halo = halo_rows(polar)
    bands = expand_bands(band_offset, tap_count, tap_weight)
    own_first, other_first = [], []
    own_last, other_last = [], []
    start = 0
    for count in CUTS:
        own = interpolate(polar, halo, bands, start, count)
        other = exchange(own, "fq", 1)
        first, *rest = range_transform(ids, own, other, range_table, split)
        own_first.append(first)
        other_first.append(exchange(first, "el", 1))
        landed = [rest[0]] + [exchange(rest[s], "az", s) for s in range(1, az_count)]
        crossed = cross_transform(ids, landed, cross_tables, 1.0 / math.sqrt(A))
        own_last.append(crossed)
        other_last.append(exchange(crossed, "el", 1))
        start += count
    parts = (cuts // 2, cuts // 2)
    landed = [[] for _ in parts]
    for s in reversed(range(az_count)):
        made = first_heights(ids, own_first, other_first, s, parts)
        for p, value in enumerate(made):
            landed[p].insert(0, exchange(value, "az", s) if s else value)
    shape = (2, cuts, bins, A)
    scale = 1.0 / math.sqrt(A * 2 * cuts)
    image = cross_transform(ids, landed[0], cross_tables, scale, None, shape, 0)
    image = last_heights(ids, own_last, other_last, image, shape, split, bins - split, 0)
    image = cross_transform(ids, landed[1], cross_tables, scale, image, shape, 1)
    return image


def on_device(polar, band_offset, tap_count, tap_weight):
    _, cuts, cols, freqs = polar.shape
    az_count = lax.axis_size("az")
    bins = F // (az_count * lax.axis_size("fq"))
    fits = (
        lax.axis_size("el") == 2
        and lax.axis_size("fq") == 2
        and az_count in (2, 4)
        and cuts == sum(CUTS)
        and cols % (2 * LANES) == 0
        and freqs % LANES == 0
        and bins > SPLIT
        and bins % SPLIT == 0
        and A % 512 == 0
        and 2 * HW == ROWS
    )
    chosen = planned_path if fits else general_path
    return chosen(polar, band_offset, tap_count, tap_weight)


def solution(mesh):
    in_specs = (
        P(None, ("grp", "el"), "az", "fq"),
        P("az", "fq"),
        P("az", "fq"),
        P(None, "az", "fq"),
    )
    out_specs = P(None, ("grp", "el"), ("az", "fq"), None)
    return jax.shard_map(
        on_device, mesh=mesh, in_specs=in_specs, out_specs=out_specs, check_vma=False
    )
```

```python
import math

import jax
import jax.numpy as jnp
import ml_dtypes
import numpy as np
from jax import lax
from jax.experimental import pallas as pl
from jax.experimental.pallas import tpu as pltpu
from jax.sharding import PartitionSpec as P

F = 768
A = 1024
E = 32
HW = 8
KT = 8

LANES = 128
ROWS = 16


def with_halo(cells, sides, width):
    for axis, dim in sides:
        count = lax.axis_size(axis)
        ends = count - 1
        head = lax.slice_in_dim(cells, 0, width, axis=dim)
        tail = lax.slice_in_dim(cells, cells.shape[dim] - width, cells.shape[dim], axis=dim)
        cells = jnp.concatenate(
            [
                lax.ppermute(tail, axis, [(i, (i + 1) % count) for i in range(ends)]),
                cells,
                lax.ppermute(head, axis, [((i + 1) % count, i) for i in range(ends)]),
            ],
            axis=dim,
        )
    return cells


def table_pair(row_ids, col_ids, length):
    product = row_ids[:, None] * col_ids[None, :] % length
    angle = product.astype(jnp.float32) * (2.0 * math.pi / length)
    return (jnp.cos(angle).astype(jnp.bfloat16), jnp.sin(angle).astype(jnp.bfloat16))


def general_path(polar, band_offset, tap_count, tap_weight):
    shape_all = polar.shape
    col_count = shape_all[2]
    freq_count = shape_all[3]
    az_count = lax.axis_size("az")
    fq_count = lax.axis_size("fq")
    el_count = lax.axis_size("el")
    padded = with_halo(polar, (("az", 2),), HW)
    window = col_count + 2 * HW
    column = jnp.arange(col_count, dtype=jnp.int32)[:, None]
    position = jnp.arange(window, dtype=jnp.int32)[None, :, None]
    band_matrix = jnp.zeros((col_count, window, freq_count), jnp.bfloat16)
    for tap_index in range(KT):
        reach = column + HW + band_offset + tap_index
        matches = (position == reach[:, None, :]) & (tap_index < tap_count)[:, None, :]
        band_matrix = jnp.where(matches, tap_weight[tap_index][:, None, :], band_matrix)
    interpolated = jnp.einsum(
        "jaf,ceaf->cejf", band_matrix, padded, preferred_element_type=jnp.float32
    ).astype(jnp.bfloat16)
    fq_index = lax.axis_index("fq")
    bin_count = F // (fq_count * az_count)
    az_block = jnp.arange(az_count, dtype=jnp.int32)[:, None]
    bin_local = jnp.arange(bin_count, dtype=jnp.int32)[None, :]
    range_bins = ((az_block * fq_count + fq_index) * bin_count + bin_local).reshape(-1)
    cos_f, sin_f = table_pair(jnp.arange(F, dtype=jnp.int32), range_bins, F)
    shard_piece = lax.all_gather(interpolated, "fq", axis=3, tiled=True)
    cos_rows = cos_f
    sin_rows = sin_f
    real_part = jnp.einsum(
        "ejf,fk->ekj", shard_piece[0], cos_rows, preferred_element_type=jnp.float32
    ) - jnp.einsum("ejf,fk->ekj", shard_piece[1], sin_rows, preferred_element_type=jnp.float32)
    imag_part = jnp.einsum(
        "ejf,fk->ekj", shard_piece[0], sin_rows, preferred_element_type=jnp.float32
    ) + jnp.einsum("ejf,fk->ekj", shard_piece[1], cos_rows, preferred_element_type=jnp.float32)
    summed = jnp.stack([real_part, imag_part])
    ranged = (summed * (1.0 / math.sqrt(F))).astype(jnp.bfloat16)
    azim_ids = jnp.arange(A, dtype=jnp.int32)
    cos_a, sin_a = table_pair(azim_ids, azim_ids, A)
    block_data = lax.all_to_all(ranged, "az", split_axis=2, concat_axis=3, tiled=True)
    real_part = jnp.einsum(
        "ekj,jm->ekm", block_data[0], cos_a, preferred_element_type=jnp.float32
    ) - jnp.einsum("ekj,jm->ekm", block_data[1], sin_a, preferred_element_type=jnp.float32)
    imag_part = jnp.einsum(
        "ekj,jm->ekm", block_data[0], sin_a, preferred_element_type=jnp.float32
    ) + jnp.einsum("ekj,jm->ekm", block_data[1], cos_a, preferred_element_type=jnp.float32)
    crossed = (jnp.stack([real_part, imag_part]) * (1.0 / math.sqrt(A))).astype(jnp.bfloat16)
    elev_ids = jnp.arange(E, dtype=jnp.int32)
    el_index = lax.axis_index("el")
    height_count = E // el_count
    height_rows = el_index * height_count + jnp.arange(height_count, dtype=jnp.int32)
    cos_e, sin_e = table_pair(elev_ids, height_rows, E)
    shard_piece = lax.all_gather(crossed, "el", axis=1, tiled=True)
    cos_rows = cos_e
    sin_rows = sin_e
    real_part = jnp.einsum(
        "eh,ekm->hkm", cos_rows, shard_piece[0], preferred_element_type=jnp.float32
    ) - jnp.einsum("eh,ekm->hkm", sin_rows, shard_piece[1], preferred_element_type=jnp.float32)
    imag_part = jnp.einsum(
        "eh,ekm->hkm", sin_rows, shard_piece[0], preferred_element_type=jnp.float32
    ) + jnp.einsum("eh,ekm->hkm", cos_rows, shard_piece[1], preferred_element_type=jnp.float32)
    totals = jnp.stack([real_part, imag_part])
    image_out = (totals * (1.0 / math.sqrt(E))).astype(jnp.bfloat16)
    return image_out


CUTS = (6, 6, 4)
PARTS = (8, 4, 4)
SPLIT = 48
VMEM = 60 * 1024 * 1024


def host_table(row_ids, col_ids, length):
    product = (row_ids[:, None] * col_ids[None, :]) % length
    angle = product.astype(np.float32) * np.float32(2.0 * math.pi / length)
    return (np.cos(angle).astype(ml_dtypes.bfloat16), np.sin(angle).astype(ml_dtypes.bfloat16))


def params():
    return pltpu.CompilerParams(vmem_limit_bytes=VMEM)


def cost(flops, nbytes):
    return pl.CostEstimate(flops=int(flops) // 1000, bytes_accessed=int(nbytes) // 1000, transcendentals=0)


def after(values):
    return [pl.BlockSpec(memory_space=pl.ANY)] * len(values)


def band_kernel(offset_ref, count_ref, weight_ref, out_ref):
    rows, freqs = offset_ref.shape

    def tile(index, carry):
        row = pl.ds(pl.multiple_of(index * ROWS, ROWS), ROWS)
        for start in range(0, freqs, LANES):
            lane = pl.ds(start, LANES)
            base = offset_ref[row, lane] + HW
            count = count_ref[row, lane]
            zero = jnp.zeros((ROWS, LANES), jnp.float32)
            slots = [
                jnp.where(count > tap, weight_ref[tap, row, lane].astype(jnp.float32), zero)
                for tap in range(KT)
            ]
            step = 1
            while step < KT:
                chosen = (base & step) != 0
                slots = [jnp.where(chosen, slots[(r - step) % KT], slots[r]) for r in range(KT)]
                step *= 2
            for r in range(KT):
                out_ref[r, row, lane] = slots[r].astype(jnp.bfloat16)
        return carry

    lax.fori_loop(0, rows // ROWS, tile, 0)


def place_taps(band_offset, tap_count, tap_weight):
    cols, freqs = band_offset.shape
    step = cols // 2
    return pl.pallas_call(
        band_kernel,
        grid=(2,),
        in_specs=[
            pl.BlockSpec((step, freqs), lambda i: (i, 0)),
            pl.BlockSpec((step, freqs), lambda i: (i, 0)),
            pl.BlockSpec((KT, step, freqs), lambda i: (0, i, 0)),
        ],
        out_specs=pl.BlockSpec((KT, step, freqs), lambda i: (0, i, 0)),
        out_shape=jax.ShapeDtypeStruct((KT, cols, freqs), jnp.bfloat16),
        compiler_params=params(),
        cost_estimate=cost(100 * cols * freqs, 40 * cols * freqs),
        name="place_taps",
    )(band_offset, tap_count, tap_weight)


def interp_rows(pad_ref, band_ref, offset_ref, out_ref):
    _, cuts, cols, freqs = out_ref.shape

    def tile(index, carry):
        row = pl.multiple_of(index * ROWS, ROWS)
        for f in range(freqs // LANES):
            lane = pl.ds(f * LANES, LANES)
            taps = [band_ref[r, pl.ds(row, ROWS), lane].astype(jnp.float32) for r in range(KT)]
            base = offset_ref[pl.ds(row, ROWS), lane] + HW
            past = [base > r for r in range(KT + 1)]
            for part in range(2):
                for cut in range(cuts):
                    plane = part * cuts + cut
                    near = [
                        pad_ref[plane, f, pl.ds(row + d, ROWS), :] for d in range(2 * HW + 1)
                    ]
                    total = None
                    for r in range(KT):
                        value = jnp.where(past[r], near[r + KT], near[r])
                        if r == 0:
                            value = jnp.where(past[KT], near[2 * KT], value)
                        value = value * taps[r]
                        total = value if total is None else total + value
                    out_ref[part, cut, pl.ds(row, ROWS), lane] = total.astype(jnp.bfloat16)
        return carry

    lax.fori_loop(0, cols // ROWS, tile, 0)


def interp_kernel(polar_ref, band_ref, offset_ref, *refs, bordered):
    out_ref, pad_ref = refs[-2:]
    _, cuts, cols, freqs = polar_ref.shape
    for part in range(2):
        for cut in range(cuts):
            plane = part * cuts + cut
            for f in range(freqs // LANES):
                lane = pl.ds(f * LANES, LANES)
                if bordered:
                    halo = refs[0][part, cut, :, lane].astype(jnp.float32)
                else:
                    halo = jnp.zeros((2 * HW, LANES), jnp.float32)
                pad_ref[plane, f, pl.ds(0, HW), :] = halo[:HW]
                pad_ref[plane, f, pl.ds(HW, cols), :] = polar_ref[part, cut, :, lane].astype(jnp.float32)
                pad_ref[plane, f, pl.ds(HW + cols, HW), :] = halo[HW:]
    interp_rows(pad_ref, band_ref, offset_ref, out_ref)


def interpolate(polar, halo, taps, band_offset, first, count, earlier=()):
    _, _, cols, freqs = polar.shape
    group = 2
    skip = first // group
    border = [] if halo is None else [halo]
    return pl.pallas_call(
        lambda *refs: interp_kernel(*refs, bordered=len(border) == 1),
        grid=(count // group,),
        in_specs=[
            pl.BlockSpec((2, group, cols, freqs), lambda i: (0, skip + i, 0, 0)),
            pl.BlockSpec((KT, cols, freqs), lambda i: (0, 0, 0)),
            pl.BlockSpec((cols, freqs), lambda i: (0, 0)),
        ]
        + [pl.BlockSpec((2, group, 2 * HW, freqs), lambda i: (0, skip + i, 0, 0))] * len(border)
        + after(earlier),
        out_specs=pl.BlockSpec((2, group, cols, freqs), lambda i: (0, i, 0, 0)),
        out_shape=jax.ShapeDtypeStruct((2, count, cols, freqs), jnp.bfloat16),
        scratch_shapes=[
            pltpu.VMEM((2 * group, freqs // LANES, cols + 2 * HW, LANES), jnp.float32)
        ],
        compiler_params=params(),
        cost_estimate=cost(2 * count * cols * freqs * 34, 8 * count * cols * freqs),
        name="interpolate",
    )(polar, taps, band_offset, *border, *earlier)


def edge_kernel(polar_ref, halo_ref, band_ref, offset_ref, made_ref, out_ref, pad_ref):
    del made_ref
    _, cuts, rows, freqs = polar_ref.shape
    for part in range(2):
        for cut in range(cuts):
            for f in range(freqs // LANES):
                plane, lane = part * cuts + cut, pl.ds(f * LANES, LANES)
                halo = halo_ref[part, cut, :, lane].astype(jnp.float32)
                body = polar_ref[part, cut, :, lane].astype(jnp.float32)

                @pl.when(pl.program_id(0) == 0)
                def _():
                    pad_ref[plane, f, pl.ds(0, HW), :] = halo[:HW]
                    pad_ref[plane, f, pl.ds(HW, rows - HW), :] = body[: rows - HW]

                @pl.when(pl.program_id(0) == 1)
                def _():
                    pad_ref[plane, f, pl.ds(0, rows - HW), :] = body[HW:]
                    pad_ref[plane, f, pl.ds(rows - HW, HW), :] = halo[HW:]

    interp_rows(pad_ref, band_ref, offset_ref, out_ref)


def interpolate_edges(polar, halo, taps, band_offset, made):
    _, count, cols, freqs = made.shape
    wide = cols // (2 * ROWS) - 1
    last = cols // ROWS - 1
    return pl.pallas_call(
        edge_kernel,
        grid=(2,),
        in_specs=[
            pl.BlockSpec((2, count, 2 * ROWS, freqs), lambda i: (0, 0, i * wide, 0)),
            pl.BlockSpec((2, count, 2 * HW, freqs), lambda i: (0, 0, 0, 0)),
            pl.BlockSpec((KT, ROWS, freqs), lambda i: (0, i * last, 0)),
            pl.BlockSpec((ROWS, freqs), lambda i: (i * last, 0)),
            pl.BlockSpec(memory_space=pl.ANY),
        ],
        out_specs=pl.BlockSpec((2, count, ROWS, freqs), lambda i: (0, 0, i * last, 0)),
        out_shape=jax.ShapeDtypeStruct(made.shape, jnp.bfloat16),
        scratch_shapes=[pltpu.VMEM((2 * count, freqs // LANES, 2 * ROWS, LANES), jnp.float32)],
        input_output_aliases={4: 0},
        compiler_params=params(),
        cost_estimate=cost(4 * count * ROWS * freqs * 34, 16 * count * ROWS * freqs),
        name="interpolate_edges",
    )(polar, halo, taps, band_offset, made)


def range_kernel(ids_ref, own_ref, other_ref, *refs, blocks, earlier):
    tables = refs[:blocks]
    first_ref, *rest = refs[blocks + earlier :]
    cuts, cols = own_ref.shape[1:3]
    bins = tables[0].shape[2]
    split = first_ref.shape[3]
    scale = 1.0 / math.sqrt(F)
    table = jnp.concatenate([ref[0, 0] for ref in tables], axis=0)
    for cut in range(cuts):
        real = [own_ref[0, cut], other_ref[0, cut]]
        imag = [own_ref[1, cut], other_ref[1, cut]]
        values = jnp.concatenate(
            [
                jnp.concatenate(real + [-v for v in imag], axis=1),
                jnp.concatenate(imag + real, axis=1),
            ],
            axis=0,
        )
        product = lax.dot_general(
            table, values, (((1,), (1,)), ((), ())), preferred_element_type=jnp.float32
        )
        product = (product * scale).astype(jnp.bfloat16)
        for s in range(blocks):
            for part in range(2):
                value = product[s * bins : (s + 1) * bins, part * cols : (part + 1) * cols]
                first_ref[part, cut, s] = value[:split]
                rest[s][part, cut] = value[split:]


def range_transform(ids, own, other, table, split, earlier=()):
    _, count, cols, freqs = own.shape
    _, blocks, bins, full = table.shape
    rest = bins - split
    group = 2

    def block_of(s):
        return pl.BlockSpec((1, 1, bins, full), lambda i, ids: (ids[1], ids[0] ^ s, 0, 0))

    return pl.pallas_call(
        lambda *refs: range_kernel(*refs, blocks=blocks, earlier=len(earlier)),
        grid_spec=pltpu.PrefetchScalarGridSpec(
            num_scalar_prefetch=1,
            grid=(count // group,),
            in_specs=[pl.BlockSpec((2, group, cols, freqs), lambda i, ids: (0, i, 0, 0))] * 2
            + [block_of(s) for s in range(blocks)]
            + after(earlier),
            out_specs=[
                pl.BlockSpec((2, group, blocks, split, cols), lambda i, ids: (0, i, 0, 0, 0))
            ]
            + [pl.BlockSpec((2, group, rest, cols), lambda i, ids: (0, i, 0, 0))] * blocks,
        ),
        out_shape=[jax.ShapeDtypeStruct((2, count, blocks, split, cols), jnp.bfloat16)]
        + [jax.ShapeDtypeStruct((2, count, rest, cols), jnp.bfloat16)] * blocks,
        compiler_params=params(),
        cost_estimate=cost(4 * count * cols * full * blocks * bins, 12 * count * cols * freqs),
        name="range_transform",
    )(ids, own, other, *([table] * blocks), *earlier)


def height_table(cuts, rows):
    heights = []
    for el in range(2):
        pair = []
        for parity in range(2):
            h = el * cuts + parity + 2 * np.arange(cuts // 2)
            cos, sin = (t.astype(np.float32) for t in host_table(h, np.arange(cuts), 2 * cuts))
            sign = -1.0 if el and parity else 1.0
            whole = sign * np.block([[cos, -sin], [sin, cos]])
            pair.append(np.kron(whole, np.eye(rows, dtype=np.float32)))
        heights.append(np.stack(pair))
    return np.stack(heights).astype(ml_dtypes.bfloat16)


def height_kernel(ids_ref, matrix_ref, *refs, chunks, sets, outs, scale, skipped):
    ins = refs[: 2 * chunks]
    out_refs = refs[2 * chunks + skipped :]
    rows, lanes = ins[0].shape[-2:]
    half = matrix_ref.shape[2] // (2 * rows)
    for index in range(sets):
        sums, differences = [], []
        for part in range(2):
            for own, other in zip(ins[:chunks], ins[chunks:]):
                pad = (index,) if len(own.shape) == 5 else ()
                for e in range(own.shape[1]):
                    a, b = own[(part, e) + pad], other[(part, e) + pad]
                    sums.append(a + b)
                    differences.append(a - b)
        results = [
            jnp.dot(
                matrix_ref[0, parity],
                jnp.concatenate(values, axis=0),
                preferred_element_type=jnp.float32,
            )
            for parity, values in enumerate((sums, differences))
        ]
        h = 0
        for ref in out_refs[index * outs : (index + 1) * outs]:
            for row in range(ref.shape[1]):
                for part in range(2):
                    start = (part * half + h // 2) * rows
                    value = results[h % 2][start : start + rows]
                    if scale is not None:
                        value = value * scale
                    ref[part, row] = value.astype(jnp.bfloat16)
                h += 1


def first_heights(ids, matrix, own, other, pair, parts, earlier=()):
    chunks = len(own)
    _, _, blocks, split, cols = own[0].shape
    total = sum(v.shape[1] for v in own)
    sets = 2
    spec = [
        pl.BlockSpec((2, v.shape[1], sets, ROWS, cols), lambda i, ids: (0, 0, pair, i, 0))
        for v in own
    ]
    outs = list(parts) * sets
    return pl.pallas_call(
        lambda *refs: height_kernel(
            *refs, chunks=chunks, sets=sets, outs=len(parts), scale=None, skipped=len(earlier)
        ),
        grid_spec=pltpu.PrefetchScalarGridSpec(
            num_scalar_prefetch=1,
            grid=(split // ROWS,),
            in_specs=[pl.BlockSpec((1,) + matrix.shape[1:], lambda i, ids: (ids[2], 0, 0, 0))]
            + spec
            + spec
            + after(earlier),
            out_specs=[pl.BlockSpec((2, h, ROWS, cols), lambda i, ids: (0, 0, i, 0)) for h in outs],
        ),
        out_shape=[jax.ShapeDtypeStruct((2, h, split, cols), jnp.bfloat16) for h in outs],
        compiler_params=params(),
        cost_estimate=cost(sets * split * cols * 32768, 12 * sets * total * split * cols),
        name="first_heights",
    )(ids, matrix, *own, *other, *earlier)


def last_heights(ids, matrix, own, other, places, image, shape, skip, rows, earlier=()):
    chunks = len(own)
    full = own[0].shape[3]
    width = min(full, 512)
    total = sum(v.shape[1] for v in own)

    def chunk(v, place):
        return pl.BlockSpec(
            (2, v.shape[1], ROWS, width), lambda i, j, ids: (0, 0, place // ROWS + i, j)
        )

    spec = [chunk(v, place) for v, place in zip(own, places)]
    extra = [] if image is None else [image]
    first = skip // ROWS
    return pl.pallas_call(
        lambda *refs: height_kernel(
            *refs,
            chunks=chunks,
            sets=1,
            outs=1,
            scale=1.0 / math.sqrt(2 * total),
            skipped=len(earlier) + len(extra),
        ),
        grid_spec=pltpu.PrefetchScalarGridSpec(
            num_scalar_prefetch=1,
            grid=(rows // ROWS, full // width),
            in_specs=[pl.BlockSpec((1,) + matrix.shape[1:], lambda i, j, ids: (ids[2], 0, 0, 0))]
            + spec
            + spec
            + after(extra)
            + after(earlier),
            out_specs=pl.BlockSpec((2, total, ROWS, width), lambda i, j, ids: (0, 0, first + i, j)),
        ),
        out_shape=jax.ShapeDtypeStruct(shape, jnp.bfloat16),
        input_output_aliases={2 + 2 * chunks: 0} if extra else {},
        compiler_params=params(),
        cost_estimate=cost(rows * full * 32768, 12 * total * rows * full),
        name="last_heights",
    )(ids, matrix, *own, *other, *extra, *earlier)


def cross_kernel(ids_ref, *refs, groups, blocks, scale, skipped, outs):
    ins = [refs[g * blocks : (g + 1) * blocks] for g in range(groups)]
    cos_ref, sin_ref = refs[groups * blocks : groups * blocks + 2]
    out_refs = refs[groups * blocks + 2 + skipped : -1]
    rows_ref = refs[-1]
    bins, cols = ins[0][0].shape[2:]
    cuts = [group[0].shape[1] for group in ins]
    rows = sum(cuts) * bins

    @pl.when(pl.program_id(0) == 0)
    def _():
        for s in range(blocks):
            start = pl.multiple_of((ids_ref[0] ^ s) * cols, cols)
            for part in range(2):
                place = part * rows
                for group, count in zip(ins, cuts):
                    rows_ref[pl.ds(place, count * bins), pl.ds(start, cols)] = group[s][
                        part
                    ].reshape(count * bins, cols)
                    place += count * bins

    values = rows_ref[...]
    with_cos = jnp.dot(values, cos_ref[...], preferred_element_type=jnp.float32)
    with_sin = jnp.dot(values, sin_ref[...], preferred_element_type=jnp.float32)
    real = (with_cos[:rows] - with_sin[rows:]) * scale
    imag = (with_sin[:rows] + with_cos[rows:]) * scale
    for part, value in ((0, real), (1, imag)):
        value = value.astype(jnp.bfloat16).reshape(sum(cuts), bins, value.shape[1])
        place = 0
        for ref in out_refs:
            size = ref.shape[2]
            ref[part] = value[:, place : place + size]
            place += size


def cross_transform(ids, ins, tables, scale, sizes=None, image=None, shape=None, place=0, earlier=()):
    groups, blocks = len(ins), len(ins[0])
    bins, cols = ins[0][0].shape[2:]
    total = sum(group[0].shape[1] for group in ins)
    full = tables[0].shape[1]
    width = min(full, 512)
    extra = [] if image is None else [image]
    if shape is None:
        shapes = [(2, total, size, full) for size in sizes]
    else:
        sizes, shapes = [bins], [shape]
    result = pl.pallas_call(
        lambda *refs: cross_kernel(
            *refs,
            groups=groups,
            blocks=blocks,
            scale=scale,
            skipped=len(extra) + len(earlier),
            outs=len(sizes),
        ),
        grid_spec=pltpu.PrefetchScalarGridSpec(
            num_scalar_prefetch=1,
            grid=(full // width,),
            in_specs=[
                pl.BlockSpec((2, v.shape[1], bins, cols), lambda i, ids: (0, 0, 0, 0))
                for group in ins
                for v in group
            ]
            + [pl.BlockSpec((full, width), lambda i, ids: (0, i))] * 2
            + after(extra)
            + after(earlier),
            out_specs=[
                pl.BlockSpec((2, total, size, width), lambda i, ids: (0, place, 0, i))
                for size in sizes
            ],
            scratch_shapes=[pltpu.VMEM((2 * total * bins, full), jnp.bfloat16)],
        ),
        out_shape=[jax.ShapeDtypeStruct(v, jnp.bfloat16) for v in shapes],
        input_output_aliases={1 + groups * blocks + 2: 0} if extra else {},
        compiler_params=params(),
        cost_estimate=cost(8 * total * bins * full * full, 8 * total * bins * full + 4 * full * full),
        name="cross_transform",
    )(ids, *[v for group in ins for v in group], *tables, *extra, *earlier)
    return result if image is None and len(sizes) > 1 else result[0]


def exchange(value, axis, s):
    return lax.ppermute(value, axis, [(i, i ^ s) for i in range(lax.axis_size(axis))])


def halo_rows(polar):
    count = lax.axis_size("az")
    cols = polar.shape[2]
    ends = count - 1
    head = lax.slice_in_dim(polar, 0, HW, axis=2)
    tail = lax.slice_in_dim(polar, cols - HW, cols, axis=2)
    return jnp.concatenate(
        [
            lax.ppermute(tail, "az", [(i, i + 1) for i in range(ends)]),
            lax.ppermute(head, "az", [(i + 1, i) for i in range(ends)]),
        ],
        axis=2,
    )


def planned_path(polar, band_offset, tap_count, tap_weight):
    _, cuts, cols, freqs = polar.shape
    az_count = lax.axis_size("az")
    fq_count = lax.axis_size("fq")
    bins = F // (az_count * fq_count)
    split = SPLIT
    rest = bins - split
    ids = jnp.stack([lax.axis_index("az"), lax.axis_index("fq"), lax.axis_index("el")])
    tables = []
    for core in range(fq_count):
        order = np.concatenate([np.arange(freqs) + freqs * (core ^ s) for s in range(fq_count)])
        blocks = []
        for az in range(az_count):
            ks = (az * fq_count + core) * bins + np.arange(bins)
            blocks.append(np.concatenate(host_table(ks, order, F), axis=1))
        tables.append(np.stack(blocks))
    range_table = jnp.asarray(np.stack(tables))
    cross_tables = [jnp.asarray(t) for t in host_table(np.arange(A), np.arange(A), A)]
    matrix = jnp.asarray(height_table(cuts, ROWS))

    taps = place_taps(band_offset, tap_count, tap_weight)
    polar, taps = lax.optimization_barrier((polar, taps))
    halo = halo_rows(polar)
    starts = np.cumsum((0,) + CUTS)
    last = len(CUTS) - 1
    scale = 1.0 / math.sqrt(A)

    def interp(i, earlier=()):
        return interpolate(polar, halo, taps, band_offset, int(starts[i]), CUTS[i], earlier)

    def to_owners(blocks):
        come = {s: exchange(blocks[s], "az", s) for s in reversed(range(1, az_count))}
        return [blocks[0]] + [come[s] for s in range(1, az_count)]

    bare = interpolate(polar, None, taps, band_offset, 0, CUTS[0])
    made = interpolate_edges(polar, halo, taps, band_offset, bare)
    other = exchange(made, "fq", 1)
    ahead = interp(1, (made,))
    own_first, other_first, landed = [], [], []
    moving = ([], ())
    for i in range(last + 1):
        first, *blocks = range_transform(ids, made, other, range_table, split, (ahead,))
        if 0 < i < last:
            ahead = interp(i + 1, (first,))
        held = (first, blocks, ahead, moving)
        first, blocks, ahead, moving = lax.optimization_barrier(held)
        if i > 0:
            landed.append(moving[0])
            other_first.append(moving[1])
        own_first.append(first)
        moving = (to_owners(blocks), exchange(first, "el", 1))
        if i < last:
            made, other = ahead, exchange(ahead, "fq", 1)
    c0 = cross_transform(ids, landed, cross_tables, scale, [rest], earlier=(first,))
    c0, moving = lax.optimization_barrier((c0, moving))
    landed.append(moving[0])
    other_first.append(moving[1])
    other_c0 = exchange(c0, "el", 1)

    h1 = first_heights(ids, matrix, own_first, other_first, 1, PARTS, (c0,))
    count = len(PARTS)
    far = [h1[:count], h1[count:]]
    h0 = first_heights(ids, matrix, own_first, other_first, 0, PARTS, (h1[0],))
    near = [h0[:count], h0[count:]]
    made = [[near[0][p], near[1][p], far[0][p], far[1][p]] for p in range(count)]
    late = [rest - ROWS, ROWS]
    c1, c2 = cross_transform(ids, landed[-1:], cross_tables, scale, late, earlier=(h0[0],))
    other_c1 = exchange(c1, "el", 1)
    arrived = [to_owners(made[0])]
    shape = (2, cuts, bins, A)
    full_scale = 1.0 / math.sqrt(A * 2 * cuts)
    made[1], arrived[0] = lax.optimization_barrier((made[1], arrived[0]))
    arrived.append(to_owners(made[1]))
    image = cross_transform(
        ids, [arrived[0]], cross_tables, full_scale, image=None, shape=shape, place=0, earlier=(c1,)
    )
    made[2], arrived[1], c2, other_c0, image = lax.optimization_barrier(
        (made[2], arrived[1], c2, other_c0, image)
    )
    arrived.append(to_owners(made[2]))
    other_c2 = exchange(c2, "el", 1)
    image = cross_transform(
        ids, [arrived[1]], cross_tables, full_scale, image=image, shape=shape, place=PARTS[0] // PARTS[1]
    )
    image = last_heights(
        ids, matrix, [c0, c1], [other_c0, other_c1], (0, 0), image, shape, split, late[0]
    )
    image = last_heights(
        ids, matrix, [c0, c2], [other_c0, other_c2], (late[0], 0), image, shape, split + late[0], late[1]
    )
    image = cross_transform(
        ids,
        [arrived[2]],
        cross_tables,
        full_scale,
        image=image,
        shape=shape,
        place=(PARTS[0] + PARTS[1]) // PARTS[2],
    )
    return image


def on_device(polar, band_offset, tap_count, tap_weight):
    _, cuts, cols, freqs = polar.shape
    az_count = lax.axis_size("az")
    bins = F // (az_count * lax.axis_size("fq"))
    fits = (
        lax.axis_size("el") == 2
        and lax.axis_size("fq") == 2
        and az_count == 4
        and cuts == sum(CUTS) == sum(PARTS)
        and cols % (2 * LANES) == 0
        and freqs % LANES == 0
        and bins > SPLIT
        and bins == 2 * SPLIT
        and A % 512 == 0
        and 2 * HW == ROWS
    )
    chosen = planned_path if fits else general_path
    return chosen(polar, band_offset, tap_count, tap_weight)


def solution(mesh):
    in_specs = (
        P(None, ("grp", "el"), "az", "fq"),
        P("az", "fq"),
        P("az", "fq"),
        P(None, "az", "fq"),
    )
    out_specs = P(None, ("grp", "el"), ("az", "fq"), None)
    return jax.shard_map(
        on_device, mesh=mesh, in_specs=in_specs, out_specs=out_specs, check_vma=False
    )
```

```python
import math

import jax
import jax.numpy as jnp
import ml_dtypes
import numpy as np
from jax import lax
from jax.experimental import pallas as pl
from jax.experimental.pallas import tpu as pltpu
from jax.sharding import PartitionSpec as P

F = 768
A = 1024
E = 32
HW = 8
KT = 8

LANES = 128
ROWS = 16


def with_halo(cells, sides, width):
    for axis, dim in sides:
        count = lax.axis_size(axis)
        ends = count - 1
        head = lax.slice_in_dim(cells, 0, width, axis=dim)
        tail = lax.slice_in_dim(cells, cells.shape[dim] - width, cells.shape[dim], axis=dim)
        cells = jnp.concatenate(
            [
                lax.ppermute(tail, axis, [(i, (i + 1) % count) for i in range(ends)]),
                cells,
                lax.ppermute(head, axis, [((i + 1) % count, i) for i in range(ends)]),
            ],
            axis=dim,
        )
    return cells


def table_pair(row_ids, col_ids, length):
    product = row_ids[:, None] * col_ids[None, :] % length
    angle = product.astype(jnp.float32) * (2.0 * math.pi / length)
    return (jnp.cos(angle).astype(jnp.bfloat16), jnp.sin(angle).astype(jnp.bfloat16))


def general_path(polar, band_offset, tap_count, tap_weight):
    shape_all = polar.shape
    col_count = shape_all[2]
    freq_count = shape_all[3]
    az_count = lax.axis_size("az")
    fq_count = lax.axis_size("fq")
    el_count = lax.axis_size("el")
    padded = with_halo(polar, (("az", 2),), HW)
    window = col_count + 2 * HW
    column = jnp.arange(col_count, dtype=jnp.int32)[:, None]
    position = jnp.arange(window, dtype=jnp.int32)[None, :, None]
    band_matrix = jnp.zeros((col_count, window, freq_count), jnp.bfloat16)
    for tap_index in range(KT):
        reach = column + HW + band_offset + tap_index
        matches = (position == reach[:, None, :]) & (tap_index < tap_count)[:, None, :]
        band_matrix = jnp.where(matches, tap_weight[tap_index][:, None, :], band_matrix)
    interpolated = jnp.einsum(
        "jaf,ceaf->cejf", band_matrix, padded, preferred_element_type=jnp.float32
    ).astype(jnp.bfloat16)
    fq_index = lax.axis_index("fq")
    bin_count = F // (fq_count * az_count)
    az_block = jnp.arange(az_count, dtype=jnp.int32)[:, None]
    bin_local = jnp.arange(bin_count, dtype=jnp.int32)[None, :]
    range_bins = ((az_block * fq_count + fq_index) * bin_count + bin_local).reshape(-1)
    cos_f, sin_f = table_pair(jnp.arange(F, dtype=jnp.int32), range_bins, F)
    shard_piece = lax.all_gather(interpolated, "fq", axis=3, tiled=True)
    cos_rows = cos_f
    sin_rows = sin_f
    real_part = jnp.einsum(
        "ejf,fk->ekj", shard_piece[0], cos_rows, preferred_element_type=jnp.float32
    ) - jnp.einsum("ejf,fk->ekj", shard_piece[1], sin_rows, preferred_element_type=jnp.float32)
    imag_part = jnp.einsum(
        "ejf,fk->ekj", shard_piece[0], sin_rows, preferred_element_type=jnp.float32
    ) + jnp.einsum("ejf,fk->ekj", shard_piece[1], cos_rows, preferred_element_type=jnp.float32)
    summed = jnp.stack([real_part, imag_part])
    ranged = (summed * (1.0 / math.sqrt(F))).astype(jnp.bfloat16)
    azim_ids = jnp.arange(A, dtype=jnp.int32)
    cos_a, sin_a = table_pair(azim_ids, azim_ids, A)
    block_data = lax.all_to_all(ranged, "az", split_axis=2, concat_axis=3, tiled=True)
    real_part = jnp.einsum(
        "ekj,jm->ekm", block_data[0], cos_a, preferred_element_type=jnp.float32
    ) - jnp.einsum("ekj,jm->ekm", block_data[1], sin_a, preferred_element_type=jnp.float32)
    imag_part = jnp.einsum(
        "ekj,jm->ekm", block_data[0], sin_a, preferred_element_type=jnp.float32
    ) + jnp.einsum("ekj,jm->ekm", block_data[1], cos_a, preferred_element_type=jnp.float32)
    crossed = (jnp.stack([real_part, imag_part]) * (1.0 / math.sqrt(A))).astype(jnp.bfloat16)
    elev_ids = jnp.arange(E, dtype=jnp.int32)
    el_index = lax.axis_index("el")
    height_count = E // el_count
    height_rows = el_index * height_count + jnp.arange(height_count, dtype=jnp.int32)
    cos_e, sin_e = table_pair(elev_ids, height_rows, E)
    shard_piece = lax.all_gather(crossed, "el", axis=1, tiled=True)
    cos_rows = cos_e
    sin_rows = sin_e
    real_part = jnp.einsum(
        "eh,ekm->hkm", cos_rows, shard_piece[0], preferred_element_type=jnp.float32
    ) - jnp.einsum("eh,ekm->hkm", sin_rows, shard_piece[1], preferred_element_type=jnp.float32)
    imag_part = jnp.einsum(
        "eh,ekm->hkm", sin_rows, shard_piece[0], preferred_element_type=jnp.float32
    ) + jnp.einsum("eh,ekm->hkm", cos_rows, shard_piece[1], preferred_element_type=jnp.float32)
    totals = jnp.stack([real_part, imag_part])
    image_out = (totals * (1.0 / math.sqrt(E))).astype(jnp.bfloat16)
    return image_out


CHUNKS = ((0, 6), (6, 6), (12, 4))
PARTS = (8, 8)
SPLIT = 48
VMEM = 20 * 1024 * 1024
WIDE_VMEM = 60 * 1024 * 1024


def host_table(row_ids, col_ids, length):
    product = (row_ids[:, None] * col_ids[None, :]) % length
    angle = product.astype(np.float32) * np.float32(2.0 * math.pi / length)
    return (np.cos(angle).astype(ml_dtypes.bfloat16), np.sin(angle).astype(ml_dtypes.bfloat16))


def params(limit=VMEM):
    return pltpu.CompilerParams(vmem_limit_bytes=limit)


def cost(flops, nbytes):
    return pl.CostEstimate(flops=int(flops) // 1000, bytes_accessed=int(nbytes) // 1000, transcendentals=0)


def after(values):
    return [pl.BlockSpec(memory_space=pl.ANY)] * len(values)


def interp_rows(pad_ref, offset_ref, count_ref, weight_ref, out_ref, lane=slice(None)):
    _, cuts, cols, _ = out_ref.shape
    lanes = pad_ref.shape[2]
    step = 8

    def tile(index, carry):
        row = pl.multiple_of(index * ROWS, ROWS)
        rows = pl.ds(row, ROWS)
        base = offset_ref[rows, lane] + HW
        count = count_ref[rows, lane]
        zero = jnp.zeros((ROWS, lanes), jnp.float32)
        taps = [
            jnp.where(count > tap, weight_ref[tap, rows, lane].astype(jnp.float32), zero)
            for tap in range(KT)
        ]
        shift = 1
        while shift < KT:
            chosen = (base & shift) != 0
            taps = [jnp.where(chosen, taps[(r - shift) % KT], taps[r]) for r in range(KT)]
            shift *= 2
        halves = [slice(i, i + step) for i in range(0, ROWS, step)]
        past = [[base[half] > r for r in range(KT + 1)] for half in halves]
        taps = [[tap[half] for tap in taps] for half in halves]
        for part in range(2):
            for cut in range(cuts):
                plane = part * cuts + cut
                near = [
                    pad_ref[plane, pl.ds(row + d, step), :] for d in range(2 * HW + 1 + ROWS - step)
                ]
                totals = []
                for i in range(len(halves)):
                    here = near[i * step :]
                    total = None
                    for r in range(KT):
                        value = jnp.where(past[i][r], here[r + KT], here[r])
                        if r == 0:
                            value = jnp.where(past[i][KT], here[2 * KT], value)
                        value = value * taps[i][r]
                        total = value if total is None else total + value
                    totals.append(total)
                out_ref[part, cut, rows, lane] = jnp.concatenate(totals, axis=0).astype(jnp.bfloat16)
        return carry

    lax.fori_loop(0, cols // ROWS, tile, 0)


def interp_kernel(polar_ref, offset_ref, count_ref, weight_ref, *refs, bordered):
    out_ref, pad_ref = refs[-2:]
    _, cuts, cols, lanes = polar_ref.shape
    for part in range(2):
        for cut in range(cuts):
            plane = part * cuts + cut
            if bordered:
                halo = refs[0][part, cut].astype(jnp.float32)
            else:
                halo = jnp.zeros((2 * HW, lanes), jnp.float32)
            pad_ref[plane, pl.ds(0, HW), :] = halo[:HW]
            pad_ref[plane, pl.ds(HW, cols), :] = polar_ref[part, cut].astype(jnp.float32)
            pad_ref[plane, pl.ds(HW + cols, HW), :] = halo[HW:]
    interp_rows(pad_ref, offset_ref, count_ref, weight_ref, out_ref)


def chunk_spec(count, rows, first):
    return pl.BlockSpec((2, count, rows, LANES), lambda i: (0, first // count, 0, i))


def interpolate(polar, halo, bands, first, count, earlier=(), limit=VMEM):
    _, _, cols, freqs = polar.shape
    border = [] if halo is None else [halo]
    return pl.pallas_call(
        lambda *refs: interp_kernel(*refs, bordered=len(border) == 1),
        grid=(freqs // LANES,),
        in_specs=[
            chunk_spec(count, cols, first),
            pl.BlockSpec((cols, LANES), lambda i: (0, i)),
            pl.BlockSpec((cols, LANES), lambda i: (0, i)),
            pl.BlockSpec((KT, cols, LANES), lambda i: (0, 0, i)),
        ]
        + [chunk_spec(count, 2 * HW, first)] * len(border)
        + after(earlier),
        out_specs=chunk_spec(count, cols, 0),
        out_shape=jax.ShapeDtypeStruct((2, count, cols, freqs), jnp.bfloat16),
        scratch_shapes=[pltpu.VMEM((2 * count, cols + 2 * HW, LANES), jnp.float32)],
        compiler_params=params(limit),
        cost_estimate=cost(2 * count * cols * freqs * 34, 8 * count * cols * freqs),
        name="interpolate",
    )(polar, *bands, *border, *earlier)


def edge_kernel(polar_ref, halo_ref, offset_ref, count_ref, weight_ref, made_ref, out_ref, pad_ref):
    del made_ref
    _, cuts, rows, freqs = polar_ref.shape
    for start in range(0, freqs, LANES):
        lane = pl.ds(start, LANES)
        for part in range(2):
            for cut in range(cuts):
                plane = part * cuts + cut
                halo = halo_ref[part, cut, :, lane].astype(jnp.float32)
                body = polar_ref[part, cut, :, lane].astype(jnp.float32)
                left = jnp.concatenate([halo[:HW], body[: rows - HW]], axis=0)
                right = jnp.concatenate([body[HW:], halo[HW:]], axis=0)
                pad_ref[plane] = jnp.where(pl.program_id(0) == 0, left, right)
        interp_rows(pad_ref, offset_ref, count_ref, weight_ref, out_ref, lane)


def interpolate_edges(polar, halo, bands, first, made):
    _, count, cols, freqs = made.shape
    wide = cols // (2 * ROWS) - 1
    last = cols // ROWS - 1
    return pl.pallas_call(
        edge_kernel,
        grid=(2,),
        in_specs=[
            pl.BlockSpec((2, count, 2 * ROWS, freqs), lambda i: (0, first // count, i * wide, 0)),
            pl.BlockSpec((2, count, 2 * HW, freqs), lambda i: (0, first // count, 0, 0)),
            pl.BlockSpec((ROWS, freqs), lambda i: (i * last, 0)),
            pl.BlockSpec((ROWS, freqs), lambda i: (i * last, 0)),
            pl.BlockSpec((KT, ROWS, freqs), lambda i: (0, i * last, 0)),
            pl.BlockSpec(memory_space=pl.ANY),
        ],
        out_specs=pl.BlockSpec((2, count, ROWS, freqs), lambda i: (0, 0, i * last, 0)),
        out_shape=jax.ShapeDtypeStruct(made.shape, jnp.bfloat16),
        scratch_shapes=[pltpu.VMEM((2 * count, 2 * ROWS, LANES), jnp.float32)],
        input_output_aliases={5: 0},
        compiler_params=params(WIDE_VMEM),
        cost_estimate=cost(4 * count * ROWS * freqs * 34, 16 * count * ROWS * freqs),
        name="interpolate_edges",
    )(polar, halo, *bands, made)


def range_kernel(ids_ref, own_ref, other_ref, *refs, blocks, earlier):
    tables = refs[:blocks]
    first_ref, *rest = refs[blocks + earlier :]
    cuts, cols = own_ref.shape[1:3]
    bins = tables[0].shape[2]
    split = first_ref.shape[3]
    scale = 1.0 / math.sqrt(F)
    table = jnp.concatenate([ref[0, 0] for ref in tables], axis=0)
    for cut in range(cuts):
        real = [own_ref[0, cut], other_ref[0, cut]]
        imag = [own_ref[1, cut], other_ref[1, cut]]
        values = jnp.concatenate(
            [
                jnp.concatenate(real + [-v for v in imag], axis=1),
                jnp.concatenate(imag + real, axis=1),
            ],
            axis=0,
        )
        product = lax.dot_general(
            table, values, (((1,), (1,)), ((), ())), preferred_element_type=jnp.float32
        )
        product = (product * scale).astype(jnp.bfloat16)
        for s in range(blocks):
            for part in range(2):
                value = product[s * bins : (s + 1) * bins, part * cols : (part + 1) * cols]
                first_ref[part, cut, s] = value[:split]
                rest[s][part, cut] = value[split:]


def range_transform(ids, own, other, table, split, earlier=(), limit=VMEM):
    _, count, cols, freqs = own.shape
    _, blocks, bins, full = table.shape
    rest = bins - split
    group = 2

    def block_of(s):
        return pl.BlockSpec((1, 1, bins, full), lambda i, ids: (ids[1], ids[0] ^ s, 0, 0))

    return pl.pallas_call(
        lambda *refs: range_kernel(*refs, blocks=blocks, earlier=len(earlier)),
        grid_spec=pltpu.PrefetchScalarGridSpec(
            num_scalar_prefetch=1,
            grid=(count // group,),
            in_specs=[pl.BlockSpec((2, group, cols, freqs), lambda i, ids: (0, i, 0, 0))] * 2
            + [block_of(s) for s in range(blocks)]
            + after(earlier),
            out_specs=[
                pl.BlockSpec((2, group, blocks, split, cols), lambda i, ids: (0, i, 0, 0, 0))
            ]
            + [pl.BlockSpec((2, group, rest, cols), lambda i, ids: (0, i, 0, 0))] * blocks,
        ),
        out_shape=[jax.ShapeDtypeStruct((2, count, blocks, split, cols), jnp.bfloat16)]
        + [jax.ShapeDtypeStruct((2, count, rest, cols), jnp.bfloat16)] * blocks,
        compiler_params=params(limit),
        cost_estimate=cost(4 * count * cols * full * blocks * bins, 12 * count * cols * freqs),
        name="range_transform",
    )(ids, own, other, *([table] * blocks), *earlier)


def height_table(cuts, rows, order):
    heights = []
    for el in range(2):
        pair = []
        for parity in range(2):
            h = el * cuts + parity + 2 * np.arange(cuts // 2)
            cos, sin = (t.astype(np.float32) for t in host_table(h, order, 2 * cuts))
            sign = -1.0 if el and parity else 1.0
            whole = sign * np.block([[cos, -sin], [sin, cos]])
            pair.append(np.kron(whole, np.eye(rows, dtype=np.float32)))
        heights.append(np.stack(pair))
    return np.stack(heights).astype(ml_dtypes.bfloat16)


def height_kernel(ids_ref, matrix_ref, *refs, chunks, sets, outs, scale, skipped):
    ins = refs[: 2 * chunks]
    out_refs = refs[2 * chunks + skipped :]
    rows, lanes = ins[0].shape[-2:]
    half = matrix_ref.shape[2] // (2 * rows)
    for index in range(sets):
        sums, differences = [], []
        for part in range(2):
            for own, other in zip(ins[:chunks], ins[chunks:]):
                pad = (index,) if len(own.shape) == 5 else ()
                for e in range(own.shape[1]):
                    a, b = own[(part, e) + pad], other[(part, e) + pad]
                    sums.append(a + b)
                    differences.append(a - b)
        results = [
            jnp.dot(
                matrix_ref[0, parity],
                jnp.concatenate(values, axis=0),
                preferred_element_type=jnp.float32,
            )
            for parity, values in enumerate((sums, differences))
        ]
        h = 0
        for ref in out_refs[index * outs : (index + 1) * outs]:
            for row in range(ref.shape[1]):
                for part in range(2):
                    start = (part * half + h // 2) * rows
                    value = results[h % 2][start : start + rows]
                    if scale is not None:
                        value = value * scale
                    ref[part, row] = value.astype(jnp.bfloat16)
                h += 1


def first_heights(ids, matrix, own, other, parts, earlier=()):
    chunks = len(own)
    _, _, blocks, split, cols = own[0].shape
    total = sum(v.shape[1] for v in own)
    spec = [
        pl.BlockSpec((2, v.shape[1], blocks, ROWS, cols), lambda i, ids: (0, 0, 0, i, 0))
        for v in own
    ]
    outs = list(parts) * blocks
    made = pl.pallas_call(
        lambda *refs: height_kernel(
            *refs, chunks=chunks, sets=blocks, outs=len(parts), scale=None, skipped=len(earlier)
        ),
        grid_spec=pltpu.PrefetchScalarGridSpec(
            num_scalar_prefetch=1,
            grid=(split // ROWS,),
            in_specs=[pl.BlockSpec((1,) + matrix.shape[1:], lambda i, ids: (ids[2], 0, 0, 0))]
            + spec
            + spec
            + after(earlier),
            out_specs=[pl.BlockSpec((2, h, ROWS, cols), lambda i, ids: (0, 0, i, 0)) for h in outs],
        ),
        out_shape=[jax.ShapeDtypeStruct((2, h, split, cols), jnp.bfloat16) for h in outs],
        compiler_params=params(),
        cost_estimate=cost(blocks * split * cols * 32768, 12 * blocks * total * split * cols),
        name="first_heights",
    )(ids, matrix, *own, *other, *earlier)
    return [[made[s * len(parts) + p] for s in range(blocks)] for p in range(len(parts))]


def last_heights(ids, matrix, own, other, places, image, shape, skip, rows, earlier=()):
    chunks = len(own)
    full = own[0].shape[3]
    width = min(full, 512)
    total = sum(v.shape[1] for v in own)

    def chunk(v, place):
        return pl.BlockSpec(
            (2, v.shape[1], ROWS, width), lambda i, j, ids: (0, 0, place // ROWS + i, j)
        )

    spec = [chunk(v, place) for v, place in zip(own, places)]
    extra = [] if image is None else [image]
    first = skip // ROWS
    return pl.pallas_call(
        lambda *refs: height_kernel(
            *refs,
            chunks=chunks,
            sets=1,
            outs=1,
            scale=1.0 / math.sqrt(2 * total),
            skipped=len(earlier) + len(extra),
        ),
        grid_spec=pltpu.PrefetchScalarGridSpec(
            num_scalar_prefetch=1,
            grid=(rows // ROWS, full // width),
            in_specs=[pl.BlockSpec((1,) + matrix.shape[1:], lambda i, j, ids: (ids[2], 0, 0, 0))]
            + spec
            + spec
            + after(extra)
            + after(earlier),
            out_specs=pl.BlockSpec((2, total, ROWS, width), lambda i, j, ids: (0, 0, first + i, j)),
        ),
        out_shape=jax.ShapeDtypeStruct(shape, jnp.bfloat16),
        input_output_aliases={2 + 2 * chunks: 0} if extra else {},
        compiler_params=params(),
        cost_estimate=cost(rows * full * 32768, 12 * total * rows * full),
        name="last_heights",
    )(ids, matrix, *own, *other, *extra, *earlier)


def cross_kernel(ids_ref, *refs, groups, blocks, scale, skipped, outs):
    ins = [refs[g * blocks : (g + 1) * blocks] for g in range(groups)]
    cos_ref, sin_ref = refs[groups * blocks : groups * blocks + 2]
    out_refs = refs[groups * blocks + 2 + skipped : -1]
    rows_ref = refs[-1]
    bins, cols = ins[0][0].shape[2:]
    cuts = [group[0].shape[1] for group in ins]
    rows = sum(cuts) * bins

    @pl.when(pl.program_id(0) == 0)
    def _():
        for s in range(blocks):
            start = pl.multiple_of((ids_ref[0] ^ s) * cols, cols)
            for part in range(2):
                place = part * rows
                for group, count in zip(ins, cuts):
                    rows_ref[pl.ds(place, count * bins), pl.ds(start, cols)] = group[s][
                        part
                    ].reshape(count * bins, cols)
                    place += count * bins

    values = rows_ref[...]
    with_cos = jnp.dot(values, cos_ref[...], preferred_element_type=jnp.float32)
    with_sin = jnp.dot(values, sin_ref[...], preferred_element_type=jnp.float32)
    real = (with_cos[:rows] - with_sin[rows:]) * scale
    imag = (with_sin[:rows] + with_cos[rows:]) * scale
    for part, value in ((0, real), (1, imag)):
        value = value.astype(jnp.bfloat16).reshape(sum(cuts), bins, value.shape[1])
        place = 0
        for ref in out_refs:
            size = ref.shape[2]
            ref[part] = value[:, place : place + size]
            place += size


def cross_transform(ids, ins, tables, scale, sizes=None, image=None, shape=None, place=0, earlier=()):
    groups, blocks = len(ins), len(ins[0])
    bins, cols = ins[0][0].shape[2:]
    total = sum(group[0].shape[1] for group in ins)
    full = tables[0].shape[1]
    width = min(full, 512)
    extra = [] if image is None else [image]
    if shape is None:
        shapes = [(2, total, size, full) for size in sizes]
    else:
        sizes, shapes = [bins], [shape]
    result = pl.pallas_call(
        lambda *refs: cross_kernel(
            *refs,
            groups=groups,
            blocks=blocks,
            scale=scale,
            skipped=len(extra) + len(earlier),
            outs=len(sizes),
        ),
        grid_spec=pltpu.PrefetchScalarGridSpec(
            num_scalar_prefetch=1,
            grid=(full // width,),
            in_specs=[
                pl.BlockSpec((2, v.shape[1], bins, cols), lambda i, ids: (0, 0, 0, 0))
                for group in ins
                for v in group
            ]
            + [pl.BlockSpec((full, width), lambda i, ids: (0, i))] * 2
            + after(extra)
            + after(earlier),
            out_specs=[
                pl.BlockSpec((2, total, size, width), lambda i, ids: (0, place, 0, i))
                for size in sizes
            ],
            scratch_shapes=[pltpu.VMEM((2 * total * bins, full), jnp.bfloat16)],
        ),
        out_shape=[jax.ShapeDtypeStruct(v, jnp.bfloat16) for v in shapes],
        input_output_aliases={1 + groups * blocks + 2: 0} if extra else {},
        compiler_params=params(),
        cost_estimate=cost(8 * total * bins * full * full, 8 * total * bins * full + 4 * full * full),
        name="cross_transform",
    )(ids, *[v for group in ins for v in group], *tables, *extra, *earlier)
    return result if image is None and len(sizes) > 1 else result[0]


def exchange(value, axis, s):
    return lax.ppermute(value, axis, [(i, i ^ s) for i in range(lax.axis_size(axis))])


def halo_rows(polar):
    count = lax.axis_size("az")
    cols = polar.shape[2]
    ends = count - 1
    head = lax.slice_in_dim(polar, 0, HW, axis=2)
    tail = lax.slice_in_dim(polar, cols - HW, cols, axis=2)
    return jnp.concatenate(
        [
            lax.ppermute(tail, "az", [(i, i + 1) for i in range(ends)]),
            lax.ppermute(head, "az", [(i + 1, i) for i in range(ends)]),
        ],
        axis=2,
    )


def planned_path(polar, band_offset, tap_count, tap_weight):
    _, cuts, cols, freqs = polar.shape
    az_count = lax.axis_size("az")
    fq_count = lax.axis_size("fq")
    bins = F // (az_count * fq_count)
    split = SPLIT
    rest = bins - split
    ids = jnp.stack([lax.axis_index("az"), lax.axis_index("fq"), lax.axis_index("el")])
    tables = []
    for core in range(fq_count):
        order = np.concatenate([np.arange(freqs) + freqs * (core ^ s) for s in range(fq_count)])
        blocks = []
        for az in range(az_count):
            ks = (az * fq_count + core) * bins + np.arange(bins)
            blocks.append(np.concatenate(host_table(ks, order, F), axis=1))
        tables.append(np.stack(blocks))
    range_table = jnp.asarray(np.stack(tables))
    cross_tables = [jnp.asarray(t) for t in host_table(np.arange(A), np.arange(A), A)]
    order = np.concatenate([start + np.arange(count) for start, count in CHUNKS])
    matrix = jnp.asarray(height_table(cuts, ROWS, order))

    bands = (band_offset, tap_count, tap_weight)
    halo = halo_rows(polar)
    last = len(CHUNKS) - 1
    scale = 1.0 / math.sqrt(A)

    def interp(i, earlier=(), limit=VMEM):
        return interpolate(polar, halo, bands, *CHUNKS[i], earlier, limit)

    def to_owners(blocks, which=range(az_count - 1, 0, -1)):
        return {s: exchange(blocks[s], "az", s) for s in which}

    def in_order(blocks, come):
        return [blocks[0]] + [come[s] for s in range(1, az_count)]

    bare = interpolate(polar, None, bands, *CHUNKS[0], (), WIDE_VMEM)
    made = interpolate_edges(polar, halo, bands, CHUNKS[0][0], bare)
    other = exchange(made, "fq", 1)
    ahead = interp(1, (made,), WIDE_VMEM)
    own_first, other_first, landed = [], [], []
    moving = None
    for i in range(last + 1):
        limit = VMEM if i else WIDE_VMEM
        first, *blocks = range_transform(ids, made, other, range_table, split, (ahead,), limit)
        if 0 < i < last:
            ahead = interp(i + 1, (first,))
        first, blocks, ahead, moving = lax.optimization_barrier((first, blocks, ahead, moving))
        if i > 0:
            landed.append(in_order(held, moving[0]))
            other_first.append(moving[1])
        own_first.append(first)
        held = blocks
        moving = (to_owners(blocks), exchange(first, "el", 1))
        if i < last:
            made, other = ahead, exchange(ahead, "fq", 1)
    c0 = cross_transform(ids, landed, cross_tables, scale, [rest], earlier=(first,))
    c0, moving = lax.optimization_barrier((c0, moving))
    landed.append(in_order(held, moving[0]))
    other_first.append(moving[1])
    other_c0 = exchange(c0, "el", 1)

    made = first_heights(ids, matrix, own_first, other_first, PARTS, (c0,))
    come = to_owners(made[0])
    c1 = cross_transform(ids, landed[-1:], cross_tables, scale, [rest], earlier=(made[0][0],))
    other_c1 = exchange(c1, "el", 1)
    shape = (2, cuts, bins, A)
    full_scale = 1.0 / math.sqrt(A * 2 * cuts)
    made, come, c1 = lax.optimization_barrier((made, come, c1))
    arrived = in_order(made[0], come)
    come = to_owners(made[1])
    image = cross_transform(
        ids, [arrived], cross_tables, full_scale, image=None, shape=shape, place=0, earlier=(c1,)
    )
    image = last_heights(
        ids, matrix, [c0, c1], [other_c0, other_c1], (0, 0), image, shape, split, rest
    )
    image = cross_transform(
        ids,
        [in_order(made[1], come)],
        cross_tables,
        full_scale,
        image=image,
        shape=shape,
        place=PARTS[0] // PARTS[1],
    )
    return image


def on_device(polar, band_offset, tap_count, tap_weight):
    _, cuts, cols, freqs = polar.shape
    az_count = lax.axis_size("az")
    bins = F // (az_count * lax.axis_size("fq"))
    fits = (
        lax.axis_size("el") == 2
        and lax.axis_size("fq") == 2
        and az_count == 4
        and cuts == sum(count for _, count in CHUNKS) == sum(PARTS)
        and cols % (2 * LANES) == 0
        and freqs % LANES == 0
        and bins > SPLIT
        and bins == 2 * SPLIT
        and A % 512 == 0
        and 2 * HW == ROWS
    )
    chosen = planned_path if fits else general_path
    return chosen(polar, band_offset, tap_count, tap_weight)


def solution(mesh):
    in_specs = (
        P(None, ("grp", "el"), "az", "fq"),
        P("az", "fq"),
        P("az", "fq"),
        P(None, "az", "fq"),
    )
    out_specs = P(None, ("grp", "el"), ("az", "fq"), None)
    return jax.shard_map(
        on_device, mesh=mesh, in_specs=in_specs, out_specs=out_specs, check_vma=False
    )
```

```python
import math

import jax
import jax.numpy as jnp
import ml_dtypes
import numpy as np
from jax import lax
from jax.experimental import pallas as pl
from jax.experimental.pallas import tpu as pltpu
from jax.sharding import PartitionSpec as P

F = 768
A = 1024
E = 32
HW = 8
KT = 8

LANES = 128
ROWS = 16


def with_halo(cells, sides, width):
    for axis, dim in sides:
        count = lax.axis_size(axis)
        ends = count - 1
        head = lax.slice_in_dim(cells, 0, width, axis=dim)
        tail = lax.slice_in_dim(cells, cells.shape[dim] - width, cells.shape[dim], axis=dim)
        cells = jnp.concatenate(
            [
                lax.ppermute(tail, axis, [(i, (i + 1) % count) for i in range(ends)]),
                cells,
                lax.ppermute(head, axis, [((i + 1) % count, i) for i in range(ends)]),
            ],
            axis=dim,
        )
    return cells


def table_pair(row_ids, col_ids, length):
    product = row_ids[:, None] * col_ids[None, :] % length
    angle = product.astype(jnp.float32) * (2.0 * math.pi / length)
    return (jnp.cos(angle).astype(jnp.bfloat16), jnp.sin(angle).astype(jnp.bfloat16))


def general_path(polar, band_offset, tap_count, tap_weight):
    shape_all = polar.shape
    col_count = shape_all[2]
    freq_count = shape_all[3]
    az_count = lax.axis_size("az")
    fq_count = lax.axis_size("fq")
    el_count = lax.axis_size("el")
    padded = with_halo(polar, (("az", 2),), HW)
    window = col_count + 2 * HW
    column = jnp.arange(col_count, dtype=jnp.int32)[:, None]
    position = jnp.arange(window, dtype=jnp.int32)[None, :, None]
    band_matrix = jnp.zeros((col_count, window, freq_count), jnp.bfloat16)
    for tap_index in range(KT):
        reach = column + HW + band_offset + tap_index
        matches = (position == reach[:, None, :]) & (tap_index < tap_count)[:, None, :]
        band_matrix = jnp.where(matches, tap_weight[tap_index][:, None, :], band_matrix)
    interpolated = jnp.einsum(
        "jaf,ceaf->cejf", band_matrix, padded, preferred_element_type=jnp.float32
    ).astype(jnp.bfloat16)
    fq_index = lax.axis_index("fq")
    bin_count = F // (fq_count * az_count)
    az_block = jnp.arange(az_count, dtype=jnp.int32)[:, None]
    bin_local = jnp.arange(bin_count, dtype=jnp.int32)[None, :]
    range_bins = ((az_block * fq_count + fq_index) * bin_count + bin_local).reshape(-1)
    cos_f, sin_f = table_pair(jnp.arange(F, dtype=jnp.int32), range_bins, F)
    shard_piece = lax.all_gather(interpolated, "fq", axis=3, tiled=True)
    cos_rows = cos_f
    sin_rows = sin_f
    real_part = jnp.einsum(
        "ejf,fk->ekj", shard_piece[0], cos_rows, preferred_element_type=jnp.float32
    ) - jnp.einsum("ejf,fk->ekj", shard_piece[1], sin_rows, preferred_element_type=jnp.float32)
    imag_part = jnp.einsum(
        "ejf,fk->ekj", shard_piece[0], sin_rows, preferred_element_type=jnp.float32
    ) + jnp.einsum("ejf,fk->ekj", shard_piece[1], cos_rows, preferred_element_type=jnp.float32)
    summed = jnp.stack([real_part, imag_part])
    ranged = (summed * (1.0 / math.sqrt(F))).astype(jnp.bfloat16)
    azim_ids = jnp.arange(A, dtype=jnp.int32)
    cos_a, sin_a = table_pair(azim_ids, azim_ids, A)
    block_data = lax.all_to_all(ranged, "az", split_axis=2, concat_axis=3, tiled=True)
    real_part = jnp.einsum(
        "ekj,jm->ekm", block_data[0], cos_a, preferred_element_type=jnp.float32
    ) - jnp.einsum("ekj,jm->ekm", block_data[1], sin_a, preferred_element_type=jnp.float32)
    imag_part = jnp.einsum(
        "ekj,jm->ekm", block_data[0], sin_a, preferred_element_type=jnp.float32
    ) + jnp.einsum("ekj,jm->ekm", block_data[1], cos_a, preferred_element_type=jnp.float32)
    crossed = (jnp.stack([real_part, imag_part]) * (1.0 / math.sqrt(A))).astype(jnp.bfloat16)
    elev_ids = jnp.arange(E, dtype=jnp.int32)
    el_index = lax.axis_index("el")
    height_count = E // el_count
    height_rows = el_index * height_count + jnp.arange(height_count, dtype=jnp.int32)
    cos_e, sin_e = table_pair(elev_ids, height_rows, E)
    shard_piece = lax.all_gather(crossed, "el", axis=1, tiled=True)
    cos_rows = cos_e
    sin_rows = sin_e
    real_part = jnp.einsum(
        "eh,ekm->hkm", cos_rows, shard_piece[0], preferred_element_type=jnp.float32
    ) - jnp.einsum("eh,ekm->hkm", sin_rows, shard_piece[1], preferred_element_type=jnp.float32)
    imag_part = jnp.einsum(
        "eh,ekm->hkm", sin_rows, shard_piece[0], preferred_element_type=jnp.float32
    ) + jnp.einsum("eh,ekm->hkm", cos_rows, shard_piece[1], preferred_element_type=jnp.float32)
    totals = jnp.stack([real_part, imag_part])
    image_out = (totals * (1.0 / math.sqrt(E))).astype(jnp.bfloat16)
    return image_out


CHUNKS = ((0, 6), (6, 6), (12, 4))
PARTS = (8, 8)
SPLIT = 48
VMEM = 20 * 1024 * 1024
WIDE_VMEM = 60 * 1024 * 1024


def host_table(row_ids, col_ids, length):
    product = (row_ids[:, None] * col_ids[None, :]) % length
    angle = product.astype(np.float32) * np.float32(2.0 * math.pi / length)
    return (np.cos(angle).astype(ml_dtypes.bfloat16), np.sin(angle).astype(ml_dtypes.bfloat16))


def params(limit=VMEM):
    return pltpu.CompilerParams(vmem_limit_bytes=limit)


def cost(flops, nbytes):
    return pl.CostEstimate(flops=int(flops) // 1000, bytes_accessed=int(nbytes) // 1000, transcendentals=0)


def after(values):
    return [pl.BlockSpec(memory_space=pl.ANY)] * len(values)


def interp_rows(pad_ref, offset_ref, count_ref, weight_ref, out_ref, lane=slice(None)):
    _, cuts, cols, _ = out_ref.shape
    lanes = pad_ref.shape[2]
    step = 8

    def tile(index, carry):
        row = pl.multiple_of(index * ROWS, ROWS)
        rows = pl.ds(row, ROWS)
        base = offset_ref[rows, lane] + HW
        count = count_ref[rows, lane]
        zero = jnp.zeros((ROWS, lanes), jnp.float32)
        taps = [
            jnp.where(count > tap, weight_ref[tap, rows, lane].astype(jnp.float32), zero)
            for tap in range(KT)
        ]
        shift = 1
        while shift < KT:
            chosen = (base & shift) != 0
            taps = [jnp.where(chosen, taps[(r - shift) % KT], taps[r]) for r in range(KT)]
            shift *= 2
        halves = [slice(i, i + step) for i in range(0, ROWS, step)]
        past = [[base[half] > r for r in range(KT + 1)] for half in halves]
        taps = [[tap[half] for tap in taps] for half in halves]
        for part in range(2):
            for cut in range(cuts):
                plane = part * cuts + cut
                near = [
                    pad_ref[plane, pl.ds(row + d, step), :] for d in range(2 * HW + 1 + ROWS - step)
                ]
                totals = []
                for i in range(len(halves)):
                    here = near[i * step :]
                    total = None
                    for r in range(KT):
                        value = jnp.where(past[i][r], here[r + KT], here[r])
                        if r == 0:
                            value = jnp.where(past[i][KT], here[2 * KT], value)
                        value = value * taps[i][r]
                        total = value if total is None else total + value
                    totals.append(total)
                out_ref[part, cut, rows, lane] = jnp.concatenate(totals, axis=0).astype(jnp.bfloat16)
        return carry

    lax.fori_loop(0, cols // ROWS, tile, 0)


def interp_kernel(polar_ref, offset_ref, count_ref, weight_ref, *refs, bordered):
    out_ref, pad_ref = refs[-2:]
    _, cuts, cols, lanes = polar_ref.shape
    for part in range(2):
        for cut in range(cuts):
            plane = part * cuts + cut
            if bordered:
                halo = refs[0][part, cut].astype(jnp.float32)
            else:
                halo = jnp.zeros((2 * HW, lanes), jnp.float32)
            pad_ref[plane, pl.ds(0, HW), :] = halo[:HW]
            pad_ref[plane, pl.ds(HW, cols), :] = polar_ref[part, cut].astype(jnp.float32)
            pad_ref[plane, pl.ds(HW + cols, HW), :] = halo[HW:]
    interp_rows(pad_ref, offset_ref, count_ref, weight_ref, out_ref)


def chunk_spec(count, rows, first):
    return pl.BlockSpec((2, count, rows, LANES), lambda i: (0, first // count, 0, i))


def interpolate(polar, halo, bands, first, count, earlier=(), limit=VMEM):
    _, _, cols, freqs = polar.shape
    border = [] if halo is None else [halo]
    return pl.pallas_call(
        lambda *refs: interp_kernel(*refs, bordered=len(border) == 1),
        grid=(freqs // LANES,),
        in_specs=[
            chunk_spec(count, cols, first),
            pl.BlockSpec((cols, LANES), lambda i: (0, i)),
            pl.BlockSpec((cols, LANES), lambda i: (0, i)),
            pl.BlockSpec((KT, cols, LANES), lambda i: (0, 0, i)),
        ]
        + [chunk_spec(count, 2 * HW, first)] * len(border)
        + after(earlier),
        out_specs=chunk_spec(count, cols, 0),
        out_shape=jax.ShapeDtypeStruct((2, count, cols, freqs), jnp.bfloat16),
        scratch_shapes=[pltpu.VMEM((2 * count, cols + 2 * HW, LANES), jnp.float32)],
        compiler_params=params(limit),
        cost_estimate=cost(2 * count * cols * freqs * 34, 8 * count * cols * freqs),
        name="interpolate",
    )(polar, *bands, *border, *earlier)


def edge_kernel(polar_ref, halo_ref, offset_ref, count_ref, weight_ref, made_ref, out_ref, pad_ref):
    del made_ref
    _, cuts, rows, freqs = polar_ref.shape
    for start in range(0, freqs, LANES):
        lane = pl.ds(start, LANES)
        for part in range(2):
            for cut in range(cuts):
                plane = part * cuts + cut
                halo = halo_ref[part, cut, :, lane].astype(jnp.float32)
                body = polar_ref[part, cut, :, lane].astype(jnp.float32)
                left = jnp.concatenate([halo[:HW], body[: rows - HW]], axis=0)
                right = jnp.concatenate([body[HW:], halo[HW:]], axis=0)
                pad_ref[plane] = jnp.where(pl.program_id(0) == 0, left, right)
        interp_rows(pad_ref, offset_ref, count_ref, weight_ref, out_ref, lane)


def interpolate_edges(polar, halo, bands, first, made):
    _, count, cols, freqs = made.shape
    wide = cols // (2 * ROWS) - 1
    last = cols // ROWS - 1
    return pl.pallas_call(
        edge_kernel,
        grid=(2,),
        in_specs=[
            pl.BlockSpec((2, count, 2 * ROWS, freqs), lambda i: (0, first // count, i * wide, 0)),
            pl.BlockSpec((2, count, 2 * HW, freqs), lambda i: (0, first // count, 0, 0)),
            pl.BlockSpec((ROWS, freqs), lambda i: (i * last, 0)),
            pl.BlockSpec((ROWS, freqs), lambda i: (i * last, 0)),
            pl.BlockSpec((KT, ROWS, freqs), lambda i: (0, i * last, 0)),
            pl.BlockSpec(memory_space=pl.ANY),
        ],
        out_specs=pl.BlockSpec((2, count, ROWS, freqs), lambda i: (0, 0, i * last, 0)),
        out_shape=jax.ShapeDtypeStruct(made.shape, jnp.bfloat16),
        scratch_shapes=[pltpu.VMEM((2 * count, 2 * ROWS, LANES), jnp.float32)],
        input_output_aliases={5: 0},
        compiler_params=params(WIDE_VMEM),
        cost_estimate=cost(4 * count * ROWS * freqs * 34, 16 * count * ROWS * freqs),
        name="interpolate_edges",
    )(polar, halo, *bands, made)


def range_kernel(ids_ref, own_ref, other_ref, *refs, blocks, earlier):
    tables = refs[:blocks]
    first_ref, *rest = refs[blocks + earlier :]
    cuts, cols = own_ref.shape[1:3]
    bins = tables[0].shape[2]
    split = first_ref.shape[3]
    scale = 1.0 / math.sqrt(F)
    table = jnp.concatenate([ref[0, 0] for ref in tables], axis=0)
    for cut in range(cuts):
        real = [own_ref[0, cut], other_ref[0, cut]]
        imag = [own_ref[1, cut], other_ref[1, cut]]
        values = jnp.concatenate(
            [
                jnp.concatenate(real + [-v for v in imag], axis=1),
                jnp.concatenate(imag + real, axis=1),
            ],
            axis=0,
        )
        product = lax.dot_general(
            table, values, (((1,), (1,)), ((), ())), preferred_element_type=jnp.float32
        )
        product = (product * scale).astype(jnp.bfloat16)
        for s in range(blocks):
            for part in range(2):
                value = product[s * bins : (s + 1) * bins, part * cols : (part + 1) * cols]
                first_ref[part, cut, s] = value[:split]
                rest[s][part, cut] = value[split:]


def range_transform(ids, own, other, table, split, earlier=(), limit=VMEM):
    _, count, cols, freqs = own.shape
    _, blocks, bins, full = table.shape
    rest = bins - split
    group = 2

    def block_of(s):
        return pl.BlockSpec((1, 1, bins, full), lambda i, ids: (ids[1], ids[0] ^ s, 0, 0))

    return pl.pallas_call(
        lambda *refs: range_kernel(*refs, blocks=blocks, earlier=len(earlier)),
        grid_spec=pltpu.PrefetchScalarGridSpec(
            num_scalar_prefetch=1,
            grid=(count // group,),
            in_specs=[pl.BlockSpec((2, group, cols, freqs), lambda i, ids: (0, i, 0, 0))] * 2
            + [block_of(s) for s in range(blocks)]
            + after(earlier),
            out_specs=[
                pl.BlockSpec((2, group, blocks, split, cols), lambda i, ids: (0, i, 0, 0, 0))
            ]
            + [pl.BlockSpec((2, group, rest, cols), lambda i, ids: (0, i, 0, 0))] * blocks,
        ),
        out_shape=[jax.ShapeDtypeStruct((2, count, blocks, split, cols), jnp.bfloat16)]
        + [jax.ShapeDtypeStruct((2, count, rest, cols), jnp.bfloat16)] * blocks,
        compiler_params=params(limit),
        cost_estimate=cost(4 * count * cols * full * blocks * bins, 12 * count * cols * freqs),
        name="range_transform",
    )(ids, own, other, *([table] * blocks), *earlier)


def height_table(cuts, rows, order):
    heights = []
    for el in range(2):
        pair = []
        for parity in range(2):
            h = el * cuts + parity + 2 * np.arange(cuts // 2)
            cos, sin = (t.astype(np.float32) for t in host_table(h, order, 2 * cuts))
            sign = -1.0 if el and parity else 1.0
            whole = sign * np.block([[cos, -sin], [sin, cos]])
            pair.append(np.kron(whole, np.eye(rows, dtype=np.float32)))
        heights.append(np.stack(pair))
    return np.stack(heights).astype(ml_dtypes.bfloat16)


def height_kernel(ids_ref, matrix_ref, *refs, chunks, sets, outs, scale, skipped):
    ins = refs[: 2 * chunks]
    out_refs = refs[2 * chunks + skipped :]
    rows, lanes = ins[0].shape[-2:]
    half = matrix_ref.shape[2] // (2 * rows)
    for index in range(sets):
        sums, differences = [], []
        for part in range(2):
            for own, other in zip(ins[:chunks], ins[chunks:]):
                pad = (index,) if len(own.shape) == 5 else ()
                for e in range(own.shape[1]):
                    a, b = own[(part, e) + pad], other[(part, e) + pad]
                    sums.append(a + b)
                    differences.append(a - b)
        results = [
            jnp.dot(
                matrix_ref[0, parity],
                jnp.concatenate(values, axis=0),
                preferred_element_type=jnp.float32,
            )
            for parity, values in enumerate((sums, differences))
        ]
        h = 0
        for ref in out_refs[index * outs : (index + 1) * outs]:
            for row in range(ref.shape[1]):
                for part in range(2):
                    start = (part * half + h // 2) * rows
                    value = results[h % 2][start : start + rows]
                    if scale is not None:
                        value = value * scale
                    ref[part, row] = value.astype(jnp.bfloat16)
                h += 1


def first_heights(ids, matrix, own, other, parts, earlier=()):
    chunks = len(own)
    _, _, blocks, split, cols = own[0].shape
    total = sum(v.shape[1] for v in own)
    spec = [
        pl.BlockSpec((2, v.shape[1], blocks, ROWS, cols), lambda i, ids: (0, 0, 0, i, 0))
        for v in own
    ]
    outs = list(parts) * blocks
    made = pl.pallas_call(
        lambda *refs: height_kernel(
            *refs, chunks=chunks, sets=blocks, outs=len(parts), scale=None, skipped=len(earlier)
        ),
        grid_spec=pltpu.PrefetchScalarGridSpec(
            num_scalar_prefetch=1,
            grid=(split // ROWS,),
            in_specs=[pl.BlockSpec((1,) + matrix.shape[1:], lambda i, ids: (ids[2], 0, 0, 0))]
            + spec
            + spec
            + after(earlier),
            out_specs=[pl.BlockSpec((2, h, ROWS, cols), lambda i, ids: (0, 0, i, 0)) for h in outs],
        ),
        out_shape=[jax.ShapeDtypeStruct((2, h, split, cols), jnp.bfloat16) for h in outs],
        compiler_params=params(),
        cost_estimate=cost(blocks * split * cols * 32768, 12 * blocks * total * split * cols),
        name="first_heights",
    )(ids, matrix, *own, *other, *earlier)
    return [[made[s * len(parts) + p] for s in range(blocks)] for p in range(len(parts))]


def last_heights(ids, matrix, own, other, places, image, shape, skip, rows, earlier=()):
    chunks = len(own)
    full = own[0].shape[3]
    width = min(full, 512)
    total = sum(v.shape[1] for v in own)

    def chunk(v, place):
        return pl.BlockSpec(
            (2, v.shape[1], ROWS, width), lambda i, j, ids: (0, 0, place // ROWS + i, j)
        )

    spec = [chunk(v, place) for v, place in zip(own, places)]
    extra = [] if image is None else [image]
    first = skip // ROWS
    return pl.pallas_call(
        lambda *refs: height_kernel(
            *refs,
            chunks=chunks,
            sets=1,
            outs=1,
            scale=1.0 / math.sqrt(2 * total),
            skipped=len(earlier) + len(extra),
        ),
        grid_spec=pltpu.PrefetchScalarGridSpec(
            num_scalar_prefetch=1,
            grid=(rows // ROWS, full // width),
            in_specs=[pl.BlockSpec((1,) + matrix.shape[1:], lambda i, j, ids: (ids[2], 0, 0, 0))]
            + spec
            + spec
            + after(extra)
            + after(earlier),
            out_specs=pl.BlockSpec((2, total, ROWS, width), lambda i, j, ids: (0, 0, first + i, j)),
        ),
        out_shape=jax.ShapeDtypeStruct(shape, jnp.bfloat16),
        input_output_aliases={2 + 2 * chunks: 0} if extra else {},
        compiler_params=params(),
        cost_estimate=cost(rows * full * 32768, 12 * total * rows * full),
        name="last_heights",
    )(ids, matrix, *own, *other, *extra, *earlier)


def cross_kernel(ids_ref, *refs, groups, blocks, scale, skipped, outs):
    ins = [refs[g * blocks : (g + 1) * blocks] for g in range(groups)]
    cos_ref, sin_ref = refs[groups * blocks : groups * blocks + 2]
    out_refs = refs[groups * blocks + 2 + skipped : -1]
    rows_ref = refs[-1]
    bins, cols = ins[0][0].shape[2:]
    cuts = [group[0].shape[1] for group in ins]
    rows = sum(cuts) * bins

    @pl.when(pl.program_id(0) == 0)
    def _():
        for s in range(blocks):
            start = pl.multiple_of((ids_ref[0] ^ s) * cols, cols)
            for part in range(2):
                place = part * rows
                for group, count in zip(ins, cuts):
                    rows_ref[pl.ds(place, count * bins), pl.ds(start, cols)] = group[s][
                        part
                    ].reshape(count * bins, cols)
                    place += count * bins

    values = rows_ref[...]
    with_cos = jnp.dot(values, cos_ref[...], preferred_element_type=jnp.float32)
    with_sin = jnp.dot(values, sin_ref[...], preferred_element_type=jnp.float32)
    real = (with_cos[:rows] - with_sin[rows:]) * scale
    imag = (with_sin[:rows] + with_cos[rows:]) * scale
    for part, value in ((0, real), (1, imag)):
        value = value.astype(jnp.bfloat16).reshape(sum(cuts), bins, value.shape[1])
        place = 0
        for ref in out_refs:
            size = ref.shape[2]
            ref[part] = value[:, place : place + size]
            place += size


def cross_transform(ids, ins, tables, scale, sizes=None, image=None, shape=None, place=0, earlier=()):
    groups, blocks = len(ins), len(ins[0])
    bins, cols = ins[0][0].shape[2:]
    total = sum(group[0].shape[1] for group in ins)
    full = tables[0].shape[1]
    width = min(full, 512)
    extra = [] if image is None else [image]
    if shape is None:
        shapes = [(2, total, size, full) for size in sizes]
    else:
        sizes, shapes = [bins], [shape]
    result = pl.pallas_call(
        lambda *refs: cross_kernel(
            *refs,
            groups=groups,
            blocks=blocks,
            scale=scale,
            skipped=len(extra) + len(earlier),
            outs=len(sizes),
        ),
        grid_spec=pltpu.PrefetchScalarGridSpec(
            num_scalar_prefetch=1,
            grid=(full // width,),
            in_specs=[
                pl.BlockSpec((2, v.shape[1], bins, cols), lambda i, ids: (0, 0, 0, 0))
                for group in ins
                for v in group
            ]
            + [pl.BlockSpec((full, width), lambda i, ids: (0, i))] * 2
            + after(extra)
            + after(earlier),
            out_specs=[
                pl.BlockSpec((2, total, size, width), lambda i, ids: (0, place, 0, i))
                for size in sizes
            ],
            scratch_shapes=[pltpu.VMEM((2 * total * bins, full), jnp.bfloat16)],
        ),
        out_shape=[jax.ShapeDtypeStruct(v, jnp.bfloat16) for v in shapes],
        input_output_aliases={1 + groups * blocks + 2: 0} if extra else {},
        compiler_params=params(),
        cost_estimate=cost(8 * total * bins * full * full, 8 * total * bins * full + 4 * full * full),
        name="cross_transform",
    )(ids, *[v for group in ins for v in group], *tables, *extra, *earlier)
    return result if image is None and len(sizes) > 1 else result[0]


def exchange(value, axis, s):
    return lax.ppermute(value, axis, [(i, i ^ s) for i in range(lax.axis_size(axis))])


def halo_rows(polar):
    count = lax.axis_size("az")
    cols = polar.shape[2]
    ends = count - 1
    head = lax.slice_in_dim(polar, 0, HW, axis=2)
    tail = lax.slice_in_dim(polar, cols - HW, cols, axis=2)
    return jnp.concatenate(
        [
            lax.ppermute(tail, "az", [(i, i + 1) for i in range(ends)]),
            lax.ppermute(head, "az", [(i + 1, i) for i in range(ends)]),
        ],
        axis=2,
    )


def planned_path(polar, band_offset, tap_count, tap_weight):
    _, cuts, cols, freqs = polar.shape
    az_count = lax.axis_size("az")
    fq_count = lax.axis_size("fq")
    bins = F // (az_count * fq_count)
    split = SPLIT
    rest = bins - split
    ids = jnp.stack([lax.axis_index("az"), lax.axis_index("fq"), lax.axis_index("el")])
    tables = []
    for core in range(fq_count):
        order = np.concatenate([np.arange(freqs) + freqs * (core ^ s) for s in range(fq_count)])
        blocks = []
        for az in range(az_count):
            ks = (az * fq_count + core) * bins + np.arange(bins)
            blocks.append(np.concatenate(host_table(ks, order, F), axis=1))
        tables.append(np.stack(blocks))
    range_table = jnp.asarray(np.stack(tables))
    cross_tables = [jnp.asarray(t) for t in host_table(np.arange(A), np.arange(A), A)]
    order = np.concatenate([start + np.arange(count) for start, count in CHUNKS])
    matrix = jnp.asarray(height_table(cuts, ROWS, order))

    bands = (band_offset, tap_count, tap_weight)
    halo = halo_rows(polar)
    last = len(CHUNKS) - 1
    scale = 1.0 / math.sqrt(A)

    def interp(i, earlier=(), limit=VMEM):
        return interpolate(polar, halo, bands, *CHUNKS[i], earlier, limit)

    def to_owners(blocks, which=range(az_count - 1, 0, -1)):
        return {4 - s: exchange(blocks[s], "az", s) for s in which}

    def in_order(blocks, come):
        return [blocks[0]] + [come[4 - s] for s in range(1, az_count)]

    bare = interpolate(polar, None, bands, *CHUNKS[0], (), WIDE_VMEM)
    made = interpolate_edges(polar, halo, bands, CHUNKS[0][0], bare)
    other = exchange(made, "fq", 1)
    ahead = interp(1, (made,), WIDE_VMEM)
    own_first, other_first, landed = [], [], []
    moving = None
    for i in range(last + 1):
        limit = VMEM if i else WIDE_VMEM
        first, *blocks = range_transform(ids, made, other, range_table, split, (ahead,), limit)
        if 0 < i < last:
            ahead = interp(i + 1, (first,))
        first, blocks, ahead, moving = lax.optimization_barrier((first, blocks, ahead, moving))
        if i > 0:
            landed.append(in_order(held, moving[0]))
            other_first.append(moving[1])
        own_first.append(first)
        held = blocks
        moving = (to_owners(blocks), exchange(first, "el", 1))
        if i < last:
            made, other = ahead, exchange(ahead, "fq", 1)
    c0 = cross_transform(ids, landed, cross_tables, scale, [rest], earlier=(first,))
    c0, moving = lax.optimization_barrier((c0, moving))
    landed.append(in_order(held, moving[0]))
    other_first.append(moving[1])
    other_c0 = exchange(c0, "el", 1)

    made = first_heights(ids, matrix, own_first, other_first, PARTS, (c0,))
    come = to_owners(made[0])
    c1 = cross_transform(ids, landed[-1:], cross_tables, scale, [rest], earlier=(made[0][0],))
    other_c1 = exchange(c1, "el", 1)
    shape = (2, cuts, bins, A)
    full_scale = 1.0 / math.sqrt(A * 2 * cuts)
    made, come, c1 = lax.optimization_barrier((made, come, c1))
    arrived = in_order(made[0], come)
    come = to_owners(made[1])
    image = cross_transform(
        ids, [arrived], cross_tables, full_scale, image=None, shape=shape, place=0, earlier=(c1,)
    )
    image = last_heights(
        ids, matrix, [c0, c1], [other_c0, other_c1], (0, 0), image, shape, split, rest
    )
    image = cross_transform(
        ids,
        [in_order(made[1], come)],
        cross_tables,
        full_scale,
        image=image,
        shape=shape,
        place=PARTS[0] // PARTS[1],
    )
    return image


def on_device(polar, band_offset, tap_count, tap_weight):
    _, cuts, cols, freqs = polar.shape
    az_count = lax.axis_size("az")
    bins = F // (az_count * lax.axis_size("fq"))
    fits = (
        lax.axis_size("el") == 2
        and lax.axis_size("fq") == 2
        and az_count == 4
        and cuts == sum(count for _, count in CHUNKS) == sum(PARTS)
        and cols % (2 * LANES) == 0
        and freqs % LANES == 0
        and bins > SPLIT
        and bins == 2 * SPLIT
        and A % 512 == 0
        and 2 * HW == ROWS
    )
    chosen = planned_path if fits else general_path
    return chosen(polar, band_offset, tap_count, tap_weight)


def solution(mesh):
    in_specs = (
        P(None, ("grp", "el"), "az", "fq"),
        P("az", "fq"),
        P("az", "fq"),
        P(None, "az", "fq"),
    )
    out_specs = P(None, ("grp", "el"), ("az", "fq"), None)
    return jax.shard_map(
        on_device, mesh=mesh, in_specs=in_specs, out_specs=out_specs, check_vma=False
    )
```

```python
import math

import jax
import jax.numpy as jnp
import ml_dtypes
import numpy as np
from jax import lax
from jax.experimental import pallas as pl
from jax.experimental.pallas import tpu as pltpu
from jax.sharding import PartitionSpec as P

F = 768
A = 1024
E = 32
HW = 8
KT = 8

LANES = 128
ROWS = 16


def with_halo(cells, sides, width):
    for axis, dim in sides:
        count = lax.axis_size(axis)
        ends = count - 1
        head = lax.slice_in_dim(cells, 0, width, axis=dim)
        tail = lax.slice_in_dim(cells, cells.shape[dim] - width, cells.shape[dim], axis=dim)
        cells = jnp.concatenate(
            [
                lax.ppermute(tail, axis, [(i, (i + 1) % count) for i in range(ends)]),
                cells,
                lax.ppermute(head, axis, [((i + 1) % count, i) for i in range(ends)]),
            ],
            axis=dim,
        )
    return cells


def table_pair(row_ids, col_ids, length):
    product = row_ids[:, None] * col_ids[None, :] % length
    angle = product.astype(jnp.float32) * (2.0 * math.pi / length)
    return (jnp.cos(angle).astype(jnp.bfloat16), jnp.sin(angle).astype(jnp.bfloat16))


def general_path(polar, band_offset, tap_count, tap_weight):
    shape_all = polar.shape
    col_count = shape_all[2]
    freq_count = shape_all[3]
    az_count = lax.axis_size("az")
    fq_count = lax.axis_size("fq")
    el_count = lax.axis_size("el")
    padded = with_halo(polar, (("az", 2),), HW)
    window = col_count + 2 * HW
    column = jnp.arange(col_count, dtype=jnp.int32)[:, None]
    position = jnp.arange(window, dtype=jnp.int32)[None, :, None]
    band_matrix = jnp.zeros((col_count, window, freq_count), jnp.bfloat16)
    for tap_index in range(KT):
        reach = column + HW + band_offset + tap_index
        matches = (position == reach[:, None, :]) & (tap_index < tap_count)[:, None, :]
        band_matrix = jnp.where(matches, tap_weight[tap_index][:, None, :], band_matrix)
    interpolated = jnp.einsum(
        "jaf,ceaf->cejf", band_matrix, padded, preferred_element_type=jnp.float32
    ).astype(jnp.bfloat16)
    fq_index = lax.axis_index("fq")
    bin_count = F // (fq_count * az_count)
    az_block = jnp.arange(az_count, dtype=jnp.int32)[:, None]
    bin_local = jnp.arange(bin_count, dtype=jnp.int32)[None, :]
    range_bins = ((az_block * fq_count + fq_index) * bin_count + bin_local).reshape(-1)
    cos_f, sin_f = table_pair(jnp.arange(F, dtype=jnp.int32), range_bins, F)
    shard_piece = lax.all_gather(interpolated, "fq", axis=3, tiled=True)
    cos_rows = cos_f
    sin_rows = sin_f
    real_part = jnp.einsum(
        "ejf,fk->ekj", shard_piece[0], cos_rows, preferred_element_type=jnp.float32
    ) - jnp.einsum("ejf,fk->ekj", shard_piece[1], sin_rows, preferred_element_type=jnp.float32)
    imag_part = jnp.einsum(
        "ejf,fk->ekj", shard_piece[0], sin_rows, preferred_element_type=jnp.float32
    ) + jnp.einsum("ejf,fk->ekj", shard_piece[1], cos_rows, preferred_element_type=jnp.float32)
    summed = jnp.stack([real_part, imag_part])
    ranged = (summed * (1.0 / math.sqrt(F))).astype(jnp.bfloat16)
    azim_ids = jnp.arange(A, dtype=jnp.int32)
    cos_a, sin_a = table_pair(azim_ids, azim_ids, A)
    block_data = lax.all_to_all(ranged, "az", split_axis=2, concat_axis=3, tiled=True)
    real_part = jnp.einsum(
        "ekj,jm->ekm", block_data[0], cos_a, preferred_element_type=jnp.float32
    ) - jnp.einsum("ekj,jm->ekm", block_data[1], sin_a, preferred_element_type=jnp.float32)
    imag_part = jnp.einsum(
        "ekj,jm->ekm", block_data[0], sin_a, preferred_element_type=jnp.float32
    ) + jnp.einsum("ekj,jm->ekm", block_data[1], cos_a, preferred_element_type=jnp.float32)
    crossed = (jnp.stack([real_part, imag_part]) * (1.0 / math.sqrt(A))).astype(jnp.bfloat16)
    elev_ids = jnp.arange(E, dtype=jnp.int32)
    el_index = lax.axis_index("el")
    height_count = E // el_count
    height_rows = el_index * height_count + jnp.arange(height_count, dtype=jnp.int32)
    cos_e, sin_e = table_pair(elev_ids, height_rows, E)
    shard_piece = lax.all_gather(crossed, "el", axis=1, tiled=True)
    cos_rows = cos_e
    sin_rows = sin_e
    real_part = jnp.einsum(
        "eh,ekm->hkm", cos_rows, shard_piece[0], preferred_element_type=jnp.float32
    ) - jnp.einsum("eh,ekm->hkm", sin_rows, shard_piece[1], preferred_element_type=jnp.float32)
    imag_part = jnp.einsum(
        "eh,ekm->hkm", sin_rows, shard_piece[0], preferred_element_type=jnp.float32
    ) + jnp.einsum("eh,ekm->hkm", cos_rows, shard_piece[1], preferred_element_type=jnp.float32)
    totals = jnp.stack([real_part, imag_part])
    image_out = (totals * (1.0 / math.sqrt(E))).astype(jnp.bfloat16)
    return image_out


CHUNKS = ((0, 4), (4, 4), (8, 4), (12, 4))
PARTS = (8, 8)
SPLIT = 48
VMEM = 20 * 1024 * 1024
WIDE_VMEM = 60 * 1024 * 1024


def host_table(row_ids, col_ids, length):
    product = (row_ids[:, None] * col_ids[None, :]) % length
    angle = product.astype(np.float32) * np.float32(2.0 * math.pi / length)
    return (np.cos(angle).astype(ml_dtypes.bfloat16), np.sin(angle).astype(ml_dtypes.bfloat16))


def params(limit=VMEM):
    return pltpu.CompilerParams(vmem_limit_bytes=limit)


def cost(flops, nbytes):
    return pl.CostEstimate(flops=int(flops) // 1000, bytes_accessed=int(nbytes) // 1000, transcendentals=0)


def after(values):
    return [pl.BlockSpec(memory_space=pl.ANY)] * len(values)


def interp_rows(pad_ref, offset_ref, count_ref, weight_ref, out_ref, lane=slice(None)):
    _, cuts, cols, _ = out_ref.shape
    lanes = pad_ref.shape[2]
    step = 8

    def tile(index, carry):
        row = pl.multiple_of(index * ROWS, ROWS)
        rows = pl.ds(row, ROWS)
        base = offset_ref[rows, lane] + HW
        count = count_ref[rows, lane]
        zero = jnp.zeros((ROWS, lanes), jnp.float32)
        taps = [
            jnp.where(count > tap, weight_ref[tap, rows, lane].astype(jnp.float32), zero)
            for tap in range(KT)
        ]
        shift = 1
        while shift < KT:
            chosen = (base & shift) != 0
            taps = [jnp.where(chosen, taps[(r - shift) % KT], taps[r]) for r in range(KT)]
            shift *= 2
        halves = [slice(i, i + step) for i in range(0, ROWS, step)]
        past = [[base[half] > r for r in range(KT + 1)] for half in halves]
        taps = [[tap[half] for tap in taps] for half in halves]
        for part in range(2):
            for cut in range(cuts):
                plane = part * cuts + cut
                near = [
                    pad_ref[plane, pl.ds(row + d, step), :] for d in range(2 * HW + 1 + ROWS - step)
                ]
                totals = []
                for i in range(len(halves)):
                    here = near[i * step :]
                    total = None
                    for r in range(KT):
                        value = jnp.where(past[i][r], here[r + KT], here[r])
                        if r == 0:
                            value = jnp.where(past[i][KT], here[2 * KT], value)
                        value = value * taps[i][r]
                        total = value if total is None else total + value
                    totals.append(total)
                out_ref[part, cut, rows, lane] = jnp.concatenate(totals, axis=0).astype(jnp.bfloat16)
        return carry

    lax.fori_loop(0, cols // ROWS, tile, 0)


def interp_kernel(polar_ref, offset_ref, count_ref, weight_ref, *refs, bordered):
    out_ref, pad_ref = refs[-2:]
    _, cuts, cols, lanes = polar_ref.shape
    for part in range(2):
        for cut in range(cuts):
            plane = part * cuts + cut
            if bordered:
                halo = refs[0][part, cut].astype(jnp.float32)
            else:
                halo = jnp.zeros((2 * HW, lanes), jnp.float32)
            pad_ref[plane, pl.ds(0, HW), :] = halo[:HW]
            pad_ref[plane, pl.ds(HW, cols), :] = polar_ref[part, cut].astype(jnp.float32)
            pad_ref[plane, pl.ds(HW + cols, HW), :] = halo[HW:]
    interp_rows(pad_ref, offset_ref, count_ref, weight_ref, out_ref)


def chunk_spec(count, rows, first):
    return pl.BlockSpec((2, count, rows, LANES), lambda i: (0, first // count, 0, i))


def interpolate(polar, halo, bands, first, count, earlier=(), limit=VMEM):
    _, _, cols, freqs = polar.shape
    border = [] if halo is None else [halo]
    return pl.pallas_call(
        lambda *refs: interp_kernel(*refs, bordered=len(border) == 1),
        grid=(freqs // LANES,),
        in_specs=[
            chunk_spec(count, cols, first),
            pl.BlockSpec((cols, LANES), lambda i: (0, i)),
            pl.BlockSpec((cols, LANES), lambda i: (0, i)),
            pl.BlockSpec((KT, cols, LANES), lambda i: (0, 0, i)),
        ]
        + [chunk_spec(count, 2 * HW, first)] * len(border)
        + after(earlier),
        out_specs=chunk_spec(count, cols, 0),
        out_shape=jax.ShapeDtypeStruct((2, count, cols, freqs), jnp.bfloat16),
        scratch_shapes=[pltpu.VMEM((2 * count, cols + 2 * HW, LANES), jnp.float32)],
        compiler_params=params(limit),
        cost_estimate=cost(2 * count * cols * freqs * 34, 8 * count * cols * freqs),
        name="interpolate",
    )(polar, *bands, *border, *earlier)


def edge_kernel(polar_ref, halo_ref, offset_ref, count_ref, weight_ref, made_ref, out_ref, pad_ref):
    del made_ref
    _, cuts, rows, freqs = polar_ref.shape
    for start in range(0, freqs, LANES):
        lane = pl.ds(start, LANES)
        for part in range(2):
            for cut in range(cuts):
                plane = part * cuts + cut
                halo = halo_ref[part, cut, :, lane].astype(jnp.float32)
                body = polar_ref[part, cut, :, lane].astype(jnp.float32)
                left = jnp.concatenate([halo[:HW], body[: rows - HW]], axis=0)
                right = jnp.concatenate([body[HW:], halo[HW:]], axis=0)
                pad_ref[plane] = jnp.where(pl.program_id(0) == 0, left, right)
        interp_rows(pad_ref, offset_ref, count_ref, weight_ref, out_ref, lane)


def interpolate_edges(polar, halo, bands, first, made):
    _, count, cols, freqs = made.shape
    wide = cols // (2 * ROWS) - 1
    last = cols // ROWS - 1
    return pl.pallas_call(
        edge_kernel,
        grid=(2,),
        in_specs=[
            pl.BlockSpec((2, count, 2 * ROWS, freqs), lambda i: (0, first // count, i * wide, 0)),
            pl.BlockSpec((2, count, 2 * HW, freqs), lambda i: (0, first // count, 0, 0)),
            pl.BlockSpec((ROWS, freqs), lambda i: (i * last, 0)),
            pl.BlockSpec((ROWS, freqs), lambda i: (i * last, 0)),
            pl.BlockSpec((KT, ROWS, freqs), lambda i: (0, i * last, 0)),
            pl.BlockSpec(memory_space=pl.ANY),
        ],
        out_specs=pl.BlockSpec((2, count, ROWS, freqs), lambda i: (0, 0, i * last, 0)),
        out_shape=jax.ShapeDtypeStruct(made.shape, jnp.bfloat16),
        scratch_shapes=[pltpu.VMEM((2 * count, 2 * ROWS, LANES), jnp.float32)],
        input_output_aliases={5: 0},
        compiler_params=params(WIDE_VMEM),
        cost_estimate=cost(4 * count * ROWS * freqs * 34, 16 * count * ROWS * freqs),
        name="interpolate_edges",
    )(polar, halo, *bands, made)


def range_kernel(ids_ref, own_ref, other_ref, *refs, blocks, earlier):
    tables = refs[:blocks]
    first_ref, *rest = refs[blocks + earlier :]
    cuts, cols = own_ref.shape[1:3]
    bins = tables[0].shape[2]
    split = first_ref.shape[3]
    scale = 1.0 / math.sqrt(F)
    table = jnp.concatenate([ref[0, 0] for ref in tables], axis=0)
    for cut in range(cuts):
        real = [own_ref[0, cut], other_ref[0, cut]]
        imag = [own_ref[1, cut], other_ref[1, cut]]
        values = jnp.concatenate(
            [
                jnp.concatenate(real + [-v for v in imag], axis=1),
                jnp.concatenate(imag + real, axis=1),
            ],
            axis=0,
        )
        product = lax.dot_general(
            table, values, (((1,), (1,)), ((), ())), preferred_element_type=jnp.float32
        )
        product = (product * scale).astype(jnp.bfloat16)
        for s in range(blocks):
            for part in range(2):
                value = product[s * bins : (s + 1) * bins, part * cols : (part + 1) * cols]
                first_ref[part, cut, s] = value[:split]
                rest[s][part, cut] = value[split:]


def range_transform(ids, own, other, table, split, earlier=(), limit=VMEM):
    _, count, cols, freqs = own.shape
    _, blocks, bins, full = table.shape
    rest = bins - split
    group = 2

    def block_of(s):
        return pl.BlockSpec((1, 1, bins, full), lambda i, ids: (ids[1], ids[0] ^ s, 0, 0))

    return pl.pallas_call(
        lambda *refs: range_kernel(*refs, blocks=blocks, earlier=len(earlier)),
        grid_spec=pltpu.PrefetchScalarGridSpec(
            num_scalar_prefetch=1,
            grid=(count // group,),
            in_specs=[pl.BlockSpec((2, group, cols, freqs), lambda i, ids: (0, i, 0, 0))] * 2
            + [block_of(s) for s in range(blocks)]
            + after(earlier),
            out_specs=[
                pl.BlockSpec((2, group, blocks, split, cols), lambda i, ids: (0, i, 0, 0, 0))
            ]
            + [pl.BlockSpec((2, group, rest, cols), lambda i, ids: (0, i, 0, 0))] * blocks,
        ),
        out_shape=[jax.ShapeDtypeStruct((2, count, blocks, split, cols), jnp.bfloat16)]
        + [jax.ShapeDtypeStruct((2, count, rest, cols), jnp.bfloat16)] * blocks,
        compiler_params=params(limit),
        cost_estimate=cost(4 * count * cols * full * blocks * bins, 12 * count * cols * freqs),
        name="range_transform",
    )(ids, own, other, *([table] * blocks), *earlier)


def height_table(cuts, rows, order):
    heights = []
    for el in range(2):
        pair = []
        for parity in range(2):
            h = el * cuts + parity + 2 * np.arange(cuts // 2)
            cos, sin = (t.astype(np.float32) for t in host_table(h, order, 2 * cuts))
            sign = -1.0 if el and parity else 1.0
            whole = sign * np.block([[cos, -sin], [sin, cos]])
            pair.append(np.kron(whole, np.eye(rows, dtype=np.float32)))
        heights.append(np.stack(pair))
    return np.stack(heights).astype(ml_dtypes.bfloat16)


def height_kernel(ids_ref, matrix_ref, *refs, chunks, sets, outs, scale, skipped):
    ins = refs[: 2 * chunks]
    out_refs = refs[2 * chunks + skipped :]
    rows, lanes = ins[0].shape[-2:]
    half = matrix_ref.shape[2] // (2 * rows)
    for index in range(sets):
        sums, differences = [], []
        for part in range(2):
            for own, other in zip(ins[:chunks], ins[chunks:]):
                pad = (index,) if len(own.shape) == 5 else ()
                for e in range(own.shape[1]):
                    a, b = own[(part, e) + pad], other[(part, e) + pad]
                    sums.append(a + b)
                    differences.append(a - b)
        results = [
            jnp.dot(
                matrix_ref[0, parity],
                jnp.concatenate(values, axis=0),
                preferred_element_type=jnp.float32,
            )
            for parity, values in enumerate((sums, differences))
        ]
        h = 0
        for ref in out_refs[index * outs : (index + 1) * outs]:
            for row in range(ref.shape[1]):
                for part in range(2):
                    start = (part * half + h // 2) * rows
                    value = results[h % 2][start : start + rows]
                    if scale is not None:
                        value = value * scale
                    ref[part, row] = value.astype(jnp.bfloat16)
                h += 1


def first_heights(ids, matrix, own, other, parts, earlier=()):
    chunks = len(own)
    _, _, blocks, split, cols = own[0].shape
    total = sum(v.shape[1] for v in own)
    spec = [
        pl.BlockSpec((2, v.shape[1], blocks, ROWS, cols), lambda i, ids: (0, 0, 0, i, 0))
        for v in own
    ]
    outs = list(parts) * blocks
    made = pl.pallas_call(
        lambda *refs: height_kernel(
            *refs, chunks=chunks, sets=blocks, outs=len(parts), scale=None, skipped=len(earlier)
        ),
        grid_spec=pltpu.PrefetchScalarGridSpec(
            num_scalar_prefetch=1,
            grid=(split // ROWS,),
            in_specs=[pl.BlockSpec((1,) + matrix.shape[1:], lambda i, ids: (ids[2], 0, 0, 0))]
            + spec
            + spec
            + after(earlier),
            out_specs=[pl.BlockSpec((2, h, ROWS, cols), lambda i, ids: (0, 0, i, 0)) for h in outs],
        ),
        out_shape=[jax.ShapeDtypeStruct((2, h, split, cols), jnp.bfloat16) for h in outs],
        compiler_params=params(),
        cost_estimate=cost(blocks * split * cols * 32768, 12 * blocks * total * split * cols),
        name="first_heights",
    )(ids, matrix, *own, *other, *earlier)
    return [[made[s * len(parts) + p] for s in range(blocks)] for p in range(len(parts))]


def last_heights(ids, matrix, own, other, places, image, shape, skip, rows, earlier=()):
    chunks = len(own)
    full = own[0].shape[3]
    width = min(full, 512)
    total = sum(v.shape[1] for v in own)

    def chunk(v, place):
        return pl.BlockSpec(
            (2, v.shape[1], ROWS, width), lambda i, j, ids: (0, 0, place // ROWS + i, j)
        )

    spec = [chunk(v, place) for v, place in zip(own, places)]
    extra = [] if image is None else [image]
    first = skip // ROWS
    return pl.pallas_call(
        lambda *refs: height_kernel(
            *refs,
            chunks=chunks,
            sets=1,
            outs=1,
            scale=1.0 / math.sqrt(2 * total),
            skipped=len(earlier) + len(extra),
        ),
        grid_spec=pltpu.PrefetchScalarGridSpec(
            num_scalar_prefetch=1,
            grid=(rows // ROWS, full // width),
            in_specs=[pl.BlockSpec((1,) + matrix.shape[1:], lambda i, j, ids: (ids[2], 0, 0, 0))]
            + spec
            + spec
            + after(extra)
            + after(earlier),
            out_specs=pl.BlockSpec((2, total, ROWS, width), lambda i, j, ids: (0, 0, first + i, j)),
        ),
        out_shape=jax.ShapeDtypeStruct(shape, jnp.bfloat16),
        input_output_aliases={2 + 2 * chunks: 0} if extra else {},
        compiler_params=params(),
        cost_estimate=cost(rows * full * 32768, 12 * total * rows * full),
        name="last_heights",
    )(ids, matrix, *own, *other, *extra, *earlier)


def cross_kernel(ids_ref, *refs, groups, blocks, scale, skipped, outs):
    ins = [refs[g * blocks : (g + 1) * blocks] for g in range(groups)]
    cos_ref, sin_ref = refs[groups * blocks : groups * blocks + 2]
    out_refs = refs[groups * blocks + 2 + skipped : -1]
    rows_ref = refs[-1]
    bins, cols = ins[0][0].shape[2:]
    cuts = [group[0].shape[1] for group in ins]
    rows = sum(cuts) * bins

    @pl.when(pl.program_id(0) == 0)
    def _():
        for s in range(blocks):
            start = pl.multiple_of((ids_ref[0] ^ s) * cols, cols)
            for part in range(2):
                place = part * rows
                for group, count in zip(ins, cuts):
                    rows_ref[pl.ds(place, count * bins), pl.ds(start, cols)] = group[s][
                        part
                    ].reshape(count * bins, cols)
                    place += count * bins

    values = rows_ref[...]
    with_cos = jnp.dot(values, cos_ref[...], preferred_element_type=jnp.float32)
    with_sin = jnp.dot(values, sin_ref[...], preferred_element_type=jnp.float32)
    real = (with_cos[:rows] - with_sin[rows:]) * scale
    imag = (with_sin[:rows] + with_cos[rows:]) * scale
    for part, value in ((0, real), (1, imag)):
        value = value.astype(jnp.bfloat16).reshape(sum(cuts), bins, value.shape[1])
        place = 0
        for ref in out_refs:
            size = ref.shape[2]
            ref[part] = value[:, place : place + size]
            place += size


def cross_transform(ids, ins, tables, scale, sizes=None, image=None, shape=None, place=0, earlier=()):
    groups, blocks = len(ins), len(ins[0])
    bins, cols = ins[0][0].shape[2:]
    total = sum(group[0].shape[1] for group in ins)
    full = tables[0].shape[1]
    width = min(full, 512)
    extra = [] if image is None else [image]
    if shape is None:
        shapes = [(2, total, size, full) for size in sizes]
    else:
        sizes, shapes = [bins], [shape]
    result = pl.pallas_call(
        lambda *refs: cross_kernel(
            *refs,
            groups=groups,
            blocks=blocks,
            scale=scale,
            skipped=len(extra) + len(earlier),
            outs=len(sizes),
        ),
        grid_spec=pltpu.PrefetchScalarGridSpec(
            num_scalar_prefetch=1,
            grid=(full // width,),
            in_specs=[
                pl.BlockSpec((2, v.shape[1], bins, cols), lambda i, ids: (0, 0, 0, 0))
                for group in ins
                for v in group
            ]
            + [pl.BlockSpec((full, width), lambda i, ids: (0, i))] * 2
            + after(extra)
            + after(earlier),
            out_specs=[
                pl.BlockSpec((2, total, size, width), lambda i, ids: (0, place, 0, i))
                for size in sizes
            ],
            scratch_shapes=[pltpu.VMEM((2 * total * bins, full), jnp.bfloat16)],
        ),
        out_shape=[jax.ShapeDtypeStruct(v, jnp.bfloat16) for v in shapes],
        input_output_aliases={1 + groups * blocks + 2: 0} if extra else {},
        compiler_params=params(),
        cost_estimate=cost(8 * total * bins * full * full, 8 * total * bins * full + 4 * full * full),
        name="cross_transform",
    )(ids, *[v for group in ins for v in group], *tables, *extra, *earlier)
    return result if image is None and len(sizes) > 1 else result[0]


def exchange(value, axis, s):
    return lax.ppermute(value, axis, [(i, i ^ s) for i in range(lax.axis_size(axis))])


def halo_rows(polar):
    count = lax.axis_size("az")
    cols = polar.shape[2]
    ends = count - 1
    head = lax.slice_in_dim(polar, 0, HW, axis=2)
    tail = lax.slice_in_dim(polar, cols - HW, cols, axis=2)
    return jnp.concatenate(
        [
            lax.ppermute(tail, "az", [(i, i + 1) for i in range(ends)]),
            lax.ppermute(head, "az", [(i + 1, i) for i in range(ends)]),
        ],
        axis=2,
    )


def planned_path(polar, band_offset, tap_count, tap_weight):
    _, cuts, cols, freqs = polar.shape
    az_count = lax.axis_size("az")
    fq_count = lax.axis_size("fq")
    bins = F // (az_count * fq_count)
    split = SPLIT
    rest = bins - split
    ids = jnp.stack([lax.axis_index("az"), lax.axis_index("fq"), lax.axis_index("el")])
    tables = []
    for core in range(fq_count):
        order = np.concatenate([np.arange(freqs) + freqs * (core ^ s) for s in range(fq_count)])
        blocks = []
        for az in range(az_count):
            ks = (az * fq_count + core) * bins + np.arange(bins)
            blocks.append(np.concatenate(host_table(ks, order, F), axis=1))
        tables.append(np.stack(blocks))
    range_table = jnp.asarray(np.stack(tables))
    cross_tables = [jnp.asarray(t) for t in host_table(np.arange(A), np.arange(A), A)]
    order = np.concatenate([start + np.arange(count) for start, count in CHUNKS])
    matrix = jnp.asarray(height_table(cuts, ROWS, order))

    bands = (band_offset, tap_count, tap_weight)
    halo = halo_rows(polar)
    last = len(CHUNKS) - 1
    scale = 1.0 / math.sqrt(A)

    def interp(i, earlier=(), limit=VMEM):
        return interpolate(polar, halo, bands, *CHUNKS[i], earlier, limit)

    def to_owners(blocks, which=range(az_count - 1, 0, -1)):
        return {4 - s: exchange(blocks[s], "az", s) for s in which}

    def in_order(blocks, come):
        return [blocks[0]] + [come[4 - s] for s in range(1, az_count)]

    bare = interpolate(polar, None, bands, *CHUNKS[0], (), WIDE_VMEM)
    made = interpolate_edges(polar, halo, bands, CHUNKS[0][0], bare)
    other = exchange(made, "fq", 1)
    ahead = interp(1, (made,), WIDE_VMEM)
    own_first, other_first, landed = [], [], []
    moving = None
    for i in range(last + 1):
        limit = VMEM if i else WIDE_VMEM
        first, *blocks = range_transform(ids, made, other, range_table, split, (ahead,), limit)
        if 0 < i < last:
            ahead = interp(i + 1, (first,))
        first, blocks, ahead, moving = lax.optimization_barrier((first, blocks, ahead, moving))
        if i > 0:
            landed.append(in_order(held, moving[0]))
            other_first.append(moving[1])
        own_first.append(first)
        held = blocks
        moving = (to_owners(blocks), exchange(first, "el", 1))
        if i < last:
            made, other = ahead, exchange(ahead, "fq", 1)
    c0 = cross_transform(ids, landed, cross_tables, scale, [rest], earlier=(first,))
    c0, moving = lax.optimization_barrier((c0, moving))
    landed.append(in_order(held, moving[0]))
    other_first.append(moving[1])
    other_c0 = exchange(c0, "el", 1)

    made = first_heights(ids, matrix, own_first, other_first, PARTS, (c0,))
    come = to_owners(made[0])
    late = [rest - ROWS, ROWS]
    c1, c2 = cross_transform(ids, landed[-1:], cross_tables, scale, late, earlier=(made[0][0],))
    other_c1 = exchange(c1, "el", 1)
    shape = (2, cuts, bins, A)
    full_scale = 1.0 / math.sqrt(A * 2 * cuts)
    made, come, c2 = lax.optimization_barrier((made, come, c2))
    arrived = in_order(made[0], come)
    come = to_owners(made[1])
    image = cross_transform(
        ids, [arrived], cross_tables, full_scale, image=None, shape=shape, place=0, earlier=(c1,)
    )
    image, c2, other_c0 = lax.optimization_barrier((image, c2, other_c0))
    other_c2 = exchange(c2, "el", 1)
    image = last_heights(
        ids, matrix, [c0, c1], [other_c0, other_c1], (0, 0), image, shape, split, late[0]
    )
    image = last_heights(
        ids, matrix, [c0, c2], [other_c0, other_c2], (late[0], 0), image, shape, split + late[0], late[1]
    )
    image = cross_transform(
        ids,
        [in_order(made[1], come)],
        cross_tables,
        full_scale,
        image=image,
        shape=shape,
        place=PARTS[0] // PARTS[1],
    )
    return image


def on_device(polar, band_offset, tap_count, tap_weight):
    _, cuts, cols, freqs = polar.shape
    az_count = lax.axis_size("az")
    bins = F // (az_count * lax.axis_size("fq"))
    fits = (
        lax.axis_size("el") == 2
        and lax.axis_size("fq") == 2
        and az_count == 4
        and cuts == sum(count for _, count in CHUNKS) == sum(PARTS)
        and cols % (2 * LANES) == 0
        and freqs % LANES == 0
        and bins > SPLIT
        and bins == 2 * SPLIT
        and A % 512 == 0
        and 2 * HW == ROWS
    )
    chosen = planned_path if fits else general_path
    return chosen(polar, band_offset, tap_count, tap_weight)


def solution(mesh):
    in_specs = (
        P(None, ("grp", "el"), "az", "fq"),
        P("az", "fq"),
        P("az", "fq"),
        P(None, "az", "fq"),
    )
    out_specs = P(None, ("grp", "el"), ("az", "fq"), None)
    return jax.shard_map(
        on_device, mesh=mesh, in_specs=in_specs, out_specs=out_specs, check_vma=False
    )
```

```python
import math

import jax
import jax.numpy as jnp
import ml_dtypes
import numpy as np
from jax import lax
from jax.experimental import pallas as pl
from jax.experimental.pallas import tpu as pltpu
from jax.sharding import PartitionSpec as P

F = 768
A = 1024
E = 32
HW = 8
KT = 8

LANES = 128
ROWS = 16


def with_halo(cells, sides, width):
    for axis, dim in sides:
        count = lax.axis_size(axis)
        ends = count - 1
        head = lax.slice_in_dim(cells, 0, width, axis=dim)
        tail = lax.slice_in_dim(cells, cells.shape[dim] - width, cells.shape[dim], axis=dim)
        cells = jnp.concatenate(
            [
                lax.ppermute(tail, axis, [(i, (i + 1) % count) for i in range(ends)]),
                cells,
                lax.ppermute(head, axis, [((i + 1) % count, i) for i in range(ends)]),
            ],
            axis=dim,
        )
    return cells


def table_pair(row_ids, col_ids, length):
    product = row_ids[:, None] * col_ids[None, :] % length
    angle = product.astype(jnp.float32) * (2.0 * math.pi / length)
    return (jnp.cos(angle).astype(jnp.bfloat16), jnp.sin(angle).astype(jnp.bfloat16))


def general_path(polar, band_offset, tap_count, tap_weight):
    shape_all = polar.shape
    col_count = shape_all[2]
    freq_count = shape_all[3]
    az_count = lax.axis_size("az")
    fq_count = lax.axis_size("fq")
    el_count = lax.axis_size("el")
    padded = with_halo(polar, (("az", 2),), HW)
    window = col_count + 2 * HW
    column = jnp.arange(col_count, dtype=jnp.int32)[:, None]
    position = jnp.arange(window, dtype=jnp.int32)[None, :, None]
    band_matrix = jnp.zeros((col_count, window, freq_count), jnp.bfloat16)
    for tap_index in range(KT):
        reach = column + HW + band_offset + tap_index
        matches = (position == reach[:, None, :]) & (tap_index < tap_count)[:, None, :]
        band_matrix = jnp.where(matches, tap_weight[tap_index][:, None, :], band_matrix)
    interpolated = jnp.einsum(
        "jaf,ceaf->cejf", band_matrix, padded, preferred_element_type=jnp.float32
    ).astype(jnp.bfloat16)
    fq_index = lax.axis_index("fq")
    bin_count = F // (fq_count * az_count)
    az_block = jnp.arange(az_count, dtype=jnp.int32)[:, None]
    bin_local = jnp.arange(bin_count, dtype=jnp.int32)[None, :]
    range_bins = ((az_block * fq_count + fq_index) * bin_count + bin_local).reshape(-1)
    cos_f, sin_f = table_pair(jnp.arange(F, dtype=jnp.int32), range_bins, F)
    shard_piece = lax.all_gather(interpolated, "fq", axis=3, tiled=True)
    cos_rows = cos_f
    sin_rows = sin_f
    real_part = jnp.einsum(
        "ejf,fk->ekj", shard_piece[0], cos_rows, preferred_element_type=jnp.float32
    ) - jnp.einsum("ejf,fk->ekj", shard_piece[1], sin_rows, preferred_element_type=jnp.float32)
    imag_part = jnp.einsum(
        "ejf,fk->ekj", shard_piece[0], sin_rows, preferred_element_type=jnp.float32
    ) + jnp.einsum("ejf,fk->ekj", shard_piece[1], cos_rows, preferred_element_type=jnp.float32)
    summed = jnp.stack([real_part, imag_part])
    ranged = (summed * (1.0 / math.sqrt(F))).astype(jnp.bfloat16)
    azim_ids = jnp.arange(A, dtype=jnp.int32)
    cos_a, sin_a = table_pair(azim_ids, azim_ids, A)
    block_data = lax.all_to_all(ranged, "az", split_axis=2, concat_axis=3, tiled=True)
    real_part = jnp.einsum(
        "ekj,jm->ekm", block_data[0], cos_a, preferred_element_type=jnp.float32
    ) - jnp.einsum("ekj,jm->ekm", block_data[1], sin_a, preferred_element_type=jnp.float32)
    imag_part = jnp.einsum(
        "ekj,jm->ekm", block_data[0], sin_a, preferred_element_type=jnp.float32
    ) + jnp.einsum("ekj,jm->ekm", block_data[1], cos_a, preferred_element_type=jnp.float32)
    crossed = (jnp.stack([real_part, imag_part]) * (1.0 / math.sqrt(A))).astype(jnp.bfloat16)
    elev_ids = jnp.arange(E, dtype=jnp.int32)
    el_index = lax.axis_index("el")
    height_count = E // el_count
    height_rows = el_index * height_count + jnp.arange(height_count, dtype=jnp.int32)
    cos_e, sin_e = table_pair(elev_ids, height_rows, E)
    shard_piece = lax.all_gather(crossed, "el", axis=1, tiled=True)
    cos_rows = cos_e
    sin_rows = sin_e
    real_part = jnp.einsum(
        "eh,ekm->hkm", cos_rows, shard_piece[0], preferred_element_type=jnp.float32
    ) - jnp.einsum("eh,ekm->hkm", sin_rows, shard_piece[1], preferred_element_type=jnp.float32)
    imag_part = jnp.einsum(
        "eh,ekm->hkm", sin_rows, shard_piece[0], preferred_element_type=jnp.float32
    ) + jnp.einsum("eh,ekm->hkm", cos_rows, shard_piece[1], preferred_element_type=jnp.float32)
    totals = jnp.stack([real_part, imag_part])
    image_out = (totals * (1.0 / math.sqrt(E))).astype(jnp.bfloat16)
    return image_out


CHUNKS = ((0, 4), (4, 4), (8, 4), (12, 4))
PARTS = (8, 8)
SPLIT = 48
VMEM = 20 * 1024 * 1024
WIDE_VMEM = 60 * 1024 * 1024


def host_table(row_ids, col_ids, length):
    product = (row_ids[:, None] * col_ids[None, :]) % length
    angle = product.astype(np.float32) * np.float32(2.0 * math.pi / length)
    return (np.cos(angle).astype(ml_dtypes.bfloat16), np.sin(angle).astype(ml_dtypes.bfloat16))


def params(limit=VMEM):
    return pltpu.CompilerParams(vmem_limit_bytes=limit)


def cost(flops, nbytes):
    return pl.CostEstimate(flops=int(flops) // 1000, bytes_accessed=int(nbytes) // 1000, transcendentals=0)


def after(values):
    return [pl.BlockSpec(memory_space=pl.ANY)] * len(values)


def interp_rows(pad_ref, offset_ref, count_ref, weight_ref, out_ref, lane=slice(None)):
    _, cuts, cols, _ = out_ref.shape
    lanes = pad_ref.shape[2]
    step = 8

    def tile(index, carry):
        row = pl.multiple_of(index * ROWS, ROWS)
        rows = pl.ds(row, ROWS)
        base = offset_ref[rows, lane] + HW
        count = count_ref[rows, lane]
        zero = jnp.zeros((ROWS, lanes), jnp.float32)
        taps = [
            jnp.where(count > tap, weight_ref[tap, rows, lane].astype(jnp.float32), zero)
            for tap in range(KT)
        ]
        shift = 1
        while shift < KT:
            chosen = (base & shift) != 0
            taps = [jnp.where(chosen, taps[(r - shift) % KT], taps[r]) for r in range(KT)]
            shift *= 2
        halves = [slice(i, i + step) for i in range(0, ROWS, step)]
        past = [[base[half] > r for r in range(KT + 1)] for half in halves]
        taps = [[tap[half] for tap in taps] for half in halves]
        for part in range(2):
            for cut in range(cuts):
                plane = part * cuts + cut
                near = [
                    pad_ref[plane, pl.ds(row + d, step), :] for d in range(2 * HW + 1 + ROWS - step)
                ]
                totals = []
                for i in range(len(halves)):
                    here = near[i * step :]
                    total = None
                    for r in range(KT):
                        value = jnp.where(past[i][r], here[r + KT], here[r])
                        if r == 0:
                            value = jnp.where(past[i][KT], here[2 * KT], value)
                        value = value * taps[i][r]
                        total = value if total is None else total + value
                    totals.append(total)
                out_ref[part, cut, rows, lane] = jnp.concatenate(totals, axis=0).astype(jnp.bfloat16)
        return carry

    lax.fori_loop(0, cols // ROWS, tile, 0)


def interp_kernel(polar_ref, offset_ref, count_ref, weight_ref, *refs, bordered):
    out_ref, pad_ref = refs[-2:]
    _, cuts, cols, lanes = polar_ref.shape
    for part in range(2):
        for cut in range(cuts):
            plane = part * cuts + cut
            if bordered:
                halo = refs[0][part, cut].astype(jnp.float32)
            else:
                halo = jnp.zeros((2 * HW, lanes), jnp.float32)
            pad_ref[plane, pl.ds(0, HW), :] = halo[:HW]
            pad_ref[plane, pl.ds(HW, cols), :] = polar_ref[part, cut].astype(jnp.float32)
            pad_ref[plane, pl.ds(HW + cols, HW), :] = halo[HW:]
    interp_rows(pad_ref, offset_ref, count_ref, weight_ref, out_ref)


def chunk_spec(count, rows, first):
    return pl.BlockSpec((2, count, rows, LANES), lambda i: (0, first // count, 0, i))


def interpolate(polar, halo, bands, first, count, earlier=(), limit=VMEM):
    _, _, cols, freqs = polar.shape
    border = [] if halo is None else [halo]
    return pl.pallas_call(
        lambda *refs: interp_kernel(*refs, bordered=len(border) == 1),
        grid=(freqs // LANES,),
        in_specs=[
            chunk_spec(count, cols, first),
            pl.BlockSpec((cols, LANES), lambda i: (0, i)),
            pl.BlockSpec((cols, LANES), lambda i: (0, i)),
            pl.BlockSpec((KT, cols, LANES), lambda i: (0, 0, i)),
        ]
        + [chunk_spec(count, 2 * HW, first)] * len(border)
        + after(earlier),
        out_specs=chunk_spec(count, cols, 0),
        out_shape=jax.ShapeDtypeStruct((2, count, cols, freqs), jnp.bfloat16),
        scratch_shapes=[pltpu.VMEM((2 * count, cols + 2 * HW, LANES), jnp.float32)],
        compiler_params=params(limit),
        cost_estimate=cost(2 * count * cols * freqs * 34, 8 * count * cols * freqs),
        name="interpolate",
    )(polar, *bands, *border, *earlier)


def edge_kernel(polar_ref, halo_ref, offset_ref, count_ref, weight_ref, made_ref, out_ref, pad_ref):
    del made_ref
    _, cuts, rows, freqs = polar_ref.shape
    for start in range(0, freqs, LANES):
        lane = pl.ds(start, LANES)
        for part in range(2):
            for cut in range(cuts):
                plane = part * cuts + cut
                halo = halo_ref[part, cut, :, lane].astype(jnp.float32)
                body = polar_ref[part, cut, :, lane].astype(jnp.float32)
                left = jnp.concatenate([halo[:HW], body[: rows - HW]], axis=0)
                right = jnp.concatenate([body[HW:], halo[HW:]], axis=0)
                pad_ref[plane] = jnp.where(pl.program_id(0) == 0, left, right)
        interp_rows(pad_ref, offset_ref, count_ref, weight_ref, out_ref, lane)


def interpolate_edges(polar, halo, bands, first, made):
    _, count, cols, freqs = made.shape
    wide = cols // (2 * ROWS) - 1
    last = cols // ROWS - 1
    return pl.pallas_call(
        edge_kernel,
        grid=(2,),
        in_specs=[
            pl.BlockSpec((2, count, 2 * ROWS, freqs), lambda i: (0, first // count, i * wide, 0)),
            pl.BlockSpec((2, count, 2 * HW, freqs), lambda i: (0, first // count, 0, 0)),
            pl.BlockSpec((ROWS, freqs), lambda i: (i * last, 0)),
            pl.BlockSpec((ROWS, freqs), lambda i: (i * last, 0)),
            pl.BlockSpec((KT, ROWS, freqs), lambda i: (0, i * last, 0)),
            pl.BlockSpec(memory_space=pl.ANY),
        ],
        out_specs=pl.BlockSpec((2, count, ROWS, freqs), lambda i: (0, 0, i * last, 0)),
        out_shape=jax.ShapeDtypeStruct(made.shape, jnp.bfloat16),
        scratch_shapes=[pltpu.VMEM((2 * count, 2 * ROWS, LANES), jnp.float32)],
        input_output_aliases={5: 0},
        compiler_params=params(WIDE_VMEM),
        cost_estimate=cost(4 * count * ROWS * freqs * 34, 16 * count * ROWS * freqs),
        name="interpolate_edges",
    )(polar, halo, *bands, made)


def range_kernel(ids_ref, own_ref, other_ref, *refs, blocks, earlier):
    tables = refs[:blocks]
    first_ref, *rest = refs[blocks + earlier :]
    cuts, cols = own_ref.shape[1:3]
    bins = tables[0].shape[2]
    split = first_ref.shape[3]
    scale = 1.0 / math.sqrt(F)
    table = jnp.concatenate([ref[0, 0] for ref in tables], axis=0)
    for cut in range(cuts):
        real = [own_ref[0, cut], other_ref[0, cut]]
        imag = [own_ref[1, cut], other_ref[1, cut]]
        values = jnp.concatenate(
            [
                jnp.concatenate(real + [-v for v in imag], axis=1),
                jnp.concatenate(imag + real, axis=1),
            ],
            axis=0,
        )
        product = lax.dot_general(
            table, values, (((1,), (1,)), ((), ())), preferred_element_type=jnp.float32
        )
        product = (product * scale).astype(jnp.bfloat16)
        for s in range(blocks):
            for part in range(2):
                value = product[s * bins : (s + 1) * bins, part * cols : (part + 1) * cols]
                first_ref[part, cut, s] = value[:split]
                rest[s][part, cut] = value[split:]


def range_transform(ids, own, other, table, split, earlier=(), limit=VMEM):
    _, count, cols, freqs = own.shape
    _, blocks, bins, full = table.shape
    rest = bins - split
    group = 2

    def block_of(s):
        return pl.BlockSpec((1, 1, bins, full), lambda i, ids: (ids[1], ids[0] ^ s, 0, 0))

    return pl.pallas_call(
        lambda *refs: range_kernel(*refs, blocks=blocks, earlier=len(earlier)),
        grid_spec=pltpu.PrefetchScalarGridSpec(
            num_scalar_prefetch=1,
            grid=(count // group,),
            in_specs=[pl.BlockSpec((2, group, cols, freqs), lambda i, ids: (0, i, 0, 0))] * 2
            + [block_of(s) for s in range(blocks)]
            + after(earlier),
            out_specs=[
                pl.BlockSpec((2, group, blocks, split, cols), lambda i, ids: (0, i, 0, 0, 0))
            ]
            + [pl.BlockSpec((2, group, rest, cols), lambda i, ids: (0, i, 0, 0))] * blocks,
        ),
        out_shape=[jax.ShapeDtypeStruct((2, count, blocks, split, cols), jnp.bfloat16)]
        + [jax.ShapeDtypeStruct((2, count, rest, cols), jnp.bfloat16)] * blocks,
        compiler_params=params(limit),
        cost_estimate=cost(4 * count * cols * full * blocks * bins, 12 * count * cols * freqs),
        name="range_transform",
    )(ids, own, other, *([table] * blocks), *earlier)


def height_table(cuts, rows, order):
    heights = []
    for el in range(2):
        pair = []
        for parity in range(2):
            h = el * cuts + parity + 2 * np.arange(cuts // 2)
            cos, sin = (t.astype(np.float32) for t in host_table(h, order, 2 * cuts))
            sign = -1.0 if el and parity else 1.0
            whole = sign * np.block([[cos, -sin], [sin, cos]])
            pair.append(np.kron(whole, np.eye(rows, dtype=np.float32)))
        heights.append(np.stack(pair))
    return np.stack(heights).astype(ml_dtypes.bfloat16)


def height_kernel(ids_ref, matrix_ref, *refs, chunks, sets, outs, scale, skipped):
    ins = refs[: 2 * chunks]
    out_refs = refs[2 * chunks + skipped :]
    rows, lanes = ins[0].shape[-2:]
    half = matrix_ref.shape[2] // (2 * rows)
    for index in range(sets):
        sums, differences = [], []
        for part in range(2):
            for own, other in zip(ins[:chunks], ins[chunks:]):
                pad = (index,) if len(own.shape) == 5 else ()
                for e in range(own.shape[1]):
                    a, b = own[(part, e) + pad], other[(part, e) + pad]
                    sums.append(a + b)
                    differences.append(a - b)
        results = [
            jnp.dot(
                matrix_ref[0, parity],
                jnp.concatenate(values, axis=0),
                preferred_element_type=jnp.float32,
            )
            for parity, values in enumerate((sums, differences))
        ]
        h = 0
        for ref in out_refs[index * outs : (index + 1) * outs]:
            for row in range(ref.shape[1]):
                for part in range(2):
                    start = (part * half + h // 2) * rows
                    value = results[h % 2][start : start + rows]
                    if scale is not None:
                        value = value * scale
                    ref[part, row] = value.astype(jnp.bfloat16)
                h += 1


def first_heights(ids, matrix, own, other, parts, earlier=()):
    chunks = len(own)
    _, _, blocks, split, cols = own[0].shape
    total = sum(v.shape[1] for v in own)
    spec = [
        pl.BlockSpec((2, v.shape[1], blocks, ROWS, cols), lambda i, ids: (0, 0, 0, i, 0))
        for v in own
    ]
    outs = list(parts) * blocks
    made = pl.pallas_call(
        lambda *refs: height_kernel(
            *refs, chunks=chunks, sets=blocks, outs=len(parts), scale=None, skipped=len(earlier)
        ),
        grid_spec=pltpu.PrefetchScalarGridSpec(
            num_scalar_prefetch=1,
            grid=(split // ROWS,),
            in_specs=[pl.BlockSpec((1,) + matrix.shape[1:], lambda i, ids: (ids[2], 0, 0, 0))]
            + spec
            + spec
            + after(earlier),
            out_specs=[pl.BlockSpec((2, h, ROWS, cols), lambda i, ids: (0, 0, i, 0)) for h in outs],
        ),
        out_shape=[jax.ShapeDtypeStruct((2, h, split, cols), jnp.bfloat16) for h in outs],
        compiler_params=params(),
        cost_estimate=cost(blocks * split * cols * 32768, 12 * blocks * total * split * cols),
        name="first_heights",
    )(ids, matrix, *own, *other, *earlier)
    return [[made[s * len(parts) + p] for s in range(blocks)] for p in range(len(parts))]


def last_heights(ids, matrix, own, other, places, image, shape, skip, rows, earlier=()):
    chunks = len(own)
    full = own[0].shape[3]
    width = min(full, 512)
    total = sum(v.shape[1] for v in own)

    def chunk(v, place):
        return pl.BlockSpec(
            (2, v.shape[1], ROWS, width), lambda i, j, ids: (0, 0, place // ROWS + i, j)
        )

    spec = [chunk(v, place) for v, place in zip(own, places)]
    extra = [] if image is None else [image]
    first = skip // ROWS
    return pl.pallas_call(
        lambda *refs: height_kernel(
            *refs,
            chunks=chunks,
            sets=1,
            outs=1,
            scale=1.0 / math.sqrt(2 * total),
            skipped=len(earlier) + len(extra),
        ),
        grid_spec=pltpu.PrefetchScalarGridSpec(
            num_scalar_prefetch=1,
            grid=(rows // ROWS, full // width),
            in_specs=[pl.BlockSpec((1,) + matrix.shape[1:], lambda i, j, ids: (ids[2], 0, 0, 0))]
            + spec
            + spec
            + after(extra)
            + after(earlier),
            out_specs=pl.BlockSpec((2, total, ROWS, width), lambda i, j, ids: (0, 0, first + i, j)),
        ),
        out_shape=jax.ShapeDtypeStruct(shape, jnp.bfloat16),
        input_output_aliases={2 + 2 * chunks: 0} if extra else {},
        compiler_params=params(),
        cost_estimate=cost(rows * full * 32768, 12 * total * rows * full),
        name="last_heights",
    )(ids, matrix, *own, *other, *extra, *earlier)


def cross_kernel(ids_ref, *refs, groups, blocks, scale, skipped, outs):
    ins = [refs[g * blocks : (g + 1) * blocks] for g in range(groups)]
    cos_ref, sin_ref = refs[groups * blocks : groups * blocks + 2]
    out_refs = refs[groups * blocks + 2 + skipped : -1]
    rows_ref = refs[-1]
    bins, cols = ins[0][0].shape[2:]
    cuts = [group[0].shape[1] for group in ins]
    rows = sum(cuts) * bins

    @pl.when(pl.program_id(0) == 0)
    def _():
        for s in range(blocks):
            start = pl.multiple_of((ids_ref[0] ^ s) * cols, cols)
            for part in range(2):
                place = part * rows
                for group, count in zip(ins, cuts):
                    rows_ref[pl.ds(place, count * bins), pl.ds(start, cols)] = group[s][
                        part
                    ].reshape(count * bins, cols)
                    place += count * bins

    values = rows_ref[...]
    with_cos = jnp.dot(values, cos_ref[...], preferred_element_type=jnp.float32)
    with_sin = jnp.dot(values, sin_ref[...], preferred_element_type=jnp.float32)
    real = (with_cos[:rows] - with_sin[rows:]) * scale
    imag = (with_sin[:rows] + with_cos[rows:]) * scale
    for part, value in ((0, real), (1, imag)):
        value = value.astype(jnp.bfloat16).reshape(sum(cuts), bins, value.shape[1])
        place = 0
        for ref in out_refs:
            size = ref.shape[2]
            ref[part] = value[:, place : place + size]
            place += size


def cross_transform(ids, ins, tables, scale, sizes=None, image=None, shape=None, place=0, earlier=()):
    groups, blocks = len(ins), len(ins[0])
    bins, cols = ins[0][0].shape[2:]
    total = sum(group[0].shape[1] for group in ins)
    full = tables[0].shape[1]
    width = min(full, 512)
    extra = [] if image is None else [image]
    if shape is None:
        shapes = [(2, total, size, full) for size in sizes]
    else:
        sizes, shapes = [bins], [shape]
    result = pl.pallas_call(
        lambda *refs: cross_kernel(
            *refs,
            groups=groups,
            blocks=blocks,
            scale=scale,
            skipped=len(extra) + len(earlier),
            outs=len(sizes),
        ),
        grid_spec=pltpu.PrefetchScalarGridSpec(
            num_scalar_prefetch=1,
            grid=(full // width,),
            in_specs=[
                pl.BlockSpec((2, v.shape[1], bins, cols), lambda i, ids: (0, 0, 0, 0))
                for group in ins
                for v in group
            ]
            + [pl.BlockSpec((full, width), lambda i, ids: (0, i))] * 2
            + after(extra)
            + after(earlier),
            out_specs=[
                pl.BlockSpec((2, total, size, width), lambda i, ids: (0, place, 0, i))
                for size in sizes
            ],
            scratch_shapes=[pltpu.VMEM((2 * total * bins, full), jnp.bfloat16)],
        ),
        out_shape=[jax.ShapeDtypeStruct(v, jnp.bfloat16) for v in shapes],
        input_output_aliases={1 + groups * blocks + 2: 0} if extra else {},
        compiler_params=params(),
        cost_estimate=cost(8 * total * bins * full * full, 8 * total * bins * full + 4 * full * full),
        name="cross_transform",
    )(ids, *[v for group in ins for v in group], *tables, *extra, *earlier)
    return result if image is None and len(sizes) > 1 else result[0]


def exchange(value, axis, s):
    return lax.ppermute(value, axis, [(i, i ^ s) for i in range(lax.axis_size(axis))])


def halo_rows(polar):
    count = lax.axis_size("az")
    cols = polar.shape[2]
    ends = count - 1
    head = lax.slice_in_dim(polar, 0, HW, axis=2)
    tail = lax.slice_in_dim(polar, cols - HW, cols, axis=2)
    return jnp.concatenate(
        [
            lax.ppermute(tail, "az", [(i, i + 1) for i in range(ends)]),
            lax.ppermute(head, "az", [(i + 1, i) for i in range(ends)]),
        ],
        axis=2,
    )


def planned_path(polar, band_offset, tap_count, tap_weight):
    _, cuts, cols, freqs = polar.shape
    az_count = lax.axis_size("az")
    fq_count = lax.axis_size("fq")
    bins = F // (az_count * fq_count)
    split = SPLIT
    rest = bins - split
    ids = jnp.stack([lax.axis_index("az"), lax.axis_index("fq"), lax.axis_index("el")])
    tables = []
    for core in range(fq_count):
        order = np.concatenate([np.arange(freqs) + freqs * (core ^ s) for s in range(fq_count)])
        blocks = []
        for az in range(az_count):
            ks = (az * fq_count + core) * bins + np.arange(bins)
            blocks.append(np.concatenate(host_table(ks, order, F), axis=1))
        tables.append(np.stack(blocks))
    range_table = jnp.asarray(np.stack(tables))
    cross_tables = [jnp.asarray(t) for t in host_table(np.arange(A), np.arange(A), A)]
    order = np.concatenate([start + np.arange(count) for start, count in CHUNKS])
    whole_table = height_table(cuts, ROWS, order)
    matrix = jnp.asarray(whole_table)
    by_height = whole_table.reshape(2, 2, 2, cuts // 2, ROWS, -1)
    pieces, start = [], 0
    for size in PARTS:
        piece = by_height[:, :, :, start // 2 : (start + size) // 2]
        pieces.append(jnp.asarray(piece.reshape(2, 2, size * ROWS, -1)))
        start += size

    bands = (band_offset, tap_count, tap_weight)
    halo = halo_rows(polar)
    last = len(CHUNKS) - 1
    scale = 1.0 / math.sqrt(A)

    def interp(i, earlier=(), limit=VMEM):
        return interpolate(polar, halo, bands, *CHUNKS[i], earlier, limit)

    def to_owners(blocks, which=range(az_count - 1, 0, -1)):
        return {4 - s: exchange(blocks[s], "az", s) for s in which}

    def in_order(blocks, come):
        return [blocks[0]] + [come[4 - s] for s in range(1, az_count)]

    bare = interpolate(polar, None, bands, *CHUNKS[0], (), WIDE_VMEM)
    made = interpolate_edges(polar, halo, bands, CHUNKS[0][0], bare)
    other = exchange(made, "fq", 1)
    ahead = interp(1, (made,), WIDE_VMEM)
    own_first, other_first, landed = [], [], []
    moving = None
    for i in range(last + 1):
        limit = VMEM if i else WIDE_VMEM
        first, *blocks = range_transform(ids, made, other, range_table, split, (ahead,), limit)
        if 0 < i < last:
            ahead = interp(i + 1, (first,))
        first, blocks, ahead, moving = lax.optimization_barrier((first, blocks, ahead, moving))
        if i > 0:
            landed.append(in_order(held, moving[0]))
            other_first.append(moving[1])
        own_first.append(first)
        held = blocks
        moving = (to_owners(blocks), exchange(first, "el", 1))
        if i < last:
            made, other = ahead, exchange(ahead, "fq", 1)
    c0 = cross_transform(ids, landed, cross_tables, scale, [rest], earlier=(first,))
    c0, moving = lax.optimization_barrier((c0, moving))
    landed.append(in_order(held, moving[0]))
    other_first.append(moving[1])
    other_c0 = exchange(c0, "el", 1)

    made, before = [], c0
    for piece, size in zip(pieces, PARTS):
        made += first_heights(ids, piece, own_first, other_first, (size,), (before,))
        before = made[-1][0]
    come = to_owners(made[0])
    late = [rest - ROWS, ROWS]
    c1, c2 = cross_transform(ids, landed[-1:], cross_tables, scale, late, earlier=(before,))
    other_c1 = exchange(c1, "el", 1)
    shape = (2, cuts, bins, A)
    full_scale = 1.0 / math.sqrt(A * 2 * cuts)
    made, come, c2 = lax.optimization_barrier((made, come, c2))
    arrived = in_order(made[0], come)
    come = to_owners(made[1])
    image = cross_transform(
        ids, [arrived], cross_tables, full_scale, image=None, shape=shape, place=0, earlier=(c1,)
    )
    image, c2, other_c0 = lax.optimization_barrier((image, c2, other_c0))
    other_c2 = exchange(c2, "el", 1)
    image = last_heights(
        ids, matrix, [c0, c1], [other_c0, other_c1], (0, 0), image, shape, split, late[0]
    )
    image = last_heights(
        ids, matrix, [c0, c2], [other_c0, other_c2], (late[0], 0), image, shape, split + late[0], late[1]
    )
    image = cross_transform(
        ids,
        [in_order(made[1], come)],
        cross_tables,
        full_scale,
        image=image,
        shape=shape,
        place=PARTS[0] // PARTS[1],
    )
    return image


def on_device(polar, band_offset, tap_count, tap_weight):
    _, cuts, cols, freqs = polar.shape
    az_count = lax.axis_size("az")
    bins = F // (az_count * lax.axis_size("fq"))
    fits = (
        lax.axis_size("el") == 2
        and lax.axis_size("fq") == 2
        and az_count == 4
        and cuts == sum(count for _, count in CHUNKS) == sum(PARTS)
        and cols % (2 * LANES) == 0
        and freqs % LANES == 0
        and bins > SPLIT
        and bins == 2 * SPLIT
        and A % 512 == 0
        and 2 * HW == ROWS
    )
    chosen = planned_path if fits else general_path
    return chosen(polar, band_offset, tap_count, tap_weight)


def solution(mesh):
    in_specs = (
        P(None, ("grp", "el"), "az", "fq"),
        P("az", "fq"),
        P("az", "fq"),
        P(None, "az", "fq"),
    )
    out_specs = P(None, ("grp", "el"), ("az", "fq"), None)
    return jax.shard_map(
        on_device, mesh=mesh, in_specs=in_specs, out_specs=out_specs, check_vma=False
    )
```

```python
import math

import jax
import jax.numpy as jnp
import ml_dtypes
import numpy as np
from jax import lax
from jax.experimental import pallas as pl
from jax.experimental.pallas import tpu as pltpu
from jax.sharding import PartitionSpec as P

F = 768
A = 1024
E = 32
HW = 8
KT = 8

LANES = 128
ROWS = 16


def with_halo(cells, sides, width):
    for axis, dim in sides:
        count = lax.axis_size(axis)
        ends = count - 1
        head = lax.slice_in_dim(cells, 0, width, axis=dim)
        tail = lax.slice_in_dim(cells, cells.shape[dim] - width, cells.shape[dim], axis=dim)
        cells = jnp.concatenate(
            [
                lax.ppermute(tail, axis, [(i, (i + 1) % count) for i in range(ends)]),
                cells,
                lax.ppermute(head, axis, [((i + 1) % count, i) for i in range(ends)]),
            ],
            axis=dim,
        )
    return cells


def table_pair(row_ids, col_ids, length):
    product = row_ids[:, None] * col_ids[None, :] % length
    angle = product.astype(jnp.float32) * (2.0 * math.pi / length)
    return (jnp.cos(angle).astype(jnp.bfloat16), jnp.sin(angle).astype(jnp.bfloat16))


def general_path(polar, band_offset, tap_count, tap_weight):
    shape_all = polar.shape
    col_count = shape_all[2]
    freq_count = shape_all[3]
    az_count = lax.axis_size("az")
    fq_count = lax.axis_size("fq")
    el_count = lax.axis_size("el")
    padded = with_halo(polar, (("az", 2),), HW)
    window = col_count + 2 * HW
    column = jnp.arange(col_count, dtype=jnp.int32)[:, None]
    position = jnp.arange(window, dtype=jnp.int32)[None, :, None]
    band_matrix = jnp.zeros((col_count, window, freq_count), jnp.bfloat16)
    for tap_index in range(KT):
        reach = column + HW + band_offset + tap_index
        matches = (position == reach[:, None, :]) & (tap_index < tap_count)[:, None, :]
        band_matrix = jnp.where(matches, tap_weight[tap_index][:, None, :], band_matrix)
    interpolated = jnp.einsum(
        "jaf,ceaf->cejf", band_matrix, padded, preferred_element_type=jnp.float32
    ).astype(jnp.bfloat16)
    fq_index = lax.axis_index("fq")
    bin_count = F // (fq_count * az_count)
    az_block = jnp.arange(az_count, dtype=jnp.int32)[:, None]
    bin_local = jnp.arange(bin_count, dtype=jnp.int32)[None, :]
    range_bins = ((az_block * fq_count + fq_index) * bin_count + bin_local).reshape(-1)
    cos_f, sin_f = table_pair(jnp.arange(F, dtype=jnp.int32), range_bins, F)
    shard_piece = lax.all_gather(interpolated, "fq", axis=3, tiled=True)
    cos_rows = cos_f
    sin_rows = sin_f
    real_part = jnp.einsum(
        "ejf,fk->ekj", shard_piece[0], cos_rows, preferred_element_type=jnp.float32
    ) - jnp.einsum("ejf,fk->ekj", shard_piece[1], sin_rows, preferred_element_type=jnp.float32)
    imag_part = jnp.einsum(
        "ejf,fk->ekj", shard_piece[0], sin_rows, preferred_element_type=jnp.float32
    ) + jnp.einsum("ejf,fk->ekj", shard_piece[1], cos_rows, preferred_element_type=jnp.float32)
    summed = jnp.stack([real_part, imag_part])
    ranged = (summed * (1.0 / math.sqrt(F))).astype(jnp.bfloat16)
    azim_ids = jnp.arange(A, dtype=jnp.int32)
    cos_a, sin_a = table_pair(azim_ids, azim_ids, A)
    block_data = lax.all_to_all(ranged, "az", split_axis=2, concat_axis=3, tiled=True)
    real_part = jnp.einsum(
        "ekj,jm->ekm", block_data[0], cos_a, preferred_element_type=jnp.float32
    ) - jnp.einsum("ekj,jm->ekm", block_data[1], sin_a, preferred_element_type=jnp.float32)
    imag_part = jnp.einsum(
        "ekj,jm->ekm", block_data[0], sin_a, preferred_element_type=jnp.float32
    ) + jnp.einsum("ekj,jm->ekm", block_data[1], cos_a, preferred_element_type=jnp.float32)
    crossed = (jnp.stack([real_part, imag_part]) * (1.0 / math.sqrt(A))).astype(jnp.bfloat16)
    elev_ids = jnp.arange(E, dtype=jnp.int32)
    el_index = lax.axis_index("el")
    height_count = E // el_count
    height_rows = el_index * height_count + jnp.arange(height_count, dtype=jnp.int32)
    cos_e, sin_e = table_pair(elev_ids, height_rows, E)
    shard_piece = lax.all_gather(crossed, "el", axis=1, tiled=True)
    cos_rows = cos_e
    sin_rows = sin_e
    real_part = jnp.einsum(
        "eh,ekm->hkm", cos_rows, shard_piece[0], preferred_element_type=jnp.float32
    ) - jnp.einsum("eh,ekm->hkm", sin_rows, shard_piece[1], preferred_element_type=jnp.float32)
    imag_part = jnp.einsum(
        "eh,ekm->hkm", sin_rows, shard_piece[0], preferred_element_type=jnp.float32
    ) + jnp.einsum("eh,ekm->hkm", cos_rows, shard_piece[1], preferred_element_type=jnp.float32)
    totals = jnp.stack([real_part, imag_part])
    image_out = (totals * (1.0 / math.sqrt(E))).astype(jnp.bfloat16)
    return image_out


CHUNKS = ((0, 4), (4, 4), (8, 4), (12, 4))
PARTS = (8, 8)
SPLIT = 48
VMEM = 20 * 1024 * 1024
WIDE_VMEM = 60 * 1024 * 1024


def host_table(row_ids, col_ids, length):
    product = (row_ids[:, None] * col_ids[None, :]) % length
    angle = product.astype(np.float32) * np.float32(2.0 * math.pi / length)
    return (np.cos(angle).astype(ml_dtypes.bfloat16), np.sin(angle).astype(ml_dtypes.bfloat16))


def params(limit=VMEM):
    return pltpu.CompilerParams(vmem_limit_bytes=limit)


def cost(flops, nbytes):
    return pl.CostEstimate(flops=int(flops) // 1000, bytes_accessed=int(nbytes) // 1000, transcendentals=0)


def after(values):
    return [pl.BlockSpec(memory_space=pl.ANY)] * len(values)


def interp_rows(pad_ref, offset_ref, count_ref, weight_ref, out_ref, lane=slice(None)):
    _, cuts, cols, _ = out_ref.shape
    lanes = pad_ref.shape[2]
    step = 8

    def tile(index, carry):
        row = pl.multiple_of(index * ROWS, ROWS)
        rows = pl.ds(row, ROWS)
        base = offset_ref[rows, lane] + HW
        count = count_ref[rows, lane]
        zero = jnp.zeros((ROWS, lanes), jnp.float32)
        taps = [
            jnp.where(count > tap, weight_ref[tap, rows, lane].astype(jnp.float32), zero)
            for tap in range(KT)
        ]
        shift = 1
        while shift < KT:
            chosen = (base & shift) != 0
            taps = [jnp.where(chosen, taps[(r - shift) % KT], taps[r]) for r in range(KT)]
            shift *= 2
        halves = [slice(i, i + step) for i in range(0, ROWS, step)]
        past = [[base[half] > r for r in range(KT + 1)] for half in halves]
        taps = [[tap[half] for tap in taps] for half in halves]
        for part in range(2):
            for cut in range(cuts):
                plane = part * cuts + cut
                near = [
                    pad_ref[plane, pl.ds(row + d, step), :] for d in range(2 * HW + 1 + ROWS - step)
                ]
                totals = []
                for i in range(len(halves)):
                    here = near[i * step :]
                    total = None
                    for r in range(KT):
                        value = jnp.where(past[i][r], here[r + KT], here[r])
                        if r == 0:
                            value = jnp.where(past[i][KT], here[2 * KT], value)
                        value = value * taps[i][r]
                        total = value if total is None else total + value
                    totals.append(total)
                out_ref[part, cut, rows, lane] = jnp.concatenate(totals, axis=0).astype(jnp.bfloat16)
        return carry

    lax.fori_loop(0, cols // ROWS, tile, 0)


def interp_kernel(polar_ref, offset_ref, count_ref, weight_ref, *refs, bordered):
    out_ref, pad_ref = refs[-2:]
    _, cuts, cols, lanes = polar_ref.shape
    for part in range(2):
        for cut in range(cuts):
            plane = part * cuts + cut
            if bordered:
                halo = refs[0][part, cut].astype(jnp.float32)
            else:
                halo = jnp.zeros((2 * HW, lanes), jnp.float32)
            pad_ref[plane, pl.ds(0, HW), :] = halo[:HW]
            pad_ref[plane, pl.ds(HW, cols), :] = polar_ref[part, cut].astype(jnp.float32)
            pad_ref[plane, pl.ds(HW + cols, HW), :] = halo[HW:]
    interp_rows(pad_ref, offset_ref, count_ref, weight_ref, out_ref)


def chunk_spec(count, rows, first):
    return pl.BlockSpec((2, count, rows, LANES), lambda i: (0, first // count, 0, i))


def interpolate(polar, halo, bands, first, count, earlier=(), limit=VMEM):
    _, _, cols, freqs = polar.shape
    border = [] if halo is None else [halo]
    return pl.pallas_call(
        lambda *refs: interp_kernel(*refs, bordered=len(border) == 1),
        grid=(freqs // LANES,),
        in_specs=[
            chunk_spec(count, cols, first),
            pl.BlockSpec((cols, LANES), lambda i: (0, i)),
            pl.BlockSpec((cols, LANES), lambda i: (0, i)),
            pl.BlockSpec((KT, cols, LANES), lambda i: (0, 0, i)),
        ]
        + [chunk_spec(count, 2 * HW, first)] * len(border)
        + after(earlier),
        out_specs=chunk_spec(count, cols, 0),
        out_shape=jax.ShapeDtypeStruct((2, count, cols, freqs), jnp.bfloat16),
        scratch_shapes=[pltpu.VMEM((2 * count, cols + 2 * HW, LANES), jnp.float32)],
        compiler_params=params(limit),
        cost_estimate=cost(2 * count * cols * freqs * 34, 8 * count * cols * freqs),
        name="interpolate",
    )(polar, *bands, *border, *earlier)


def edge_kernel(polar_ref, halo_ref, offset_ref, count_ref, weight_ref, made_ref, out_ref, pad_ref):
    del made_ref
    _, cuts, rows, freqs = polar_ref.shape
    for start in range(0, freqs, LANES):
        lane = pl.ds(start, LANES)
        for part in range(2):
            for cut in range(cuts):
                plane = part * cuts + cut
                halo = halo_ref[part, cut, :, lane].astype(jnp.float32)
                body = polar_ref[part, cut, :, lane].astype(jnp.float32)
                left = jnp.concatenate([halo[:HW], body[: rows - HW]], axis=0)
                right = jnp.concatenate([body[HW:], halo[HW:]], axis=0)
                pad_ref[plane] = jnp.where(pl.program_id(0) == 0, left, right)
        interp_rows(pad_ref, offset_ref, count_ref, weight_ref, out_ref, lane)


def interpolate_edges(polar, halo, bands, first, made):
    _, count, cols, freqs = made.shape
    wide = cols // (2 * ROWS) - 1
    last = cols // ROWS - 1
    return pl.pallas_call(
        edge_kernel,
        grid=(2,),
        in_specs=[
            pl.BlockSpec((2, count, 2 * ROWS, freqs), lambda i: (0, first // count, i * wide, 0)),
            pl.BlockSpec((2, count, 2 * HW, freqs), lambda i: (0, first // count, 0, 0)),
            pl.BlockSpec((ROWS, freqs), lambda i: (i * last, 0)),
            pl.BlockSpec((ROWS, freqs), lambda i: (i * last, 0)),
            pl.BlockSpec((KT, ROWS, freqs), lambda i: (0, i * last, 0)),
            pl.BlockSpec(memory_space=pl.ANY),
        ],
        out_specs=pl.BlockSpec((2, count, ROWS, freqs), lambda i: (0, 0, i * last, 0)),
        out_shape=jax.ShapeDtypeStruct(made.shape, jnp.bfloat16),
        scratch_shapes=[pltpu.VMEM((2 * count, 2 * ROWS, LANES), jnp.float32)],
        input_output_aliases={5: 0},
        compiler_params=params(WIDE_VMEM),
        cost_estimate=cost(4 * count * ROWS * freqs * 34, 16 * count * ROWS * freqs),
        name="interpolate_edges",
    )(polar, halo, *bands, made)


def range_kernel(ids_ref, own_ref, other_ref, *refs, blocks, earlier):
    tables = refs[:blocks]
    first_ref, *rest = refs[blocks + earlier : -1]
    mixed_ref = refs[-1]
    cuts, cols = own_ref.shape[1:3]
    half = tables[0].shape[3]
    split = first_ref.shape[3]
    scale = 1.0 / math.sqrt(F)
    evens, odds = (jnp.concatenate([ref[0, 0, p] for ref in tables], axis=0) for p in range(2))
    for cut in range(cuts):
        for parity, table in ((0, evens), (1, odds)):
            if parity == 0:
                real, imag = (own_ref[part, cut] + other_ref[part, cut] for part in range(2))
            else:
                real, imag = (own_ref[part, cut] - other_ref[part, cut] for part in range(2))
            values = jnp.concatenate(
                [jnp.concatenate([real, -imag], axis=1), jnp.concatenate([imag, real], axis=1)],
                axis=0,
            )
            product = scale * lax.dot_general(
                table, values, (((1,), (1,)), ((), ())), preferred_element_type=jnp.float32
            )
            for s in range(blocks):
                for tile in range(2 * cols // LANES):
                    mixed_ref[s, tile, pl.ds(parity, half, stride=2), :] = product[
                        s * half : (s + 1) * half, tile * LANES : (tile + 1) * LANES
                    ]
        for s in range(blocks):
            for tile in range(2 * cols // LANES):
                part, start = divmod(tile * LANES, cols)
                lane = pl.ds(start, LANES)
                value = mixed_ref[s, tile].astype(jnp.bfloat16)
                first_ref[part, cut, s, :, lane] = value[:split]
                rest[s][part, cut, :, lane] = value[split:]


def range_transform(ids, own, other, table, split, earlier=(), limit=VMEM):
    _, count, cols, freqs = own.shape
    _, blocks, _, half, full = table.shape
    bins = 2 * half
    rest = bins - split
    group = 2

    def block_of(s):
        return pl.BlockSpec((1, 1, 2, half, full), lambda i, ids: (ids[1], ids[0] ^ s, 0, 0, 0))

    return pl.pallas_call(
        lambda *refs: range_kernel(*refs, blocks=blocks, earlier=len(earlier)),
        grid_spec=pltpu.PrefetchScalarGridSpec(
            num_scalar_prefetch=1,
            grid=(count // group,),
            in_specs=[pl.BlockSpec((2, group, cols, freqs), lambda i, ids: (0, i, 0, 0))] * 2
            + [block_of(s) for s in range(blocks)]
            + after(earlier),
            out_specs=[
                pl.BlockSpec((2, group, blocks, split, cols), lambda i, ids: (0, i, 0, 0, 0))
            ]
            + [pl.BlockSpec((2, group, rest, cols), lambda i, ids: (0, i, 0, 0))] * blocks,
            scratch_shapes=[pltpu.VMEM((blocks, 2 * cols // LANES, bins, LANES), jnp.float32)],
        ),
        out_shape=[jax.ShapeDtypeStruct((2, count, blocks, split, cols), jnp.bfloat16)]
        + [jax.ShapeDtypeStruct((2, count, rest, cols), jnp.bfloat16)] * blocks,
        compiler_params=params(limit),
        cost_estimate=cost(4 * count * cols * full * blocks * bins, 12 * count * cols * freqs),
        name="range_transform",
    )(ids, own, other, *([table] * blocks), *earlier)


def height_table(cuts, rows, order):
    heights = []
    for el in range(2):
        pair = []
        for parity in range(2):
            h = el * cuts + parity + 2 * np.arange(cuts // 2)
            cos, sin = (t.astype(np.float32) for t in host_table(h, order, 2 * cuts))
            sign = -1.0 if el and parity else 1.0
            whole = sign * np.block([[cos, -sin], [sin, cos]])
            pair.append(np.kron(whole, np.eye(rows, dtype=np.float32)))
        heights.append(np.stack(pair))
    return np.stack(heights).astype(ml_dtypes.bfloat16)


def height_kernel(ids_ref, matrix_ref, *refs, chunks, sets, outs, scale, skipped):
    ins = refs[: 2 * chunks]
    out_refs = refs[2 * chunks + skipped :]
    rows, lanes = ins[0].shape[-2:]
    half = matrix_ref.shape[2] // (2 * rows)
    for index in range(sets):
        sums, differences = [], []
        for part in range(2):
            for own, other in zip(ins[:chunks], ins[chunks:]):
                pad = (index,) if len(own.shape) == 5 else ()
                for e in range(own.shape[1]):
                    a, b = own[(part, e) + pad], other[(part, e) + pad]
                    sums.append(a + b)
                    differences.append(a - b)
        results = [
            jnp.dot(
                matrix_ref[0, parity],
                jnp.concatenate(values, axis=0),
                preferred_element_type=jnp.float32,
            )
            for parity, values in enumerate((sums, differences))
        ]
        h = 0
        for ref in out_refs[index * outs : (index + 1) * outs]:
            for row in range(ref.shape[1]):
                for part in range(2):
                    start = (part * half + h // 2) * rows
                    value = results[h % 2][start : start + rows]
                    if scale is not None:
                        value = value * scale
                    ref[part, row] = value.astype(jnp.bfloat16)
                h += 1


def first_heights(ids, matrix, own, other, parts, earlier=()):
    chunks = len(own)
    _, _, blocks, split, cols = own[0].shape
    total = sum(v.shape[1] for v in own)
    spec = [
        pl.BlockSpec((2, v.shape[1], blocks, ROWS, cols), lambda i, ids: (0, 0, 0, i, 0))
        for v in own
    ]
    outs = list(parts) * blocks
    made = pl.pallas_call(
        lambda *refs: height_kernel(
            *refs, chunks=chunks, sets=blocks, outs=len(parts), scale=None, skipped=len(earlier)
        ),
        grid_spec=pltpu.PrefetchScalarGridSpec(
            num_scalar_prefetch=1,
            grid=(split // ROWS,),
            in_specs=[pl.BlockSpec((1,) + matrix.shape[1:], lambda i, ids: (ids[2], 0, 0, 0))]
            + spec
            + spec
            + after(earlier),
            out_specs=[pl.BlockSpec((2, h, ROWS, cols), lambda i, ids: (0, 0, i, 0)) for h in outs],
        ),
        out_shape=[jax.ShapeDtypeStruct((2, h, split, cols), jnp.bfloat16) for h in outs],
        compiler_params=params(),
        cost_estimate=cost(blocks * split * cols * 32768, 12 * blocks * total * split * cols),
        name="first_heights",
    )(ids, matrix, *own, *other, *earlier)
    return [[made[s * len(parts) + p] for s in range(blocks)] for p in range(len(parts))]


def last_heights(ids, matrix, own, other, places, image, shape, skip, rows, earlier=()):
    chunks = len(own)
    full = own[0].shape[3]
    width = min(full, 512)
    total = sum(v.shape[1] for v in own)

    def chunk(v, place):
        return pl.BlockSpec(
            (2, v.shape[1], ROWS, width), lambda i, j, ids: (0, 0, place // ROWS + i, j)
        )

    spec = [chunk(v, place) for v, place in zip(own, places)]
    extra = [] if image is None else [image]
    first = skip // ROWS
    return pl.pallas_call(
        lambda *refs: height_kernel(
            *refs,
            chunks=chunks,
            sets=1,
            outs=1,
            scale=1.0 / math.sqrt(2 * total),
            skipped=len(earlier) + len(extra),
        ),
        grid_spec=pltpu.PrefetchScalarGridSpec(
            num_scalar_prefetch=1,
            grid=(rows // ROWS, full // width),
            in_specs=[pl.BlockSpec((1,) + matrix.shape[1:], lambda i, j, ids: (ids[2], 0, 0, 0))]
            + spec
            + spec
            + after(extra)
            + after(earlier),
            out_specs=pl.BlockSpec((2, total, ROWS, width), lambda i, j, ids: (0, 0, first + i, j)),
        ),
        out_shape=jax.ShapeDtypeStruct(shape, jnp.bfloat16),
        input_output_aliases={2 + 2 * chunks: 0} if extra else {},
        compiler_params=params(),
        cost_estimate=cost(rows * full * 32768, 12 * total * rows * full),
        name="last_heights",
    )(ids, matrix, *own, *other, *extra, *earlier)


def cross_kernel(ids_ref, *refs, groups, blocks, scale, skipped, outs):
    ins = [refs[g * blocks : (g + 1) * blocks] for g in range(groups)]
    cos_ref, sin_ref = refs[groups * blocks : groups * blocks + 2]
    out_refs = refs[groups * blocks + 2 + skipped : -1]
    rows_ref = refs[-1]
    bins, cols = ins[0][0].shape[2:]
    cuts = [group[0].shape[1] for group in ins]
    rows = sum(cuts) * bins

    @pl.when(pl.program_id(0) == 0)
    def _():
        for s in range(blocks):
            start = pl.multiple_of((ids_ref[0] ^ s) * cols, cols)
            for part in range(2):
                place = part * rows
                for group, count in zip(ins, cuts):
                    rows_ref[pl.ds(place, count * bins), pl.ds(start, cols)] = group[s][
                        part
                    ].reshape(count * bins, cols)
                    place += count * bins

    values = rows_ref[...]
    with_cos = jnp.dot(values, cos_ref[...], preferred_element_type=jnp.float32)
    with_sin = jnp.dot(values, sin_ref[...], preferred_element_type=jnp.float32)
    real = (with_cos[:rows] - with_sin[rows:]) * scale
    imag = (with_sin[:rows] + with_cos[rows:]) * scale
    for part, value in ((0, real), (1, imag)):
        value = value.astype(jnp.bfloat16).reshape(sum(cuts), bins, value.shape[1])
        place = 0
        for ref in out_refs:
            size = ref.shape[2]
            ref[part] = value[:, place : place + size]
            place += size


def cross_transform(ids, ins, tables, scale, sizes=None, image=None, shape=None, place=0, earlier=()):
    groups, blocks = len(ins), len(ins[0])
    bins, cols = ins[0][0].shape[2:]
    total = sum(group[0].shape[1] for group in ins)
    full = tables[0].shape[1]
    width = min(full, 512)
    extra = [] if image is None else [image]
    if shape is None:
        shapes = [(2, total, size, full) for size in sizes]
    else:
        sizes, shapes = [bins], [shape]
    result = pl.pallas_call(
        lambda *refs: cross_kernel(
            *refs,
            groups=groups,
            blocks=blocks,
            scale=scale,
            skipped=len(extra) + len(earlier),
            outs=len(sizes),
        ),
        grid_spec=pltpu.PrefetchScalarGridSpec(
            num_scalar_prefetch=1,
            grid=(full // width,),
            in_specs=[
                pl.BlockSpec((2, v.shape[1], bins, cols), lambda i, ids: (0, 0, 0, 0))
                for group in ins
                for v in group
            ]
            + [pl.BlockSpec((full, width), lambda i, ids: (0, i))] * 2
            + after(extra)
            + after(earlier),
            out_specs=[
                pl.BlockSpec((2, total, size, width), lambda i, ids: (0, place, 0, i))
                for size in sizes
            ],
            scratch_shapes=[pltpu.VMEM((2 * total * bins, full), jnp.bfloat16)],
        ),
        out_shape=[jax.ShapeDtypeStruct(v, jnp.bfloat16) for v in shapes],
        input_output_aliases={1 + groups * blocks + 2: 0} if extra else {},
        compiler_params=params(),
        cost_estimate=cost(8 * total * bins * full * full, 8 * total * bins * full + 4 * full * full),
        name="cross_transform",
    )(ids, *[v for group in ins for v in group], *tables, *extra, *earlier)
    return result if image is None and len(sizes) > 1 else result[0]


def exchange(value, axis, s):
    return lax.ppermute(value, axis, [(i, i ^ s) for i in range(lax.axis_size(axis))])


def halo_rows(polar):
    count = lax.axis_size("az")
    cols = polar.shape[2]
    ends = count - 1
    head = lax.slice_in_dim(polar, 0, HW, axis=2)
    tail = lax.slice_in_dim(polar, cols - HW, cols, axis=2)
    return jnp.concatenate(
        [
            lax.ppermute(tail, "az", [(i, i + 1) for i in range(ends)]),
            lax.ppermute(head, "az", [(i + 1, i) for i in range(ends)]),
        ],
        axis=2,
    )


def planned_path(polar, band_offset, tap_count, tap_weight):
    _, cuts, cols, freqs = polar.shape
    az_count = lax.axis_size("az")
    fq_count = lax.axis_size("fq")
    bins = F // (az_count * fq_count)
    split = SPLIT
    rest = bins - split
    ids = jnp.stack([lax.axis_index("az"), lax.axis_index("fq"), lax.axis_index("el")])
    tables = []
    for core in range(fq_count):
        blocks = []
        for az in range(az_count):
            pair = []
            for parity in range(2):
                ks = (az * fq_count + core) * bins + parity + 2 * np.arange(bins // 2)
                sign = -1.0 if core and parity else 1.0
                pair.append(sign * np.concatenate(host_table(ks, np.arange(freqs), F), axis=1))
            blocks.append(np.stack(pair).astype(ml_dtypes.bfloat16))
        tables.append(np.stack(blocks))
    range_table = jnp.asarray(np.stack(tables))
    cross_tables = [jnp.asarray(t) for t in host_table(np.arange(A), np.arange(A), A)]
    order = np.concatenate([start + np.arange(count) for start, count in CHUNKS])
    whole_table = height_table(cuts, ROWS, order)
    matrix = jnp.asarray(whole_table)
    by_height = whole_table.reshape(2, 2, 2, cuts // 2, ROWS, -1)
    pieces, start = [], 0
    for size in PARTS:
        piece = by_height[:, :, :, start // 2 : (start + size) // 2]
        pieces.append(jnp.asarray(piece.reshape(2, 2, size * ROWS, -1)))
        start += size

    bands = (band_offset, tap_count, tap_weight)
    halo = halo_rows(polar)
    last = len(CHUNKS) - 1
    scale = 1.0 / math.sqrt(A)

    def interp(i, earlier=(), limit=VMEM):
        return interpolate(polar, halo, bands, *CHUNKS[i], earlier, limit)

    def to_owners(blocks, which=range(az_count - 1, 0, -1)):
        return {4 - s: exchange(blocks[s], "az", s) for s in which}

    def in_order(blocks, come):
        return [blocks[0]] + [come[4 - s] for s in range(1, az_count)]

    bare = interpolate(polar, None, bands, *CHUNKS[0], (), WIDE_VMEM)
    made = interpolate_edges(polar, halo, bands, CHUNKS[0][0], bare)
    other = exchange(made, "fq", 1)
    ahead = interp(1, (made,), WIDE_VMEM)
    own_first, other_first, landed = [], [], []
    moving = None
    for i in range(last + 1):
        limit = VMEM if i else WIDE_VMEM
        first, *blocks = range_transform(ids, made, other, range_table, split, (ahead,), limit)
        if 0 < i < last:
            ahead = interp(i + 1, (first,))
        first, blocks, ahead, moving = lax.optimization_barrier((first, blocks, ahead, moving))
        if i > 0:
            landed.append(in_order(held, moving[0]))
            other_first.append(moving[1])
        own_first.append(first)
        held = blocks
        moving = (to_owners(blocks), exchange(first, "el", 1))
        if i < last:
            made, other = ahead, exchange(ahead, "fq", 1)
    c0 = cross_transform(ids, landed, cross_tables, scale, [rest], earlier=(first,))
    c0, moving = lax.optimization_barrier((c0, moving))
    landed.append(in_order(held, moving[0]))
    other_first.append(moving[1])
    other_c0 = exchange(c0, "el", 1)

    made, before = [], c0
    for piece, size in zip(pieces, PARTS):
        made += first_heights(ids, piece, own_first, other_first, (size,), (before,))
        before = made[-1][0]
    come = to_owners(made[0])
    late = [rest - ROWS, ROWS]
    c1, c2 = cross_transform(ids, landed[-1:], cross_tables, scale, late, earlier=(before,))
    other_c1 = exchange(c1, "el", 1)
    shape = (2, cuts, bins, A)
    full_scale = 1.0 / math.sqrt(A * 2 * cuts)
    made, come, c2 = lax.optimization_barrier((made, come, c2))
    arrived = in_order(made[0], come)
    come = to_owners(made[1])
    image = cross_transform(
        ids, [arrived], cross_tables, full_scale, image=None, shape=shape, place=0, earlier=(c1,)
    )
    image, c2, other_c0 = lax.optimization_barrier((image, c2, other_c0))
    other_c2 = exchange(c2, "el", 1)
    image = last_heights(
        ids, matrix, [c0, c1], [other_c0, other_c1], (0, 0), image, shape, split, late[0]
    )
    image = last_heights(
        ids, matrix, [c0, c2], [other_c0, other_c2], (late[0], 0), image, shape, split + late[0], late[1]
    )
    image = cross_transform(
        ids,
        [in_order(made[1], come)],
        cross_tables,
        full_scale,
        image=image,
        shape=shape,
        place=PARTS[0] // PARTS[1],
    )
    return image


def on_device(polar, band_offset, tap_count, tap_weight):
    _, cuts, cols, freqs = polar.shape
    az_count = lax.axis_size("az")
    bins = F // (az_count * lax.axis_size("fq"))
    fits = (
        lax.axis_size("el") == 2
        and lax.axis_size("fq") == 2
        and az_count == 4
        and cuts == sum(count for _, count in CHUNKS) == sum(PARTS)
        and cols % (2 * LANES) == 0
        and freqs % LANES == 0
        and 2 * freqs == F
        and bins > SPLIT
        and bins == 2 * SPLIT
        and A % 512 == 0
        and 2 * HW == ROWS
    )
    chosen = planned_path if fits else general_path
    return chosen(polar, band_offset, tap_count, tap_weight)


def solution(mesh):
    in_specs = (
        P(None, ("grp", "el"), "az", "fq"),
        P("az", "fq"),
        P("az", "fq"),
        P(None, "az", "fq"),
    )
    out_specs = P(None, ("grp", "el"), ("az", "fq"), None)
    return jax.shard_map(
        on_device, mesh=mesh, in_specs=in_specs, out_specs=out_specs, check_vma=False
    )
```
